32 devices in a mesh: depth: 8 (over z, y), gx: 2 (over core), gy: 2 (over x).
Axes of the slice: x: 2, y: 2, z: 4, core: 2. Of those that a mesh axis runs over, the one named last changes fastest.
Arguments:
- slowness: float32 [16, 32, 512], P('depth', 'gx', 'gy'), may hold values from 0.5 to 1.5
- air_mask: int32 [16, 32, 512], P('depth', 'gx', 'gy'), may hold values from 0 to 1, as said below
- reflector: int32 [32, 512], P('gx', 'gy'), may hold values from 4 to 15
- shot_cells: int32 [8, 2], replicated, may hold values from 0 to 31
- receiver_mask: int32 [8, 32, 512], P(None, 'gx', 'gy'), may hold values 0 or 1
- residual: float32 [8, 32, 512], P(None, 'gx', 'gy'), may hold values from -6 to 6
Outputs:
- gradient: float32 [16, 32, 512], P('depth', 'gx', 'gy')
The draws below stay inside these ranges and needn't reach their ends.
Inputs may be any that keep to these rules, and one draw needn't show every extreme that they name: `air_mask`: each lateral column is air in a top run of 0 to 2 cells and earth below; some column has exactly 2 air cells.
All inputs are finite; a program needn't handle non-finite values. No bound on the sum of `receiver_mask` on one device may be relied on, other than what follows from the above.
Results may differ from the reference program's by a relative error of at most 0.0003.
Values sent between devices are 32-bit elements; how exact they have to be, the bound alone decides.
A program may use at most 64 MiB of HBM per device.

```python
import math
import jax
import jax.numpy as jnp
from jax import lax

SHOTS = 8
NX = 32
NY = 512
NZ = 16


def draw_air_mask(key, part):
    heights = jax.random.randint(jax.random.fold_in(key, 11), (NX, NY), 0, NZ // 8 + 1)
    heights = heights.at[0, 0].set(NZ // 8)
    zpos = jnp.arange(NZ, dtype=jnp.int32)[:, None, None]
    return (zpos < heights[None]).astype(jnp.int32)


def touch_ends(values, key, least, high):
    spot = [jax.random.randint(jax.random.fold_in(key, axis), (), 0, length) for axis, length in enumerate(values.shape)]
    widest = values.shape.index(max(values.shape))
    next_to = spot[:widest] + [(spot[widest] + 1) % values.shape[widest]] + spot[widest + 1:]
    return values.at[tuple(spot)].set(least).at[tuple(next_to)].set(high)


def block_scale(key, dims, pieces, least, high):
    factor_of, own = 1.0, jax.random.fold_in(key, 6)
    for dim, blocks in pieces:
        draws = jnp.exp(jax.random.uniform(jax.random.fold_in(own, dim), (blocks,), jnp.float32, least / len(pieces), high / len(pieces)))
        factor_of = factor_of * jnp.repeat(draws, dims[dim] // blocks).reshape([-1 if axis == dim else 1 for axis in range(len(dims))])
    return factor_of


def scatter_about(stream_key, extent, deviation, bound, shards=(), kind=jnp.bfloat16):
    entries = deviation * jax.random.normal(stream_key, extent, jnp.float32)
    if shards:
        entries = entries * block_scale(stream_key, extent, shards, -0.22, 0.18)
    return jnp.clip(entries, -bound, bound).astype(kind)


def setup_inputs(seed: int = 0) -> dict:
    streams_of = jax.random.split(jax.random.key(seed), 7)
    slowness = jnp.clip(0.5 + 1.0 * jax.random.uniform(streams_of[0], (NZ, NX, NY), jnp.float32) ** block_scale(streams_of[0], (NZ, NX, NY), ((0, 8), (1, 2), (2, 2)), -0.2, 0.2), 0.5, 1.5)
    air_mask = draw_air_mask(jax.random.fold_in(streams_of[6], 71), 0)
    reflector = touch_ends(jax.random.randint(streams_of[2], (NX, NY), NZ // 4, NZ), jax.random.fold_in(streams_of[2], 1), NZ // 4, NZ - 1).astype(jnp.int32)
    shot_cells = touch_ends(jax.random.randint(streams_of[3], (SHOTS, 2), 0, min(NX, NY)), jax.random.fold_in(streams_of[3], 1), 0, (min(NX, NY)) - 1).astype(jnp.int32)
    receiver_mask = touch_ends((jax.random.randint(streams_of[4], (SHOTS, NX, NY), 0, 2) < 1).astype(jnp.int32), jax.random.fold_in(streams_of[4], 1), 0, 1)
    residual = scatter_about(streams_of[5], (SHOTS, NX, NY), 1.0, 6.0, ((1, 2), (2, 2)), jnp.float32)
    return {"slowness": slowness, "air_mask": air_mask, "reflector": reflector, "shot_cells": shot_cells, "receiver_mask": receiver_mask, "residual": residual}


SOFTMIN_TEMPER = 0.5
SURF = 0.7
AIR_SLOW = 2.5
STEP_PENALTY = 10000.0
STENCIL_SHIFTS = [(first_term, second_term) for first_term in (-1, 0, 1) for second_term in (-1, 0, 1)]

def neighbour_value(field, first_term, second_term):
    padded_layer = jnp.pad(field, ((0, 0), (1, 1), (1, 1)))
    return padded_layer[:, 1 + first_term:1 + first_term + NX, 1 + second_term:1 + second_term + NY]

def backshift(field, first_term, second_term):
    padded_layer = jnp.pad(field, ((0, 0), (1, 1), (1, 1)))
    return padded_layer[:, 1 - first_term:1 - first_term + NX, 1 - second_term:1 - second_term + NY]

def reference(slowness, air_mask, reflector, shot_cells, receiver_mask, residual):
    speed = jnp.where(air_mask == 1, jnp.float32(AIR_SLOW), slowness)
    xpos = jnp.arange(NX, dtype=jnp.int32)
    ypos = jnp.arange(NY, dtype=jnp.int32)
    shot_x = shot_cells[:, 0].astype(jnp.float32)
    shot_y = shot_cells[:, 1].astype(jnp.float32)
    surface = SURF * jnp.sqrt((xpos.astype(jnp.float32)[None, :, None] - shot_x[:, None, None]) ** 2 + (ypos.astype(jnp.float32)[None, None, :] - shot_y[:, None, None]) ** 2)
    penalty_terms = []
    span_lengths = []
    for first_term, second_term in STENCIL_SHIFTS:
        valid_mask = ((xpos + first_term >= 0) & (xpos + first_term < NX))[:, None] & ((ypos + second_term >= 0) & (ypos + second_term < NY))[None, :]
        penalty_terms.append(jnp.where(valid_mask, jnp.float32(0.0), jnp.float32(STEP_PENALTY)))
        span_lengths.append(math.sqrt(1.0 + first_term * first_term + second_term * second_term))

    def forward(prior_layer, depth_layer):
        candidate_times = [neighbour_value(prior_layer, first_term, second_term) + depth_layer * span_lengths[stencil_index] + penalty_terms[stencil_index] for stencil_index, (first_term, second_term) in enumerate(STENCIL_SHIFTS)]
        lowest = candidate_times[0]
        for c in candidate_times[1:]:
            lowest = jnp.minimum(lowest, c)
        total = jnp.exp(-(candidate_times[0] - lowest) / SOFTMIN_TEMPER)
        for c in candidate_times[1:]:
            total = total + jnp.exp(-(c - lowest) / SOFTMIN_TEMPER)
        nxt = lowest - SOFTMIN_TEMPER * jnp.log(total)
        return (nxt, nxt)
    unused, times = lax.scan(forward, surface, speed)
    source = jnp.where(receiver_mask == 1, residual, jnp.float32(0.0))

    def adjoint(back, k):
        current_layer = lax.dynamic_index_in_dim(times, k, 0, keepdims=False)
        earlier = lax.dynamic_index_in_dim(times, jnp.maximum(k - 1, 0).astype(jnp.int32), 0, keepdims=False)
        previous_times = jnp.where(k > 0, earlier, surface)
        depth_layer = lax.dynamic_index_in_dim(speed, k, 0, keepdims=False)
        hit = (reflector == k).astype(jnp.float32)
        lam = source * hit[None] + back
        weight_sum = jnp.zeros_like(lam)
        back_new = jnp.zeros_like(lam)
        for stencil_index, (first_term, second_term) in enumerate(STENCIL_SHIFTS):
            softmin_weight = jnp.exp(-(neighbour_value(previous_times, first_term, second_term) + depth_layer * span_lengths[stencil_index] + penalty_terms[stencil_index] - current_layer) / SOFTMIN_TEMPER)
            weight_sum = weight_sum + softmin_weight * span_lengths[stencil_index]
            back_new = back_new + backshift(lam * softmin_weight, first_term, second_term)
        return (back_new, lax.optimization_barrier(jnp.sum(lam * weight_sum, axis=0)))
    unused2, grads = lax.scan(adjoint, jnp.zeros_like(surface), jnp.arange(NZ, dtype=jnp.int32), reverse=True)
    earth = air_mask == 0
    zpos = jnp.arange(NZ, dtype=jnp.int32)
    colsum = lax.optimization_barrier(jnp.sum(source, axis=0))
    below = zpos[:, None, None] <= reflector[None]
    raw = jnp.where(earth, grads, jnp.float32(0.0)) + jnp.where(earth & below, colsum[None], jnp.float32(0.0))
    padded_layer = jnp.pad(raw, ((0, 0), (1, 1), (1, 1)))
    beside_all = jnp.zeros_like(raw)
    for first_term, second_term in STENCIL_SHIFTS:
        if first_term != 0 or second_term != 0:
            beside_all = beside_all + padded_layer[:, 1 + first_term:1 + first_term + NX, 1 + second_term:1 + second_term + NY]
    return 0.5 * raw + 0.0625 * beside_all
```

```python
import functools
import math

import jax
import jax.numpy as jnp
from jax import lax
from jax.experimental import pallas as pl
from jax.experimental.pallas import tpu as pltpu
from jax.sharding import PartitionSpec as P

SOFTMIN_TEMPER = 0.5
SURF = 0.7
AIR_SLOW = 2.5
STEP_PENALTY = 10000.0
STENCIL_SHIFTS = [
    (first_term, second_term) for first_term in (-1, 0, 1) for second_term in (-1, 0, 1)
]


def padded(cells, sides, width):
    for axis, dim in sides:
        count = lax.axis_size(axis)
        ends = count - 1
        head = lax.slice_in_dim(cells, 0, width, axis=dim)
        tail = lax.slice_in_dim(cells, cells.shape[dim] - width, cells.shape[dim], axis=dim)
        cells = jnp.concatenate(
            [
                lax.ppermute(tail, axis, [(i, (i + 1) % count) for i in range(ends)]),
                cells,
                lax.ppermute(head, axis, [((i + 1) % count, i) for i in range(ends)]),
            ],
            axis=dim,
        )
    return cells


def passed_along(value, axis, steps):
    count = lax.axis_size(axis)
    initial, last = (max(0, -steps), min(count, count - steps))
    return lax.ppermute(value, axis, [(source, source + steps) for source in range(initial, last)])


def soft_front(candidate_times):
    lowest = candidate_times[0]
    for cand in candidate_times[1:]:
        lowest = jnp.minimum(lowest, cand)
    total = jnp.exp(-(candidate_times[0] - lowest) / SOFTMIN_TEMPER)
    for cand in candidate_times[1:]:
        total = total + jnp.exp(-(cand - lowest) / SOFTMIN_TEMPER)
    return lowest - SOFTMIN_TEMPER * jnp.log(total)


def local_generic(slowness, air_mask, reflector, shot_cells, receiver_mask, residual):
    depth_count = lax.axis_size("depth")
    depth_pos = lax.axis_index("depth")
    cz, shift_along_x, shift_along_y = slowness.shape
    shots = shot_cells.shape[0]
    nx_total = shift_along_x * lax.axis_size("gx")
    ny_total = shift_along_y * lax.axis_size("gy")
    xpos = lax.axis_index("gx") * shift_along_x + jnp.arange(shift_along_x, dtype=jnp.int32)
    ypos = lax.axis_index("gy") * shift_along_y + jnp.arange(shift_along_y, dtype=jnp.int32)
    zpos = depth_pos * cz + jnp.arange(cz, dtype=jnp.int32)
    earth = air_mask == 0
    speed = jnp.where(air_mask == 1, jnp.float32(AIR_SLOW), slowness)
    shot_x = shot_cells[:, 0].astype(jnp.float32)
    shot_y = shot_cells[:, 1].astype(jnp.float32)
    surface = SURF * jnp.sqrt(
        (xpos.astype(jnp.float32)[None, :, None] - shot_x[:, None, None]) ** 2
        + (ypos.astype(jnp.float32)[None, None, :] - shot_y[:, None, None]) ** 2
    )
    penalty_terms = []
    span_lengths = []
    for first_term, second_term in STENCIL_SHIFTS:
        valid_mask = ((xpos + first_term >= 0) & (xpos + first_term < nx_total))[:, None] & (
            (ypos + second_term >= 0) & (ypos + second_term < ny_total)
        )[None, :]
        penalty_terms.append(jnp.where(valid_mask, jnp.float32(0.0), jnp.float32(STEP_PENALTY)))
        span_lengths.append(math.sqrt(1.0 + first_term * first_term + second_term * second_term))

    def sweep_plane(prior_layer, depth_layer):
        padded_layer = padded(prior_layer, (("gx", 1), ("gy", 2)), 1)
        candidate_times = [
            padded_layer[
                :,
                1 + first_term : 1 + first_term + shift_along_x,
                1 + second_term : 1 + second_term + shift_along_y,
            ]
            + depth_layer * span_lengths[stencil_index]
            + penalty_terms[stencil_index]
            for stencil_index, (first_term, second_term) in enumerate(STENCIL_SHIFTS)
        ]
        nxt = soft_front(candidate_times)
        return (nxt, nxt)

    def make_adjoint(source_block, count):

        def adjoint_plane(back, inputs):
            depth_layer, hit, previous_times, current_layer = inputs
            lam = source_block * hit[None] + back
            stacked = jnp.concatenate([lam, current_layer, previous_times, depth_layer[None]], 0)
            padded_layer = padded(stacked, (("gx", 1), ("gy", 2)), 1)
            lam_pad = padded_layer[:count]
            cur_pad = padded_layer[count : 2 * count]
            prev_pad = padded_layer[2 * count : 3 * count]
            layer_pad = padded_layer[3 * count]
            weight_sum = jnp.zeros_like(lam)
            back_new = jnp.zeros_like(lam)
            for stencil_index, (first_term, second_term) in enumerate(STENCIL_SHIFTS):
                lateral_value = prev_pad[
                    :,
                    1 + first_term : 1 + first_term + shift_along_x,
                    1 + second_term : 1 + second_term + shift_along_y,
                ]
                softmin_weight = jnp.exp(
                    -(
                        lateral_value
                        + depth_layer * span_lengths[stencil_index]
                        + penalty_terms[stencil_index]
                        - current_layer
                    )
                    / SOFTMIN_TEMPER
                )
                weight_sum = weight_sum + softmin_weight * span_lengths[stencil_index]
                lam_from = lam_pad[
                    :,
                    1 - first_term : 1 - first_term + shift_along_x,
                    1 - second_term : 1 - second_term + shift_along_y,
                ]
                cur_from = cur_pad[
                    :,
                    1 - first_term : 1 - first_term + shift_along_x,
                    1 - second_term : 1 - second_term + shift_along_y,
                ]
                layer_from = layer_pad[
                    1 - first_term : 1 - first_term + shift_along_x,
                    1 - second_term : 1 - second_term + shift_along_y,
                ]
                prob_from = jnp.exp(
                    -(previous_times + layer_from * span_lengths[stencil_index] - cur_from)
                    / SOFTMIN_TEMPER
                )
                back_new = back_new + lam_from * prob_from
            return (back_new, jnp.sum(lam * weight_sum, axis=0))

        return adjoint_plane

    source_all = jnp.where(receiver_mask == 1, residual, jnp.float32(0.0))
    blocks = 1
    width = shots // blocks
    rounds = depth_count + blocks - 1

    def forward_round(step, carry):
        incoming, store = carry
        group = step - depth_pos
        valid_mask = (group >= 0) & (group < blocks)
        top = jnp.where(depth_pos == 0, surface, incoming)
        last, planes = lax.scan(sweep_plane, top, speed)
        block = jnp.concatenate([top[None], planes], 0)
        old = store
        store = jnp.where(valid_mask, block, old)
        incoming = passed_along(last, "depth", 1)
        return (incoming, store)

    store = jnp.zeros((cz + 1, shots, shift_along_x, shift_along_y), jnp.float32)
    incoming = jnp.zeros((width, shift_along_x, shift_along_y), jnp.float32)
    incoming, store = lax.fori_loop(0, rounds, forward_round, (incoming, store))
    hits = (zpos[:, None, None] == reflector[None]).astype(jnp.float32)

    def adjoint_round(step, carry):
        incoming_back, grad_sum = carry
        group = step - (depth_count - 1 - depth_pos)
        valid_mask = (group >= 0) & (group < blocks)
        back_top, grads = lax.scan(
            make_adjoint(source_all, width),
            incoming_back,
            (speed, hits, store[:-1], store[1:]),
            reverse=True,
        )
        grad_sum = grad_sum + jnp.where(valid_mask, grads, jnp.float32(0.0))
        incoming_back = passed_along(back_top, "depth", -1)
        return (incoming_back, grad_sum)

    start_back = jnp.zeros((width, shift_along_x, shift_along_y), jnp.float32)
    grad_total = jnp.zeros((cz, shift_along_x, shift_along_y), jnp.float32)
    start_back, grad_total = lax.fori_loop(0, rounds, adjoint_round, (start_back, grad_total))
    colsum = jnp.sum(source_all, axis=0)
    below = zpos[:, None, None] <= reflector[None]
    raw = jnp.where(earth, grad_total, jnp.float32(0.0)) + jnp.where(
        earth & below, colsum[None], jnp.float32(0.0)
    )
    padded_layer = padded(raw, (("gx", 1), ("gy", 2)), 1)
    beside_all = jnp.zeros_like(raw)
    for first_term, second_term in STENCIL_SHIFTS:
        if first_term != 0 or second_term != 0:
            beside_all = (
                beside_all
                + padded_layer[
                    :,
                    1 + first_term : 1 + first_term + shift_along_x,
                    1 + second_term : 1 + second_term + shift_along_y,
                ]
            )
    return 0.5 * raw + 0.0625 * beside_all


WIDE = 128
OWN = 64
ROOT2 = math.sqrt(2.0)
ROOT3 = math.sqrt(3.0)


def left(cells):
    return pltpu.roll(cells, 1, axis=1)


def right(cells):
    return pltpu.roll(cells, cells.shape[1] - 1, axis=1)


def above(cells):
    return pltpu.roll(cells, 1, axis=0)


def below(cells):
    return pltpu.roll(cells, cells.shape[0] - 1, axis=0)


def window_columns(shape, tile, half):
    lane = lax.broadcasted_iota(jnp.int32, shape, 1)
    shift = jnp.where(
        half == 0,
        jnp.where(lane >= 96, -WIDE, 0),
        jnp.where(lane < 32, WIDE, 0),
    )
    return tile * WIDE + lane + shift


def stencil_factors(factors, shot_cells_ref, pair, tile, half, nx, ny):
    shape = (2 * nx, WIDE)
    row = lax.broadcasted_iota(jnp.int32, shape, 0)
    second = row >= nx
    row = jnp.where(second, row - nx, row)
    col = window_columns(shape, tile, half)
    place = [
        jnp.where(second, shot_cells_ref[2 * pair + 1, d], shot_cells_ref[2 * pair, d]).astype(
            jnp.float32
        )
        for d in (0, 1)
    ]

    def surface(a, b):
        u = (row + a).astype(jnp.float32) - place[0]
        v = (col + b).astype(jnp.float32) - place[1]
        return SURF * jnp.sqrt(u * u + v * v)

    here = surface(0, 0)
    for slot, (a, b) in enumerate(((0, -1), (0, 1), (-1, 0), (1, 0))):
        inside = (row + a >= 0) & (row + a < nx) & (col + b >= 0) & (col + b < ny)
        beside = surface(a, b)
        penalty = jnp.where(inside, jnp.float32(0.0), jnp.float32(STEP_PENALTY))
        value = jnp.where(inside, beside, jnp.float32(0.0))
        factors[slot] = jnp.exp(-((value + penalty) - here) / SOFTMIN_TEMPER)
        factors[4 + slot] = jnp.where(inside, jnp.exp(-(here - beside) / SOFTMIN_TEMPER), 0.0)


def twice(cells):
    return jnp.concatenate([cells, cells], axis=0)


def forward_plane(k, speed, front, factors, fronts, spans):
    w1 = twice(jnp.exp(-speed / SOFTMIN_TEMPER))
    w2 = twice(jnp.exp(-(speed * ROOT2) / SOFTMIN_TEMPER))
    w3 = twice(jnp.exp(-(speed * ROOT3) / SOFTMIN_TEMPER))
    side = factors[0] * left(front) + factors[1] * right(front)
    edge = side + factors[2] * above(front) + factors[3] * below(front)
    corner = factors[2] * above(side) + factors[3] * below(side)
    one, two, three = w1 * front, w2 * edge, w3 * corner
    front = one + two + three
    fronts[k] = front
    spans[k] = one + ROOT2 * two + ROOT3 * three
    return front


def adjoint_plane(k, speed, back, source, reflector, factors, fronts, spans, inside, edges):
    w1 = twice(jnp.exp(-speed / SOFTMIN_TEMPER))
    w2 = twice(jnp.exp(-(speed * ROOT2) / SOFTMIN_TEMPER))
    w3 = twice(jnp.exp(-(speed * ROOT3) / SOFTMIN_TEMPER))
    lam = jnp.where(twice(reflector == k), source / fronts[k], 0.0) + back
    part = lam * spans[k] + jnp.where(twice(reflector >= k), source, 0.0)
    nx = speed.shape[0]
    raw = jnp.where(inside & (speed != AIR_SLOW), part[:nx] + part[nx:], 0.0)
    line = raw + left(raw) + right(raw)
    box = line + jnp.where(edges[0], 0.0, above(line)) + jnp.where(edges[1], 0.0, below(line))
    grad = 0.4375 * raw + 0.0625 * box
    two, three = w2 * lam, w3 * lam
    far = two + factors[4] * left(three) + factors[5] * right(three)
    back = (
        w1 * lam
        + (factors[4] * left(two) + factors[5] * right(two))
        + (factors[6] * above(far) + factors[7] * below(far))
    )
    return back, grad


def sweep_kernel(ny, shot_cells_ref, speed_ref, source_ref, reflector_ref, out_ref, factors, fronts, spans):
    depth = lax.axis_index("depth")
    half = lax.axis_index("gx")
    tile = 2 * lax.axis_index("gy") + lax.rem(depth, 2)
    nz, nx, _ = speed_ref.shape
    stencil_factors(factors, shot_cells_ref, depth // 2, tile, half, nx, ny)

    def forward(k, front):
        return forward_plane(k, speed_ref[k], front, factors, fronts, spans)

    lax.fori_loop(0, nz, forward, jnp.ones((2 * nx, WIDE), jnp.float32))
    source = source_ref[...]
    reflector = reflector_ref[...]
    col = window_columns((nx, WIDE), tile, half)
    row = lax.broadcasted_iota(jnp.int32, (nx, WIDE), 0)
    lane = lax.broadcasted_iota(jnp.int32, (nx, WIDE), 1)
    inside = (col >= 0) & (col < ny)
    mine = (lane // OWN) == half

    def adjoint(step, back):
        k = nz - 1 - step
        back, grad = adjoint_plane(
            k, speed_ref[k], back, source, reflector, factors, fronts, spans, inside, (row == 0, row == nx - 1)
        )
        out_ref[k] = jnp.where(mine, grad, 0.0)
        return back

    lax.fori_loop(0, nz, adjoint, jnp.zeros((2 * nx, WIDE), jnp.float32))


def local_split(slowness, air_mask, reflector, shot_cells, receiver_mask, residual):
    cz, bx, by = slowness.shape
    nz, nx, ny = cz * lax.axis_size("depth"), bx * lax.axis_size("gx"), by * lax.axis_size("gy")
    depth = lax.axis_index("depth")
    tile = 2 * lax.axis_index("gy") + lax.rem(depth, 2)
    half = lax.axis_index("gx")
    speed = jnp.where(air_mask == 1, jnp.float32(AIR_SLOW), slowness)
    speed = lax.all_gather(speed, ("depth",), axis=0, tiled=True)
    source = jnp.where(receiver_mask == 1, residual, jnp.float32(0.0))
    source = lax.dynamic_slice_in_dim(source, 2 * (depth // 2), 2, axis=0)
    fields = jnp.concatenate([speed, source, reflector.astype(jnp.float32)[None]], 0)
    fields = lax.all_gather(lax.all_gather(fields, "gx", axis=1, tiled=True), "gy", axis=2, tiled=True)
    near = lax.dynamic_slice_in_dim(fields, tile * WIDE, WIDE, axis=2)
    other = jnp.clip(tile + 2 * half - 1, 0, ny // WIDE - 1)
    far = lax.dynamic_slice_in_dim(fields, other * WIDE, WIDE, axis=2)
    lane = jnp.arange(WIDE)
    own = jnp.where(half == 0, lane < 96, lane >= 32)
    fields = jnp.where(own, near, far)
    out = pl.pallas_call(
        functools.partial(sweep_kernel, ny),
        out_shape=jax.ShapeDtypeStruct((nz, nx, WIDE), jnp.float32),
        in_specs=[pl.BlockSpec(memory_space=pltpu.SMEM)] + [pl.BlockSpec(memory_space=pltpu.VMEM)] * 3,
        out_specs=pl.BlockSpec(memory_space=pltpu.VMEM),
        scratch_shapes=[
            pltpu.VMEM((8, 2 * nx, WIDE), jnp.float32),
            pltpu.VMEM((nz, 2 * nx, WIDE), jnp.float32),
            pltpu.VMEM((nz, 2 * nx, WIDE), jnp.float32),
        ],
        compiler_params=pltpu.CompilerParams(vmem_limit_bytes=16 * 1024 * 1024),
    )(shot_cells, fields[:nz], fields[nz : nz + 2].reshape(2 * nx, WIDE), fields[nz + 2].astype(jnp.int32))
    zero = jnp.zeros_like(out)
    first = lax.rem(depth, 2) == 0
    out = jnp.concatenate([jnp.where(first, out, zero), jnp.where(first, zero, out)], axis=2)
    out = lax.psum_scatter(out, "depth", scatter_dimension=0, tiled=True)
    return lax.psum_scatter(out, "gx", scatter_dimension=1, tiled=True)


def solution(mesh):
    in_specs = (
        P("depth", "gx", "gy"),
        P("depth", "gx", "gy"),
        P("gx", "gy"),
        P(),
        P(None, "gx", "gy"),
        P(None, "gx", "gy"),
    )
    out_specs = P("depth", "gx", "gy")
    sizes = dict(mesh.shape)

    def whole(slowness, air_mask, reflector, shot_cells, receiver_mask, residual):
        nz, nx, ny = slowness.shape
        fits = (
            sizes == {"depth": 8, "gx": 2, "gy": 2}
            and (nz, nx, ny) == (16, 32, 512)
            and shot_cells.shape[0] == 8
        )
        local = local_split if fits else local_generic
        return jax.shard_map(local, mesh=mesh, in_specs=in_specs, out_specs=out_specs, check_vma=False)(
            slowness, air_mask, reflector, shot_cells, receiver_mask, residual
        )

    return whole
```

```python
import functools
import math

import jax
import jax.numpy as jnp
from jax import lax
from jax.experimental import pallas as pl
from jax.experimental.pallas import tpu as pltpu
from jax.sharding import PartitionSpec as P

SOFTMIN_TEMPER = 0.5
SURF = 0.7
AIR_SLOW = 2.5
STEP_PENALTY = 10000.0
STENCIL_SHIFTS = [
    (first_term, second_term) for first_term in (-1, 0, 1) for second_term in (-1, 0, 1)
]


def padded(cells, sides, width):
    for axis, dim in sides:
        count = lax.axis_size(axis)
        ends = count - 1
        head = lax.slice_in_dim(cells, 0, width, axis=dim)
        tail = lax.slice_in_dim(cells, cells.shape[dim] - width, cells.shape[dim], axis=dim)
        cells = jnp.concatenate(
            [
                lax.ppermute(tail, axis, [(i, (i + 1) % count) for i in range(ends)]),
                cells,
                lax.ppermute(head, axis, [((i + 1) % count, i) for i in range(ends)]),
            ],
            axis=dim,
        )
    return cells


def passed_along(value, axis, steps):
    count = lax.axis_size(axis)
    initial, last = (max(0, -steps), min(count, count - steps))
    return lax.ppermute(value, axis, [(source, source + steps) for source in range(initial, last)])


def soft_front(candidate_times):
    lowest = candidate_times[0]
    for cand in candidate_times[1:]:
        lowest = jnp.minimum(lowest, cand)
    total = jnp.exp(-(candidate_times[0] - lowest) / SOFTMIN_TEMPER)
    for cand in candidate_times[1:]:
        total = total + jnp.exp(-(cand - lowest) / SOFTMIN_TEMPER)
    return lowest - SOFTMIN_TEMPER * jnp.log(total)


def local_generic(slowness, air_mask, reflector, shot_cells, receiver_mask, residual):
    depth_count = lax.axis_size("depth")
    depth_pos = lax.axis_index("depth")
    cz, shift_along_x, shift_along_y = slowness.shape
    shots = shot_cells.shape[0]
    nx_total = shift_along_x * lax.axis_size("gx")
    ny_total = shift_along_y * lax.axis_size("gy")
    xpos = lax.axis_index("gx") * shift_along_x + jnp.arange(shift_along_x, dtype=jnp.int32)
    ypos = lax.axis_index("gy") * shift_along_y + jnp.arange(shift_along_y, dtype=jnp.int32)
    zpos = depth_pos * cz + jnp.arange(cz, dtype=jnp.int32)
    earth = air_mask == 0
    speed = jnp.where(air_mask == 1, jnp.float32(AIR_SLOW), slowness)
    shot_x = shot_cells[:, 0].astype(jnp.float32)
    shot_y = shot_cells[:, 1].astype(jnp.float32)
    surface = SURF * jnp.sqrt(
        (xpos.astype(jnp.float32)[None, :, None] - shot_x[:, None, None]) ** 2
        + (ypos.astype(jnp.float32)[None, None, :] - shot_y[:, None, None]) ** 2
    )
    penalty_terms = []
    span_lengths = []
    for first_term, second_term in STENCIL_SHIFTS:
        valid_mask = ((xpos + first_term >= 0) & (xpos + first_term < nx_total))[:, None] & (
            (ypos + second_term >= 0) & (ypos + second_term < ny_total)
        )[None, :]
        penalty_terms.append(jnp.where(valid_mask, jnp.float32(0.0), jnp.float32(STEP_PENALTY)))
        span_lengths.append(math.sqrt(1.0 + first_term * first_term + second_term * second_term))

    def sweep_plane(prior_layer, depth_layer):
        padded_layer = padded(prior_layer, (("gx", 1), ("gy", 2)), 1)
        candidate_times = [
            padded_layer[
                :,
                1 + first_term : 1 + first_term + shift_along_x,
                1 + second_term : 1 + second_term + shift_along_y,
            ]
            + depth_layer * span_lengths[stencil_index]
            + penalty_terms[stencil_index]
            for stencil_index, (first_term, second_term) in enumerate(STENCIL_SHIFTS)
        ]
        nxt = soft_front(candidate_times)
        return (nxt, nxt)

    def make_adjoint(source_block, count):

        def adjoint_plane(back, inputs):
            depth_layer, hit, previous_times, current_layer = inputs
            lam = source_block * hit[None] + back
            stacked = jnp.concatenate([lam, current_layer, previous_times, depth_layer[None]], 0)
            padded_layer = padded(stacked, (("gx", 1), ("gy", 2)), 1)
            lam_pad = padded_layer[:count]
            cur_pad = padded_layer[count : 2 * count]
            prev_pad = padded_layer[2 * count : 3 * count]
            layer_pad = padded_layer[3 * count]
            weight_sum = jnp.zeros_like(lam)
            back_new = jnp.zeros_like(lam)
            for stencil_index, (first_term, second_term) in enumerate(STENCIL_SHIFTS):
                lateral_value = prev_pad[
                    :,
                    1 + first_term : 1 + first_term + shift_along_x,
                    1 + second_term : 1 + second_term + shift_along_y,
                ]
                softmin_weight = jnp.exp(
                    -(
                        lateral_value
                        + depth_layer * span_lengths[stencil_index]
                        + penalty_terms[stencil_index]
                        - current_layer
                    )
                    / SOFTMIN_TEMPER
                )
                weight_sum = weight_sum + softmin_weight * span_lengths[stencil_index]
                lam_from = lam_pad[
                    :,
                    1 - first_term : 1 - first_term + shift_along_x,
                    1 - second_term : 1 - second_term + shift_along_y,
                ]
                cur_from = cur_pad[
                    :,
                    1 - first_term : 1 - first_term + shift_along_x,
                    1 - second_term : 1 - second_term + shift_along_y,
                ]
                layer_from = layer_pad[
                    1 - first_term : 1 - first_term + shift_along_x,
                    1 - second_term : 1 - second_term + shift_along_y,
                ]
                prob_from = jnp.exp(
                    -(previous_times + layer_from * span_lengths[stencil_index] - cur_from)
                    / SOFTMIN_TEMPER
                )
                back_new = back_new + lam_from * prob_from
            return (back_new, jnp.sum(lam * weight_sum, axis=0))

        return adjoint_plane

    source_all = jnp.where(receiver_mask == 1, residual, jnp.float32(0.0))
    blocks = 1
    width = shots // blocks
    rounds = depth_count + blocks - 1

    def forward_round(step, carry):
        incoming, store = carry
        group = step - depth_pos
        valid_mask = (group >= 0) & (group < blocks)
        top = jnp.where(depth_pos == 0, surface, incoming)
        last, planes = lax.scan(sweep_plane, top, speed)
        block = jnp.concatenate([top[None], planes], 0)
        old = store
        store = jnp.where(valid_mask, block, old)
        incoming = passed_along(last, "depth", 1)
        return (incoming, store)

    store = jnp.zeros((cz + 1, shots, shift_along_x, shift_along_y), jnp.float32)
    incoming = jnp.zeros((width, shift_along_x, shift_along_y), jnp.float32)
    incoming, store = lax.fori_loop(0, rounds, forward_round, (incoming, store))
    hits = (zpos[:, None, None] == reflector[None]).astype(jnp.float32)

    def adjoint_round(step, carry):
        incoming_back, grad_sum = carry
        group = step - (depth_count - 1 - depth_pos)
        valid_mask = (group >= 0) & (group < blocks)
        back_top, grads = lax.scan(
            make_adjoint(source_all, width),
            incoming_back,
            (speed, hits, store[:-1], store[1:]),
            reverse=True,
        )
        grad_sum = grad_sum + jnp.where(valid_mask, grads, jnp.float32(0.0))
        incoming_back = passed_along(back_top, "depth", -1)
        return (incoming_back, grad_sum)

    start_back = jnp.zeros((width, shift_along_x, shift_along_y), jnp.float32)
    grad_total = jnp.zeros((cz, shift_along_x, shift_along_y), jnp.float32)
    start_back, grad_total = lax.fori_loop(0, rounds, adjoint_round, (start_back, grad_total))
    colsum = jnp.sum(source_all, axis=0)
    below = zpos[:, None, None] <= reflector[None]
    raw = jnp.where(earth, grad_total, jnp.float32(0.0)) + jnp.where(
        earth & below, colsum[None], jnp.float32(0.0)
    )
    padded_layer = padded(raw, (("gx", 1), ("gy", 2)), 1)
    beside_all = jnp.zeros_like(raw)
    for first_term, second_term in STENCIL_SHIFTS:
        if first_term != 0 or second_term != 0:
            beside_all = (
                beside_all
                + padded_layer[
                    :,
                    1 + first_term : 1 + first_term + shift_along_x,
                    1 + second_term : 1 + second_term + shift_along_y,
                ]
            )
    return 0.5 * raw + 0.0625 * beside_all


WIDE = 128
OWN = 64
SIDE = 32
ROOT2 = math.sqrt(2.0)
ROOT3 = math.sqrt(3.0)


def left(cells):
    return pltpu.roll(cells, 1, axis=1)


def right(cells):
    return pltpu.roll(cells, cells.shape[1] - 1, axis=1)


def above(cells):
    return pltpu.roll(cells, 1, axis=0)


def below(cells):
    return pltpu.roll(cells, cells.shape[0] - 1, axis=0)


def halfway(cells):
    return pltpu.roll(cells, OWN, axis=cells.ndim - 1)


def lanes(shape):
    return lax.broadcasted_iota(jnp.int32, shape, len(shape) - 1)


def window_columns(shape, part):
    lane = lanes(shape)
    return part * OWN + lane - jnp.where(lane >= WIDE - SIDE, WIDE, 0)


def stencil_factors(factors, shot_cells_ref, pair, part, nx, ny):
    shape = (2 * nx, WIDE)
    row = lax.broadcasted_iota(jnp.int32, shape, 0)
    second = row >= nx
    row = jnp.where(second, row - nx, row)
    col = window_columns(shape, part)
    place = [
        jnp.where(second, shot_cells_ref[2 * pair + 1, d], shot_cells_ref[2 * pair, d]).astype(
            jnp.float32
        )
        for d in (0, 1)
    ]

    def surface(a, b):
        u = (row + a).astype(jnp.float32) - place[0]
        v = (col + b).astype(jnp.float32) - place[1]
        return SURF * jnp.sqrt(u * u + v * v)

    here = surface(0, 0)
    for slot, (a, b) in enumerate(((0, -1), (0, 1), (-1, 0), (1, 0))):
        inside = (row + a >= 0) & (row + a < nx) & (col + b >= 0) & (col + b < ny)
        beside = surface(a, b)
        penalty = jnp.where(inside, jnp.float32(0.0), jnp.float32(STEP_PENALTY))
        value = jnp.where(inside, beside, jnp.float32(0.0))
        factors[slot] = jnp.exp(-((value + penalty) - here) / SOFTMIN_TEMPER)
        factors[4 + slot] = jnp.where(inside, jnp.exp(-(here - beside) / SOFTMIN_TEMPER), 0.0)


def twice(cells):
    return jnp.concatenate([cells, cells], axis=0)


def forward_plane(k, speed, front, factors, fronts, spans):
    w1 = twice(jnp.exp(-speed / SOFTMIN_TEMPER))
    w2 = twice(jnp.exp(-(speed * ROOT2) / SOFTMIN_TEMPER))
    w3 = twice(jnp.exp(-(speed * ROOT3) / SOFTMIN_TEMPER))
    side = factors[0] * left(front) + factors[1] * right(front)
    edge = side + factors[2] * above(front) + factors[3] * below(front)
    corner = factors[2] * above(side) + factors[3] * below(side)
    one, two, three = w1 * front, w2 * edge, w3 * corner
    front = one + two + three
    fronts[k] = front
    spans[k] = one + ROOT2 * two + ROOT3 * three
    return front


def adjoint_plane(k, speed, back, source, reflector, factors, fronts, spans, inside, edges):
    w1 = twice(jnp.exp(-speed / SOFTMIN_TEMPER))
    w2 = twice(jnp.exp(-(speed * ROOT2) / SOFTMIN_TEMPER))
    w3 = twice(jnp.exp(-(speed * ROOT3) / SOFTMIN_TEMPER))
    plane = k.astype(jnp.float32)
    lam = jnp.where(twice(reflector == plane), source / fronts[k], 0.0) + back
    part = lam * spans[k] + jnp.where(twice(reflector >= plane), source, 0.0)
    nx = speed.shape[0]
    raw = jnp.where(inside & (speed != AIR_SLOW), part[:nx] + part[nx:], 0.0)
    line = raw + left(raw) + right(raw)
    box = line + jnp.where(edges[0], 0.0, above(line)) + jnp.where(edges[1], 0.0, below(line))
    grad = 0.4375 * raw + 0.0625 * box
    two, three = w2 * lam, w3 * lam
    far = two + factors[4] * left(three) + factors[5] * right(three)
    back = (
        w1 * lam
        + (factors[4] * left(two) + factors[5] * right(two))
        + (factors[6] * above(far) + factors[7] * below(far))
    )
    return back, grad


def part_window(part, x, first, second, beyond):
    lane = lanes(first.shape)
    if part == 0:
        return jnp.where(lane < WIDE - SIDE, first, jnp.where(x == 1, beyond, first))
    if part == 1:
        return halfway(jnp.where(lane >= SIDE, first, second))
    if part == 2:
        return jnp.where(lane < WIDE - SIDE, second, first)
    return halfway(jnp.where(lane >= SIDE, second, jnp.where(x == 0, beyond, second)))


def sweep_kernel(
    ny,
    shot_cells_ref,
    slowness_hbm,
    air_hbm,
    reflector_hbm,
    receiver_hbm,
    residual_hbm,
    out_ref,
    slowness,
    air,
    reflect,
    receiver,
    resid,
    rim_out,
    rim_in,
    wins,
    speeds,
    shots_rim_out,
    shots_rim_in,
    shots_side,
    fields,
    factors,
    fronts,
    spans,
    packed,
    sibling_sum,
    both,
    gathered,
    load_sem,
    rim_send,
    rim_recv,
    slab_send,
    slab_recv,
    pass_send,
    pass_recv,
    shots_send,
    shots_recv,
    side_send,
    side_recv,
    pair_send,
    pair_recv,
    sum_send,
    sum_recv,
):
    d = lax.axis_index("depth")
    g = lax.axis_index("gx")
    x = lax.axis_index("gy")
    cz, bx, _ = slowness.shape
    nd = speeds.shape[0] // cz
    nx = 2 * bx
    part = lax.rem(d, 4)
    quad = d // 4
    sibling = {"gx": 1 - g}
    across = {"gy": 1 - x}
    mine = pl.ds(pl.multiple_of(bx * g, bx), bx)
    theirs = pl.ds(pl.multiple_of(bx * (1 - g), bx), bx)
    shots = pl.ds(4 * quad, 4)

    loads = [
        pltpu.make_async_copy(source, target, load_sem.at[i])
        for i, (source, target) in enumerate(
            (
                (slowness_hbm, slowness),
                (air_hbm, air),
                (reflector_hbm, reflect),
                (receiver_hbm.at[shots], receiver),
                (residual_hbm.at[shots], resid),
            )
        )
    ]
    for load in loads:
        load.start()
    barrier = pltpu.get_barrier_semaphore()

    def greet(i, carry):
        pl.semaphore_signal(barrier, inc=1, device_id={"depth": lax.rem(d + i, nd)}, device_id_type=pl.DeviceIdType.MESH)
        return carry

    lax.fori_loop(1, nd, greet, 0)
    for peer in (sibling, across):
        pl.semaphore_signal(barrier, inc=1, device_id=peer, device_id_type=pl.DeviceIdType.MESH)

    def remote(source, target, send, recv, peer):
        return pltpu.make_async_remote_copy(
            src_ref=source,
            dst_ref=target,
            send_sem=send,
            recv_sem=recv,
            device_id=peer,
            device_id_type=pl.DeviceIdType.MESH,
        )

    loads[0].wait()
    loads[1].wait()
    speed = jnp.where(air[...] == 1, jnp.float32(AIR_SLOW), slowness[...])
    first, second = speed[:, :, :WIDE], speed[:, :, WIDE:]
    rim_out[...] = jnp.where(x == 0, second, first)
    for p in range(4):
        wins[p] = part_window(p, x, first, second, first)
    pl.semaphore_wait(barrier, nd + 1)

    rim = remote(rim_out, rim_in, rim_send, rim_recv, across)
    rim.start()
    late = 3 * (1 - x)

    def slab(target):
        return remote(
            wins.at[lax.rem(target, 4)],
            speeds.at[pl.ds(cz * d, cz), mine],
            slab_send.at[target],
            slab_recv.at[d],
            {"depth": target},
        )

    def send_early(i, carry):
        target = lax.rem(d + i, nd)

        @pl.when(lax.rem(target, 4) != late)
        def _():
            slab(target).start()

        return carry

    lax.fori_loop(1, nd, send_early, 0)
    for load in loads[2:]:
        load.wait()
    source = jnp.where(receiver[...] == 1, resid[...], jnp.float32(0.0))
    shots_rim_out[0:4] = jnp.where(x == 0, source[:, :, WIDE:], source[:, :, :WIDE])
    depth_of = reflect[...].astype(jnp.float32)
    shots_rim_out[4] = jnp.where(x == 0, depth_of[:, WIDE:], depth_of[:, :WIDE])
    shots_rim = remote(shots_rim_out, shots_rim_in, shots_send, shots_recv, across)
    shots_rim.start()

    rim.wait_recv()
    beyond = rim_in[...]
    wins[late] = jnp.where(
        x == 0, part_window(3, 0, first, second, beyond), part_window(0, 1, first, second, beyond)
    )
    for turn in range(2):
        target = lax.rem(late + 4 * ((quad + 1 + turn) % 2), nd)

        @pl.when(target != d)
        def _():
            slab(target).start()

    speeds[pl.ds(cz * d, cz), mine] = wins[part]
    stencil_factors(factors, shot_cells_ref, 2 * quad + g, 4 * x + part, nx, ny)

    shots_rim.wait_recv()

    def windowed(first, second, beyond):
        picks = [part_window(p, x, first, second, beyond) for p in range(4)]
        return jnp.where(
            part < 2, jnp.where(part == 0, picks[0], picks[1]), jnp.where(part == 2, picks[2], picks[3])
        )

    around = windowed(source[:, :, :WIDE], source[:, :, WIDE:], shots_rim_in[0:4])
    fields[0:2, mine] = jnp.where(g == 0, around[0:2], around[2:4])
    shots_side[0:2] = jnp.where(g == 0, around[2:4], around[0:2])
    around = windowed(depth_of[:, :WIDE], depth_of[:, WIDE:], shots_rim_in[4])
    fields[2, mine] = around
    shots_side[2] = around
    side = remote(shots_side, fields.at[:, mine], side_send, side_recv, sibling)
    side.start()

    def passing(s):
        block = speeds.at[pl.ds(cz * s, cz), mine]
        return remote(block, block, pass_send.at[s], pass_recv.at[s], sibling)

    def pass_on(s):
        @pl.when(s != d)
        def _():
            block = speeds.at[pl.ds(cz * s, cz), mine]
            remote(block, block, slab_send.at[s], slab_recv.at[s], sibling).wait_recv()

        passing(s).start()

    pass_on(0)

    def forward(s, front):
        @pl.when(s < nd - 1)
        def _():
            pass_on(s + 1)

        block = speeds.at[pl.ds(cz * s, cz), theirs]
        remote(block, block, pass_send.at[s], pass_recv.at[s], sibling).wait_recv()
        for i in range(2):
            k = 2 * s + i
            front = forward_plane(k, speeds[k], front, factors, fronts, spans)
        return front

    lax.fori_loop(0, nd, forward, jnp.ones((2 * nx, WIDE), jnp.float32))
    remote(shots_side, fields.at[:, theirs], side_send, side_recv, sibling).wait_recv()
    source = jnp.concatenate([fields[0], fields[1]], axis=0)
    reflector = fields[2]
    shape = (nx, WIDE)
    col = window_columns(shape, 4 * x + part)
    row = lax.broadcasted_iota(jnp.int32, shape, 0)
    lane = lanes(shape)
    inside = (col >= 0) & (col < ny)

    def pairing(s):
        return remote(packed.at[s, theirs], sibling_sum.at[s], pair_send.at[s], pair_recv.at[s], sibling)

    def summing(s):
        return remote(both.at[s], gathered.at[d], sum_send.at[s], sum_recv.at[d], {"depth": s})

    def hand_on(s):
        pairing(s).wait_recv()
        total = packed[s, mine] + sibling_sum[s]

        @pl.when(s == d)
        def _():
            gathered[s] = total

        @pl.when(s != d)
        def _():
            both[s] = total
            summing(s).start()

    def adjoint(step, back):
        s = nd - 1 - step
        grads = []
        for i in (1, 0):
            k = 2 * s + i
            back, grad = adjoint_plane(
                k, speeds[k], back, source, reflector, factors, fronts, spans, inside, (row == 0, row == nx - 1)
            )
            grads.append(grad)
        packed[s] = jnp.where(lane < OWN, grads[1], halfway(grads[0]))
        pairing(s).start()

        @pl.when(step > 0)
        def _():
            hand_on(s + 1)

        return back

    lax.fori_loop(0, nd, adjoint, jnp.zeros((2 * nx, WIDE), jnp.float32))
    hand_on(0)

    rim.wait_send()
    shots_rim.wait_send()
    side.wait_send()

    def finish(s, carry):
        passing(s).wait_send()
        pairing(s).wait_send()

        @pl.when(s != d)
        def _():
            slab(s).wait_send()
            summing(s).wait_send()
            remote(both.at[s], gathered.at[s], sum_send.at[s], sum_recv.at[s], {"depth": s}).wait_recv()

        return carry

    lax.fori_loop(0, nd, finish, 0)
    totals = [gathered[p] + gathered[4 + p] for p in range(4)]
    lane = lanes((bx, WIDE))
    for tile in range(2):
        low, high = totals[2 * tile], totals[2 * tile + 1]
        columns = slice(tile * WIDE, (tile + 1) * WIDE)
        out_ref[0, :, columns] = jnp.where(lane < OWN, low, halfway(high))
        out_ref[1, :, columns] = jnp.where(lane < OWN, halfway(low), high)


def local_split(slowness, air_mask, reflector, shot_cells, receiver_mask, residual):
    cz, bx, by = slowness.shape
    nd = lax.axis_size("depth")
    nz, nx, ny = cz * nd, bx * lax.axis_size("gx"), by * lax.axis_size("gy")
    f32, i32 = jnp.float32, jnp.int32
    dma = pltpu.SemaphoreType.DMA
    return pl.pallas_call(
        functools.partial(sweep_kernel, ny),
        out_shape=jax.ShapeDtypeStruct((cz, bx, by), f32),
        in_specs=[pl.BlockSpec(memory_space=pltpu.SMEM)] + [pl.BlockSpec(memory_space=pl.ANY)] * 5,
        out_specs=pl.BlockSpec(memory_space=pltpu.VMEM),
        scratch_shapes=[
            pltpu.VMEM((cz, bx, by), f32),
            pltpu.VMEM((cz, bx, by), i32),
            pltpu.VMEM((bx, by), i32),
            pltpu.VMEM((4, bx, by), i32),
            pltpu.VMEM((4, bx, by), f32),
            pltpu.VMEM((cz, bx, WIDE), f32),
            pltpu.VMEM((cz, bx, WIDE), f32),
            pltpu.VMEM((4, cz, bx, WIDE), f32),
            pltpu.VMEM((nz, nx, WIDE), f32),
            pltpu.VMEM((5, bx, WIDE), f32),
            pltpu.VMEM((5, bx, WIDE), f32),
            pltpu.VMEM((3, bx, WIDE), f32),
            pltpu.VMEM((3, nx, WIDE), f32),
            pltpu.VMEM((8, 2 * nx, WIDE), f32),
            pltpu.VMEM((nz, 2 * nx, WIDE), f32),
            pltpu.VMEM((nz, 2 * nx, WIDE), f32),
            pltpu.VMEM((nd, nx, WIDE), f32),
            pltpu.VMEM((nd, bx, WIDE), f32),
            pltpu.VMEM((nd, bx, WIDE), f32),
            pltpu.VMEM((nd, bx, WIDE), f32),
            dma((5,)),
            dma,
            dma,
            dma((nd,)),
            dma((nd,)),
            dma((nd,)),
            dma((nd,)),
            dma,
            dma,
            dma,
            dma,
            dma((nd,)),
            dma((nd,)),
            dma((nd,)),
            dma((nd,)),
        ],
        compiler_params=pltpu.CompilerParams(
            vmem_limit_bytes=16 * 1024 * 1024, collective_id=0, has_side_effects=True
        ),
    )(shot_cells, slowness, air_mask, reflector, receiver_mask, residual)


def solution(mesh):
    in_specs = (
        P("depth", "gx", "gy"),
        P("depth", "gx", "gy"),
        P("gx", "gy"),
        P(),
        P(None, "gx", "gy"),
        P(None, "gx", "gy"),
    )
    out_specs = P("depth", "gx", "gy")
    sizes = dict(mesh.shape)

    def whole(slowness, air_mask, reflector, shot_cells, receiver_mask, residual):
        nz, nx, ny = slowness.shape
        fits = (
            sizes == {"depth": 8, "gx": 2, "gy": 2}
            and (nz, nx, ny) == (16, 32, 512)
            and shot_cells.shape[0] == 8
        )
        local = local_split if fits else local_generic
        return jax.shard_map(local, mesh=mesh, in_specs=in_specs, out_specs=out_specs, check_vma=False)(
            slowness, air_mask, reflector, shot_cells, receiver_mask, residual
        )

    return whole
```

```python
import functools
import math

import jax
import jax.numpy as jnp
from jax import lax
from jax.experimental import pallas as pl
from jax.experimental.pallas import tpu as pltpu
from jax.sharding import PartitionSpec as P

SOFTMIN_TEMPER = 0.5
SURF = 0.7
AIR_SLOW = 2.5
STEP_PENALTY = 10000.0
STENCIL_SHIFTS = [
    (first_term, second_term) for first_term in (-1, 0, 1) for second_term in (-1, 0, 1)
]


def padded(cells, sides, width):
    for axis, dim in sides:
        count = lax.axis_size(axis)
        ends = count - 1
        head = lax.slice_in_dim(cells, 0, width, axis=dim)
        tail = lax.slice_in_dim(cells, cells.shape[dim] - width, cells.shape[dim], axis=dim)
        cells = jnp.concatenate(
            [
                lax.ppermute(tail, axis, [(i, (i + 1) % count) for i in range(ends)]),
                cells,
                lax.ppermute(head, axis, [((i + 1) % count, i) for i in range(ends)]),
            ],
            axis=dim,
        )
    return cells


def passed_along(value, axis, steps):
    count = lax.axis_size(axis)
    initial, last = (max(0, -steps), min(count, count - steps))
    return lax.ppermute(value, axis, [(source, source + steps) for source in range(initial, last)])


def soft_front(candidate_times):
    lowest = candidate_times[0]
    for cand in candidate_times[1:]:
        lowest = jnp.minimum(lowest, cand)
    total = jnp.exp(-(candidate_times[0] - lowest) / SOFTMIN_TEMPER)
    for cand in candidate_times[1:]:
        total = total + jnp.exp(-(cand - lowest) / SOFTMIN_TEMPER)
    return lowest - SOFTMIN_TEMPER * jnp.log(total)


def local_generic(slowness, air_mask, reflector, shot_cells, receiver_mask, residual):
    depth_count = lax.axis_size("depth")
    depth_pos = lax.axis_index("depth")
    cz, shift_along_x, shift_along_y = slowness.shape
    shots = shot_cells.shape[0]
    nx_total = shift_along_x * lax.axis_size("gx")
    ny_total = shift_along_y * lax.axis_size("gy")
    xpos = lax.axis_index("gx") * shift_along_x + jnp.arange(shift_along_x, dtype=jnp.int32)
    ypos = lax.axis_index("gy") * shift_along_y + jnp.arange(shift_along_y, dtype=jnp.int32)
    zpos = depth_pos * cz + jnp.arange(cz, dtype=jnp.int32)
    earth = air_mask == 0
    speed = jnp.where(air_mask == 1, jnp.float32(AIR_SLOW), slowness)
    shot_x = shot_cells[:, 0].astype(jnp.float32)
    shot_y = shot_cells[:, 1].astype(jnp.float32)
    surface = SURF * jnp.sqrt(
        (xpos.astype(jnp.float32)[None, :, None] - shot_x[:, None, None]) ** 2
        + (ypos.astype(jnp.float32)[None, None, :] - shot_y[:, None, None]) ** 2
    )
    penalty_terms = []
    span_lengths = []
    for first_term, second_term in STENCIL_SHIFTS:
        valid_mask = ((xpos + first_term >= 0) & (xpos + first_term < nx_total))[:, None] & (
            (ypos + second_term >= 0) & (ypos + second_term < ny_total)
        )[None, :]
        penalty_terms.append(jnp.where(valid_mask, jnp.float32(0.0), jnp.float32(STEP_PENALTY)))
        span_lengths.append(math.sqrt(1.0 + first_term * first_term + second_term * second_term))

    def sweep_plane(prior_layer, depth_layer):
        padded_layer = padded(prior_layer, (("gx", 1), ("gy", 2)), 1)
        candidate_times = [
            padded_layer[
                :,
                1 + first_term : 1 + first_term + shift_along_x,
                1 + second_term : 1 + second_term + shift_along_y,
            ]
            + depth_layer * span_lengths[stencil_index]
            + penalty_terms[stencil_index]
            for stencil_index, (first_term, second_term) in enumerate(STENCIL_SHIFTS)
        ]
        nxt = soft_front(candidate_times)
        return (nxt, nxt)

    def make_adjoint(source_block, count):

        def adjoint_plane(back, inputs):
            depth_layer, hit, previous_times, current_layer = inputs
            lam = source_block * hit[None] + back
            stacked = jnp.concatenate([lam, current_layer, previous_times, depth_layer[None]], 0)
            padded_layer = padded(stacked, (("gx", 1), ("gy", 2)), 1)
            lam_pad = padded_layer[:count]
            cur_pad = padded_layer[count : 2 * count]
            prev_pad = padded_layer[2 * count : 3 * count]
            layer_pad = padded_layer[3 * count]
            weight_sum = jnp.zeros_like(lam)
            back_new = jnp.zeros_like(lam)
            for stencil_index, (first_term, second_term) in enumerate(STENCIL_SHIFTS):
                lateral_value = prev_pad[
                    :,
                    1 + first_term : 1 + first_term + shift_along_x,
                    1 + second_term : 1 + second_term + shift_along_y,
                ]
                softmin_weight = jnp.exp(
                    -(
                        lateral_value
                        + depth_layer * span_lengths[stencil_index]
                        + penalty_terms[stencil_index]
                        - current_layer
                    )
                    / SOFTMIN_TEMPER
                )
                weight_sum = weight_sum + softmin_weight * span_lengths[stencil_index]
                lam_from = lam_pad[
                    :,
                    1 - first_term : 1 - first_term + shift_along_x,
                    1 - second_term : 1 - second_term + shift_along_y,
                ]
                cur_from = cur_pad[
                    :,
                    1 - first_term : 1 - first_term + shift_along_x,
                    1 - second_term : 1 - second_term + shift_along_y,
                ]
                layer_from = layer_pad[
                    1 - first_term : 1 - first_term + shift_along_x,
                    1 - second_term : 1 - second_term + shift_along_y,
                ]
                prob_from = jnp.exp(
                    -(previous_times + layer_from * span_lengths[stencil_index] - cur_from)
                    / SOFTMIN_TEMPER
                )
                back_new = back_new + lam_from * prob_from
            return (back_new, jnp.sum(lam * weight_sum, axis=0))

        return adjoint_plane

    source_all = jnp.where(receiver_mask == 1, residual, jnp.float32(0.0))
    blocks = 1
    width = shots // blocks
    rounds = depth_count + blocks - 1

    def forward_round(step, carry):
        incoming, store = carry
        group = step - depth_pos
        valid_mask = (group >= 0) & (group < blocks)
        top = jnp.where(depth_pos == 0, surface, incoming)
        last, planes = lax.scan(sweep_plane, top, speed)
        block = jnp.concatenate([top[None], planes], 0)
        old = store
        store = jnp.where(valid_mask, block, old)
        incoming = passed_along(last, "depth", 1)
        return (incoming, store)

    store = jnp.zeros((cz + 1, shots, shift_along_x, shift_along_y), jnp.float32)
    incoming = jnp.zeros((width, shift_along_x, shift_along_y), jnp.float32)
    incoming, store = lax.fori_loop(0, rounds, forward_round, (incoming, store))
    hits = (zpos[:, None, None] == reflector[None]).astype(jnp.float32)

    def adjoint_round(step, carry):
        incoming_back, grad_sum = carry
        group = step - (depth_count - 1 - depth_pos)
        valid_mask = (group >= 0) & (group < blocks)
        back_top, grads = lax.scan(
            make_adjoint(source_all, width),
            incoming_back,
            (speed, hits, store[:-1], store[1:]),
            reverse=True,
        )
        grad_sum = grad_sum + jnp.where(valid_mask, grads, jnp.float32(0.0))
        incoming_back = passed_along(back_top, "depth", -1)
        return (incoming_back, grad_sum)

    start_back = jnp.zeros((width, shift_along_x, shift_along_y), jnp.float32)
    grad_total = jnp.zeros((cz, shift_along_x, shift_along_y), jnp.float32)
    start_back, grad_total = lax.fori_loop(0, rounds, adjoint_round, (start_back, grad_total))
    colsum = jnp.sum(source_all, axis=0)
    below = zpos[:, None, None] <= reflector[None]
    raw = jnp.where(earth, grad_total, jnp.float32(0.0)) + jnp.where(
        earth & below, colsum[None], jnp.float32(0.0)
    )
    padded_layer = padded(raw, (("gx", 1), ("gy", 2)), 1)
    beside_all = jnp.zeros_like(raw)
    for first_term, second_term in STENCIL_SHIFTS:
        if first_term != 0 or second_term != 0:
            beside_all = (
                beside_all
                + padded_layer[
                    :,
                    1 + first_term : 1 + first_term + shift_along_x,
                    1 + second_term : 1 + second_term + shift_along_y,
                ]
            )
    return 0.5 * raw + 0.0625 * beside_all


WIDE = 128
OWN = 64
SIDE = 32
ROOT2 = math.sqrt(2.0)
ROOT3 = math.sqrt(3.0)


def left(cells):
    return pltpu.roll(cells, 1, axis=1)


def right(cells):
    return pltpu.roll(cells, cells.shape[1] - 1, axis=1)


def above(cells):
    return pltpu.roll(cells, 1, axis=0)


def below(cells):
    return pltpu.roll(cells, cells.shape[0] - 1, axis=0)


def halfway(cells):
    return pltpu.roll(cells, OWN, axis=cells.ndim - 1)


def lanes(shape):
    return lax.broadcasted_iota(jnp.int32, shape, len(shape) - 1)


def window_columns(shape, part):
    lane = lanes(shape)
    return part * OWN + lane - jnp.where(lane >= WIDE - SIDE, WIDE, 0)


def stencil_factors(factors, shot_cells_ref, pair, part, nx, ny):
    shape = (2 * nx, WIDE)
    row = lax.broadcasted_iota(jnp.int32, shape, 0)
    second = row >= nx
    row = jnp.where(second, row - nx, row)
    col = window_columns(shape, part)
    place = [
        jnp.where(second, shot_cells_ref[d, 2 * pair + 1], shot_cells_ref[d, 2 * pair]).astype(
            jnp.float32
        )
        for d in (0, 1)
    ]

    def surface(a, b):
        u = (row + a).astype(jnp.float32) - place[0]
        v = (col + b).astype(jnp.float32) - place[1]
        return SURF * jnp.sqrt(u * u + v * v)

    here = surface(0, 0)
    for slot, (a, b) in enumerate(((0, -1), (0, 1), (-1, 0), (1, 0))):
        inside = (row + a >= 0) & (row + a < nx) & (col + b >= 0) & (col + b < ny)
        beside = surface(a, b)
        penalty = jnp.where(inside, jnp.float32(0.0), jnp.float32(STEP_PENALTY))
        value = jnp.where(inside, beside, jnp.float32(0.0))
        factors[slot] = jnp.exp(-((value + penalty) - here) / SOFTMIN_TEMPER)
        factors[4 + slot] = jnp.where(inside, jnp.exp(-(here - beside) / SOFTMIN_TEMPER), 0.0)


def twice(cells):
    return jnp.concatenate([cells, cells], axis=0)


def forward_plane(k, speed, front, factors, fronts, spans):
    w1 = twice(jnp.exp(-speed / SOFTMIN_TEMPER))
    w2 = twice(jnp.exp(-(speed * ROOT2) / SOFTMIN_TEMPER))
    w3 = twice(jnp.exp(-(speed * ROOT3) / SOFTMIN_TEMPER))
    side = factors[0] * left(front) + factors[1] * right(front)
    edge = side + factors[2] * above(front) + factors[3] * below(front)
    corner = factors[2] * above(side) + factors[3] * below(side)
    one, two, three = w1 * front, w2 * edge, w3 * corner
    front = one + two + three
    fronts[k] = front
    spans[k] = one + ROOT2 * two + ROOT3 * three
    return front


def adjoint_plane(k, speed, back, source, reflector, factors, fronts, spans, inside, edges):
    w1 = twice(jnp.exp(-speed / SOFTMIN_TEMPER))
    w2 = twice(jnp.exp(-(speed * ROOT2) / SOFTMIN_TEMPER))
    w3 = twice(jnp.exp(-(speed * ROOT3) / SOFTMIN_TEMPER))
    plane = k.astype(jnp.float32)
    lam = jnp.where(twice(reflector == plane), source / fronts[k], 0.0) + back
    part = lam * spans[k] + jnp.where(twice(reflector >= plane), source, 0.0)
    nx = speed.shape[0]
    raw = jnp.where(inside & (speed != AIR_SLOW), part[:nx] + part[nx:], 0.0)
    line = raw + left(raw) + right(raw)
    box = line + jnp.where(edges[0], 0.0, above(line)) + jnp.where(edges[1], 0.0, below(line))
    grad = 0.4375 * raw + 0.0625 * box
    two, three = w2 * lam, w3 * lam
    far = two + factors[4] * left(three) + factors[5] * right(three)
    back = (
        w1 * lam
        + (factors[4] * left(two) + factors[5] * right(two))
        + (factors[6] * above(far) + factors[7] * below(far))
    )
    return back, grad


def part_window(part, x, first, second, beyond):
    lane = lanes(first.shape)
    if part == 0:
        return jnp.where(lane < WIDE - SIDE, first, jnp.where(x == 1, beyond, first))
    if part == 1:
        return halfway(jnp.where(lane >= SIDE, first, second))
    if part == 2:
        return jnp.where(lane < WIDE - SIDE, second, first)
    return halfway(jnp.where(lane >= SIDE, second, jnp.where(x == 0, beyond, second)))


def sweep_kernel(
    ny,
    shot_cells_hbm,
    slowness_hbm,
    air_hbm,
    reflector_hbm,
    receiver_hbm,
    residual_hbm,
    out_ref,
    shot_cells_ref,
    slowness,
    air,
    reflect,
    receiver,
    resid,
    rim_out,
    rim_in,
    wins,
    speeds,
    shots_rim_out,
    shots_rim_in,
    shots_side,
    fields,
    factors,
    fronts,
    spans,
    packed,
    sibling_sum,
    both,
    gathered,
    load_sem,
    rim_send,
    rim_recv,
    slab_send,
    slab_recv,
    pass_send,
    pass_recv,
    shots_send,
    shots_recv,
    side_send,
    side_recv,
    pair_send,
    pair_recv,
    sum_send,
    sum_recv,
):
    d = lax.axis_index("depth")
    g = lax.axis_index("gx")
    x = lax.axis_index("gy")
    cz, bx, _ = slowness.shape
    nd = speeds.shape[0] // cz
    nx = 2 * bx
    part = lax.rem(d, 4)
    quad = d // 4
    sibling = {"gx": 1 - g}
    across = {"gy": 1 - x}
    mine = pl.ds(pl.multiple_of(bx * g, bx), bx)
    theirs = pl.ds(pl.multiple_of(bx * (1 - g), bx), bx)
    shots = pl.ds(4 * quad, 4)

    loads = [
        pltpu.make_async_copy(source, target, load_sem.at[i])
        for i, (source, target) in enumerate(
            (
                (slowness_hbm, slowness),
                (air_hbm, air),
                (reflector_hbm, reflect),
                (receiver_hbm.at[shots], receiver),
                (residual_hbm.at[shots], resid),
                (shot_cells_hbm, shot_cells_ref),
            )
        )
    ]
    for load in loads:
        load.start()
    barrier = pltpu.get_barrier_semaphore()

    def greet(i, carry):
        pl.semaphore_signal(barrier, inc=1, device_id={"depth": lax.rem(d + i, nd)}, device_id_type=pl.DeviceIdType.MESH)
        return carry

    lax.fori_loop(1, nd, greet, 0)
    for peer in (sibling, across):
        pl.semaphore_signal(barrier, inc=1, device_id=peer, device_id_type=pl.DeviceIdType.MESH)

    def remote(source, target, send, recv, peer):
        return pltpu.make_async_remote_copy(
            src_ref=source,
            dst_ref=target,
            send_sem=send,
            recv_sem=recv,
            device_id=peer,
            device_id_type=pl.DeviceIdType.MESH,
        )

    loads[0].wait()
    loads[1].wait()
    speed = jnp.where(air[...] == 1, jnp.float32(AIR_SLOW), slowness[...])
    first, second = speed[:, :, :WIDE], speed[:, :, WIDE:]
    rim_out[...] = jnp.where(x == 0, second, first)
    for p in range(4):
        wins[p] = part_window(p, x, first, second, first)
    pl.semaphore_wait(barrier, nd + 1)

    rim = remote(rim_out, rim_in, rim_send, rim_recv, across)
    rim.start()
    late = 3 * (1 - x)

    def slab(target):
        return remote(
            wins.at[lax.rem(target, 4)],
            speeds.at[pl.ds(cz * d, cz), mine],
            slab_send,
            slab_recv.at[d],
            {"depth": target},
        )

    def send_early(i, carry):
        target = lax.rem(d + i, nd)

        @pl.when(lax.rem(target, 4) != late)
        def _():
            slab(target).start()

        return carry

    lax.fori_loop(1, nd, send_early, 0)
    for load in loads[2:]:
        load.wait()
    source = jnp.where(receiver[...] == 1, resid[...], jnp.float32(0.0))
    shots_rim_out[0:4] = jnp.where(x == 0, source[:, :, WIDE:], source[:, :, :WIDE])
    depth_of = reflect[...].astype(jnp.float32)
    shots_rim_out[4] = jnp.where(x == 0, depth_of[:, WIDE:], depth_of[:, :WIDE])
    shots_rim = remote(shots_rim_out, shots_rim_in, shots_send, shots_recv, across)
    shots_rim.start()

    rim.wait_recv()
    beyond = rim_in[...]
    wins[late] = jnp.where(
        x == 0, part_window(3, 0, first, second, beyond), part_window(0, 1, first, second, beyond)
    )
    for turn in range(2):
        target = lax.rem(late + 4 * ((quad + 1 + turn) % 2), nd)

        @pl.when(target != d)
        def _():
            slab(target).start()

    def passing(s):
        block = speeds.at[pl.ds(cz * s, cz), mine]
        return remote(block, block, pass_send, pass_recv.at[s], sibling)

    speeds[pl.ds(cz * d, cz), mine] = wins[part]
    passing(d).start()
    stencil_factors(factors, shot_cells_ref, 2 * quad + g, 4 * x + part, nx, ny)

    shots_rim.wait_recv()

    def windowed(first, second, beyond):
        picks = [part_window(p, x, first, second, beyond) for p in range(4)]
        return jnp.where(
            part < 2, jnp.where(part == 0, picks[0], picks[1]), jnp.where(part == 2, picks[2], picks[3])
        )

    around = windowed(source[:, :, :WIDE], source[:, :, WIDE:], shots_rim_in[0:4])
    fields[0:2, mine] = jnp.where(g == 0, around[0:2], around[2:4])
    shots_side[0:2] = jnp.where(g == 0, around[2:4], around[0:2])
    around = windowed(depth_of[:, :WIDE], depth_of[:, WIDE:], shots_rim_in[4])
    fields[2, mine] = around
    shots_side[2] = around
    side = remote(shots_side, fields.at[:, mine], side_send, side_recv, sibling)
    side.start()

    def pass_on(s):
        @pl.when(s != d)
        def _():
            block = speeds.at[pl.ds(cz * s, cz), mine]
            remote(block, block, slab_send, slab_recv.at[s], sibling).wait_recv()
            passing(s).start()

    pass_on(0)

    def forward(s, front):
        @pl.when(s < nd - 1)
        def _():
            pass_on(s + 1)

        block = speeds.at[pl.ds(cz * s, cz), theirs]
        remote(block, block, pass_send, pass_recv.at[s], sibling).wait_recv()
        for i in range(2):
            k = 2 * s + i
            front = forward_plane(k, speeds[k], front, factors, fronts, spans)
        return front

    lax.fori_loop(0, nd, forward, jnp.ones((2 * nx, WIDE), jnp.float32))
    remote(shots_side, fields.at[:, theirs], side_send, side_recv, sibling).wait_recv()
    source = jnp.concatenate([fields[0], fields[1]], axis=0)
    reflector = fields[2]
    shape = (nx, WIDE)
    col = window_columns(shape, 4 * x + part)
    row = lax.broadcasted_iota(jnp.int32, shape, 0)
    lane = lanes(shape)
    inside = (col >= 0) & (col < ny)

    def pairing(s):
        return remote(packed.at[s, theirs], sibling_sum.at[s], pair_send, pair_recv.at[s], sibling)

    def summing(s):
        return remote(both.at[s], gathered.at[d], sum_send, sum_recv, {"depth": s})

    def hand_on(s):
        pairing(s).wait_recv()
        total = packed[s, mine] + sibling_sum[s]

        @pl.when(s == d)
        def _():
            gathered[s] = total

        @pl.when(s != d)
        def _():
            both[s] = total
            summing(s).start()

    def adjoint(step, back):
        s = nd - 1 - step
        grads = []
        for i in (1, 0):
            k = 2 * s + i
            back, grad = adjoint_plane(
                k, speeds[k], back, source, reflector, factors, fronts, spans, inside, (row == 0, row == nx - 1)
            )
            grads.append(grad)
        packed[s] = jnp.where(lane < OWN, grads[1], halfway(grads[0]))
        pairing(s).start()

        @pl.when(step > 0)
        def _():
            hand_on(s + 1)

        return back

    lax.fori_loop(0, nd, adjoint, jnp.zeros((2 * nx, WIDE), jnp.float32))
    hand_on(0)

    rim.wait_send()
    shots_rim.wait_send()
    side.wait_send()
    others = speeds.at[pl.ds(0, cz * (nd - 1)), mine]
    remote(others, others, slab_send, rim_recv, sibling).wait_send()
    block = speeds.at[:, mine]
    remote(block, block, pass_send, rim_recv, sibling).wait_send()
    remote(packed.at[:, theirs], sibling_sum, pair_send, rim_recv, sibling).wait_send()
    block = gathered.at[pl.ds(0, nd - 1)]
    remote(block, block, rim_send, sum_recv, sibling).wait_recv()
    remote(block, block, sum_send, rim_recv, sibling).wait_send()
    totals = [gathered[p] + gathered[4 + p] for p in range(4)]
    lane = lanes((bx, WIDE))
    for tile in range(2):
        low, high = totals[2 * tile], totals[2 * tile + 1]
        columns = slice(tile * WIDE, (tile + 1) * WIDE)
        out_ref[0, :, columns] = jnp.where(lane < OWN, low, halfway(high))
        out_ref[1, :, columns] = jnp.where(lane < OWN, halfway(low), high)


def local_split(slowness, air_mask, reflector, shot_cells, receiver_mask, residual):
    cz, bx, by = slowness.shape
    nd = lax.axis_size("depth")
    nz, nx, ny = cz * nd, bx * lax.axis_size("gx"), by * lax.axis_size("gy")
    f32, i32 = jnp.float32, jnp.int32
    dma = pltpu.SemaphoreType.DMA
    return pl.pallas_call(
        functools.partial(sweep_kernel, ny),
        out_shape=jax.ShapeDtypeStruct((cz, bx, by), f32),
        in_specs=[pl.BlockSpec(memory_space=pltpu.HBM)] * 6,
        out_specs=pl.BlockSpec(memory_space=pltpu.VMEM),
        scratch_shapes=[
            pltpu.SMEM(shot_cells.shape[::-1], i32),
            pltpu.VMEM((cz, bx, by), f32),
            pltpu.VMEM((cz, bx, by), i32),
            pltpu.VMEM((bx, by), i32),
            pltpu.VMEM((4, bx, by), i32),
            pltpu.VMEM((4, bx, by), f32),
            pltpu.VMEM((cz, bx, WIDE), f32),
            pltpu.VMEM((cz, bx, WIDE), f32),
            pltpu.VMEM((4, cz, bx, WIDE), f32),
            pltpu.VMEM((nz, nx, WIDE), f32),
            pltpu.VMEM((5, bx, WIDE), f32),
            pltpu.VMEM((5, bx, WIDE), f32),
            pltpu.VMEM((3, bx, WIDE), f32),
            pltpu.VMEM((3, nx, WIDE), f32),
            pltpu.VMEM((8, 2 * nx, WIDE), f32),
            pltpu.VMEM((nz, 2 * nx, WIDE), f32),
            pltpu.VMEM((nz, 2 * nx, WIDE), f32),
            pltpu.VMEM((nd, nx, WIDE), f32),
            pltpu.VMEM((nd, bx, WIDE), f32),
            pltpu.VMEM((nd, bx, WIDE), f32),
            pltpu.VMEM((nd, bx, WIDE), f32),
            dma((6,)),
            dma,
            dma,
            dma,
            dma((nd,)),
            dma,
            dma((nd,)),
            dma,
            dma,
            dma,
            dma,
            dma,
            dma((nd,)),
            dma,
            dma,
        ],
        compiler_params=pltpu.CompilerParams(
            vmem_limit_bytes=60 * 1024 * 1024, collective_id=0, has_side_effects=True
        ),
    )(shot_cells.T, slowness, air_mask, reflector, receiver_mask, residual)


def solution(mesh):
    in_specs = (
        P("depth", "gx", "gy"),
        P("depth", "gx", "gy"),
        P("gx", "gy"),
        P(),
        P(None, "gx", "gy"),
        P(None, "gx", "gy"),
    )
    out_specs = P("depth", "gx", "gy")
    sizes = dict(mesh.shape)

    def whole(slowness, air_mask, reflector, shot_cells, receiver_mask, residual):
        nz, nx, ny = slowness.shape
        fits = (
            sizes == {"depth": 8, "gx": 2, "gy": 2}
            and (nz, nx, ny) == (16, 32, 512)
            and shot_cells.shape[0] == 8
        )
        local = local_split if fits else local_generic
        return jax.shard_map(local, mesh=mesh, in_specs=in_specs, out_specs=out_specs, check_vma=False)(
            slowness, air_mask, reflector, shot_cells, receiver_mask, residual
        )

    return whole
```

```python
import functools
import math

import jax
import jax.numpy as jnp
from jax import lax
from jax.experimental import pallas as pl
from jax.experimental.pallas import tpu as pltpu
from jax.sharding import PartitionSpec as P

SOFTMIN_TEMPER = 0.5
SURF = 0.7
AIR_SLOW = 2.5
STEP_PENALTY = 10000.0
STENCIL_SHIFTS = [
    (first_term, second_term) for first_term in (-1, 0, 1) for second_term in (-1, 0, 1)
]


def padded(cells, sides, width):
    for axis, dim in sides:
        count = lax.axis_size(axis)
        ends = count - 1
        head = lax.slice_in_dim(cells, 0, width, axis=dim)
        tail = lax.slice_in_dim(cells, cells.shape[dim] - width, cells.shape[dim], axis=dim)
        cells = jnp.concatenate(
            [
                lax.ppermute(tail, axis, [(i, (i + 1) % count) for i in range(ends)]),
                cells,
                lax.ppermute(head, axis, [((i + 1) % count, i) for i in range(ends)]),
            ],
            axis=dim,
        )
    return cells


def passed_along(value, axis, steps):
    count = lax.axis_size(axis)
    initial, last = (max(0, -steps), min(count, count - steps))
    return lax.ppermute(value, axis, [(source, source + steps) for source in range(initial, last)])


def soft_front(candidate_times):
    lowest = candidate_times[0]
    for cand in candidate_times[1:]:
        lowest = jnp.minimum(lowest, cand)
    total = jnp.exp(-(candidate_times[0] - lowest) / SOFTMIN_TEMPER)
    for cand in candidate_times[1:]:
        total = total + jnp.exp(-(cand - lowest) / SOFTMIN_TEMPER)
    return lowest - SOFTMIN_TEMPER * jnp.log(total)


def local_generic(slowness, air_mask, reflector, shot_cells, receiver_mask, residual):
    depth_count = lax.axis_size("depth")
    depth_pos = lax.axis_index("depth")
    cz, shift_along_x, shift_along_y = slowness.shape
    shots = shot_cells.shape[0]
    nx_total = shift_along_x * lax.axis_size("gx")
    ny_total = shift_along_y * lax.axis_size("gy")
    xpos = lax.axis_index("gx") * shift_along_x + jnp.arange(shift_along_x, dtype=jnp.int32)
    ypos = lax.axis_index("gy") * shift_along_y + jnp.arange(shift_along_y, dtype=jnp.int32)
    zpos = depth_pos * cz + jnp.arange(cz, dtype=jnp.int32)
    earth = air_mask == 0
    speed = jnp.where(air_mask == 1, jnp.float32(AIR_SLOW), slowness)
    shot_x = shot_cells[:, 0].astype(jnp.float32)
    shot_y = shot_cells[:, 1].astype(jnp.float32)
    surface = SURF * jnp.sqrt(
        (xpos.astype(jnp.float32)[None, :, None] - shot_x[:, None, None]) ** 2
        + (ypos.astype(jnp.float32)[None, None, :] - shot_y[:, None, None]) ** 2
    )
    penalty_terms = []
    span_lengths = []
    for first_term, second_term in STENCIL_SHIFTS:
        valid_mask = ((xpos + first_term >= 0) & (xpos + first_term < nx_total))[:, None] & (
            (ypos + second_term >= 0) & (ypos + second_term < ny_total)
        )[None, :]
        penalty_terms.append(jnp.where(valid_mask, jnp.float32(0.0), jnp.float32(STEP_PENALTY)))
        span_lengths.append(math.sqrt(1.0 + first_term * first_term + second_term * second_term))

    def sweep_plane(prior_layer, depth_layer):
        padded_layer = padded(prior_layer, (("gx", 1), ("gy", 2)), 1)
        candidate_times = [
            padded_layer[
                :,
                1 + first_term : 1 + first_term + shift_along_x,
                1 + second_term : 1 + second_term + shift_along_y,
            ]
            + depth_layer * span_lengths[stencil_index]
            + penalty_terms[stencil_index]
            for stencil_index, (first_term, second_term) in enumerate(STENCIL_SHIFTS)
        ]
        nxt = soft_front(candidate_times)
        return (nxt, nxt)

    def make_adjoint(source_block, count):

        def adjoint_plane(back, inputs):
            depth_layer, hit, previous_times, current_layer = inputs
            lam = source_block * hit[None] + back
            stacked = jnp.concatenate([lam, current_layer, previous_times, depth_layer[None]], 0)
            padded_layer = padded(stacked, (("gx", 1), ("gy", 2)), 1)
            lam_pad = padded_layer[:count]
            cur_pad = padded_layer[count : 2 * count]
            prev_pad = padded_layer[2 * count : 3 * count]
            layer_pad = padded_layer[3 * count]
            weight_sum = jnp.zeros_like(lam)
            back_new = jnp.zeros_like(lam)
            for stencil_index, (first_term, second_term) in enumerate(STENCIL_SHIFTS):
                lateral_value = prev_pad[
                    :,
                    1 + first_term : 1 + first_term + shift_along_x,
                    1 + second_term : 1 + second_term + shift_along_y,
                ]
                softmin_weight = jnp.exp(
                    -(
                        lateral_value
                        + depth_layer * span_lengths[stencil_index]
                        + penalty_terms[stencil_index]
                        - current_layer
                    )
                    / SOFTMIN_TEMPER
                )
                weight_sum = weight_sum + softmin_weight * span_lengths[stencil_index]
                lam_from = lam_pad[
                    :,
                    1 - first_term : 1 - first_term + shift_along_x,
                    1 - second_term : 1 - second_term + shift_along_y,
                ]
                cur_from = cur_pad[
                    :,
                    1 - first_term : 1 - first_term + shift_along_x,
                    1 - second_term : 1 - second_term + shift_along_y,
                ]
                layer_from = layer_pad[
                    1 - first_term : 1 - first_term + shift_along_x,
                    1 - second_term : 1 - second_term + shift_along_y,
                ]
                prob_from = jnp.exp(
                    -(previous_times + layer_from * span_lengths[stencil_index] - cur_from)
                    / SOFTMIN_TEMPER
                )
                back_new = back_new + lam_from * prob_from
            return (back_new, jnp.sum(lam * weight_sum, axis=0))

        return adjoint_plane

    source_all = jnp.where(receiver_mask == 1, residual, jnp.float32(0.0))
    blocks = 1
    width = shots // blocks
    rounds = depth_count + blocks - 1

    def forward_round(step, carry):
        incoming, store = carry
        group = step - depth_pos
        valid_mask = (group >= 0) & (group < blocks)
        top = jnp.where(depth_pos == 0, surface, incoming)
        last, planes = lax.scan(sweep_plane, top, speed)
        block = jnp.concatenate([top[None], planes], 0)
        old = store
        store = jnp.where(valid_mask, block, old)
        incoming = passed_along(last, "depth", 1)
        return (incoming, store)

    store = jnp.zeros((cz + 1, shots, shift_along_x, shift_along_y), jnp.float32)
    incoming = jnp.zeros((width, shift_along_x, shift_along_y), jnp.float32)
    incoming, store = lax.fori_loop(0, rounds, forward_round, (incoming, store))
    hits = (zpos[:, None, None] == reflector[None]).astype(jnp.float32)

    def adjoint_round(step, carry):
        incoming_back, grad_sum = carry
        group = step - (depth_count - 1 - depth_pos)
        valid_mask = (group >= 0) & (group < blocks)
        back_top, grads = lax.scan(
            make_adjoint(source_all, width),
            incoming_back,
            (speed, hits, store[:-1], store[1:]),
            reverse=True,
        )
        grad_sum = grad_sum + jnp.where(valid_mask, grads, jnp.float32(0.0))
        incoming_back = passed_along(back_top, "depth", -1)
        return (incoming_back, grad_sum)

    start_back = jnp.zeros((width, shift_along_x, shift_along_y), jnp.float32)
    grad_total = jnp.zeros((cz, shift_along_x, shift_along_y), jnp.float32)
    start_back, grad_total = lax.fori_loop(0, rounds, adjoint_round, (start_back, grad_total))
    colsum = jnp.sum(source_all, axis=0)
    below = zpos[:, None, None] <= reflector[None]
    raw = jnp.where(earth, grad_total, jnp.float32(0.0)) + jnp.where(
        earth & below, colsum[None], jnp.float32(0.0)
    )
    padded_layer = padded(raw, (("gx", 1), ("gy", 2)), 1)
    beside_all = jnp.zeros_like(raw)
    for first_term, second_term in STENCIL_SHIFTS:
        if first_term != 0 or second_term != 0:
            beside_all = (
                beside_all
                + padded_layer[
                    :,
                    1 + first_term : 1 + first_term + shift_along_x,
                    1 + second_term : 1 + second_term + shift_along_y,
                ]
            )
    return 0.5 * raw + 0.0625 * beside_all


WIDE = 128
OWN = 64
SIDE = 32
ROOT2 = math.sqrt(2.0)
ROOT3 = math.sqrt(3.0)


def left(cells):
    return pltpu.roll(cells, 1, axis=1)


def right(cells):
    return pltpu.roll(cells, cells.shape[1] - 1, axis=1)


def above(cells):
    return pltpu.roll(cells, 1, axis=0)


def below(cells):
    return pltpu.roll(cells, cells.shape[0] - 1, axis=0)


def halfway(cells):
    return pltpu.roll(cells, OWN, axis=cells.ndim - 1)


def lanes(shape):
    return lax.broadcasted_iota(jnp.int32, shape, len(shape) - 1)


def window_columns(shape, part):
    lane = lanes(shape)
    return part * OWN + lane - jnp.where(lane >= WIDE - SIDE, WIDE, 0)


def stencil_factors(factors, shot_cells_ref, pair, part, nx, ny):
    shape = (2 * nx, WIDE)
    row = lax.broadcasted_iota(jnp.int32, shape, 0)
    second = row >= nx
    row = jnp.where(second, row - nx, row)
    col = window_columns(shape, part)
    place = [
        jnp.where(second, shot_cells_ref[d, 2 * pair + 1], shot_cells_ref[d, 2 * pair]).astype(
            jnp.float32
        )
        for d in (0, 1)
    ]

    def surface(a, b):
        u = (row + a).astype(jnp.float32) - place[0]
        v = (col + b).astype(jnp.float32) - place[1]
        return SURF * jnp.sqrt(u * u + v * v)

    here = surface(0, 0)
    for slot, (a, b) in enumerate(((0, -1), (0, 1), (-1, 0), (1, 0))):
        inside = (row + a >= 0) & (row + a < nx) & (col + b >= 0) & (col + b < ny)
        beside = surface(a, b)
        penalty = jnp.where(inside, jnp.float32(0.0), jnp.float32(STEP_PENALTY))
        value = jnp.where(inside, beside, jnp.float32(0.0))
        factors[slot] = jnp.exp(-((value + penalty) - here) / SOFTMIN_TEMPER)
        factors[4 + slot] = jnp.where(inside, jnp.exp(-(here - beside) / SOFTMIN_TEMPER), 0.0)


def twice(cells):
    return jnp.concatenate([cells, cells], axis=0)


def forward_plane(k, speed, front, factors, fronts, spans):
    w1 = twice(jnp.exp(-speed / SOFTMIN_TEMPER))
    w2 = twice(jnp.exp(-(speed * ROOT2) / SOFTMIN_TEMPER))
    w3 = twice(jnp.exp(-(speed * ROOT3) / SOFTMIN_TEMPER))
    side = factors[0] * left(front) + factors[1] * right(front)
    edge = side + factors[2] * above(front) + factors[3] * below(front)
    corner = factors[2] * above(side) + factors[3] * below(side)
    one, two, three = w1 * front, w2 * edge, w3 * corner
    front = one + two + three
    fronts[k] = front
    spans[k] = one + ROOT2 * two + ROOT3 * three
    return front


def adjoint_plane(k, speed, back, source, reflector, factors, fronts, spans, inside, edges):
    w1 = twice(jnp.exp(-speed / SOFTMIN_TEMPER))
    w2 = twice(jnp.exp(-(speed * ROOT2) / SOFTMIN_TEMPER))
    w3 = twice(jnp.exp(-(speed * ROOT3) / SOFTMIN_TEMPER))
    plane = k.astype(jnp.float32)
    lam = jnp.where(twice(reflector == plane), source / fronts[k], 0.0) + back
    part = lam * spans[k] + jnp.where(twice(reflector >= plane), source, 0.0)
    nx = speed.shape[0]
    raw = jnp.where(inside & (speed != AIR_SLOW), part[:nx] + part[nx:], 0.0)
    line = raw + left(raw) + right(raw)
    box = line + jnp.where(edges[0], 0.0, above(line)) + jnp.where(edges[1], 0.0, below(line))
    grad = 0.4375 * raw + 0.0625 * box
    two, three = w2 * lam, w3 * lam
    far = two + factors[4] * left(three) + factors[5] * right(three)
    back = (
        w1 * lam
        + (factors[4] * left(two) + factors[5] * right(two))
        + (factors[6] * above(far) + factors[7] * below(far))
    )
    return back, grad


def part_window(part, x, first, second, beyond):
    lane = lanes(first.shape)
    if part == 0:
        return jnp.where(lane < WIDE - SIDE, first, jnp.where(x == 1, beyond, first))
    if part == 1:
        return halfway(jnp.where(lane >= SIDE, first, second))
    if part == 2:
        return jnp.where(lane < WIDE - SIDE, second, first)
    return halfway(jnp.where(lane >= SIDE, second, jnp.where(x == 0, beyond, second)))


def sweep_kernel(
    ny,
    shot_cells_hbm,
    slowness_hbm,
    air_hbm,
    reflector_hbm,
    receiver_hbm,
    residual_hbm,
    out_ref,
    shot_cells_ref,
    slowness,
    air,
    reflect,
    receiver,
    resid,
    rim_out,
    rim_in,
    wins,
    speeds,
    shots_rim_out,
    shots_rim_in,
    shots_side,
    fields,
    factors,
    fronts,
    spans,
    packed,
    gathered,
    load_sem,
    rim_send,
    rim_recv,
    slab_send,
    slab_recv,
    pass_send,
    pass_recv,
    shots_send,
    shots_recv,
    side_send,
    side_recv,
    sum_send,
    sum_recv,
):
    d = lax.axis_index("depth")
    g = lax.axis_index("gx")
    x = lax.axis_index("gy")
    cz, bx, _ = slowness.shape
    nd = speeds.shape[0] // cz
    nx = 2 * bx
    part = lax.rem(d, 4)
    quad = d // 4
    sibling = {"gx": 1 - g}
    across = {"gy": 1 - x}
    mine = pl.ds(pl.multiple_of(bx * g, bx), bx)
    theirs = pl.ds(pl.multiple_of(bx * (1 - g), bx), bx)
    shots = pl.ds(4 * quad, 4)

    loads = [
        pltpu.make_async_copy(source, target, load_sem.at[i])
        for i, (source, target) in enumerate(
            (
                (slowness_hbm, slowness),
                (air_hbm, air),
                (reflector_hbm, reflect),
                (receiver_hbm.at[shots], receiver),
                (residual_hbm.at[shots], resid),
                (shot_cells_hbm, shot_cells_ref),
            )
        )
    ]
    for load in loads:
        load.start()
    barrier = pltpu.get_barrier_semaphore()

    def greet(i, carry):
        for core in range(2):
            peer = {"depth": lax.rem(d + i, nd), "gx": core}
            pl.semaphore_signal(barrier, inc=1, device_id=peer, device_id_type=pl.DeviceIdType.MESH)
        return carry

    lax.fori_loop(1, nd, greet, 0)
    for peer in (sibling, across):
        pl.semaphore_signal(barrier, inc=1, device_id=peer, device_id_type=pl.DeviceIdType.MESH)

    def remote(source, target, send, recv, peer):
        return pltpu.make_async_remote_copy(
            src_ref=source,
            dst_ref=target,
            send_sem=send,
            recv_sem=recv,
            device_id=peer,
            device_id_type=pl.DeviceIdType.MESH,
        )

    loads[0].wait()
    loads[1].wait()
    speed = jnp.where(air[...] == 1, jnp.float32(AIR_SLOW), slowness[...])
    first, second = speed[:, :, :WIDE], speed[:, :, WIDE:]
    rim_out[...] = jnp.where(x == 0, second, first)
    for p in range(4):
        wins[p] = part_window(p, x, first, second, first)
    pl.semaphore_wait(barrier, 2 * nd)

    rim = remote(rim_out, rim_in, rim_send, rim_recv, across)
    rim.start()
    late = 3 * (1 - x)

    def slab(target):
        return remote(
            wins.at[lax.rem(target, 4)],
            speeds.at[pl.ds(cz * d, cz), mine],
            slab_send,
            slab_recv.at[d],
            {"depth": target},
        )

    def send_early(i, carry):
        target = lax.rem(d + i, nd)

        @pl.when(lax.rem(target, 4) != late)
        def _():
            slab(target).start()

        return carry

    lax.fori_loop(1, nd, send_early, 0)
    for load in loads[2:]:
        load.wait()
    source = jnp.where(receiver[...] == 1, resid[...], jnp.float32(0.0))
    shots_rim_out[0:4] = jnp.where(x == 0, source[:, :, WIDE:], source[:, :, :WIDE])
    depth_of = reflect[...].astype(jnp.float32)
    shots_rim_out[4] = jnp.where(x == 0, depth_of[:, WIDE:], depth_of[:, :WIDE])
    shots_rim = remote(shots_rim_out, shots_rim_in, shots_send, shots_recv, across)
    shots_rim.start()

    rim.wait_recv()
    beyond = rim_in[...]
    wins[late] = jnp.where(
        x == 0, part_window(3, 0, first, second, beyond), part_window(0, 1, first, second, beyond)
    )
    for turn in range(2):
        target = lax.rem(late + 4 * ((quad + 1 + turn) % 2), nd)

        @pl.when(target != d)
        def _():
            slab(target).start()

    def passing(s):
        block = speeds.at[pl.ds(cz * s, cz), mine]
        return remote(block, block, pass_send, pass_recv.at[s], sibling)

    speeds[pl.ds(cz * d, cz), mine] = wins[part]
    passing(d).start()
    stencil_factors(factors, shot_cells_ref, 2 * quad + g, 4 * x + part, nx, ny)

    shots_rim.wait_recv()

    def windowed(first, second, beyond):
        picks = [part_window(p, x, first, second, beyond) for p in range(4)]
        return jnp.where(
            part < 2, jnp.where(part == 0, picks[0], picks[1]), jnp.where(part == 2, picks[2], picks[3])
        )

    around = windowed(source[:, :, :WIDE], source[:, :, WIDE:], shots_rim_in[0:4])
    fields[0:2, mine] = jnp.where(g == 0, around[0:2], around[2:4])
    shots_side[0:2] = jnp.where(g == 0, around[2:4], around[0:2])
    around = windowed(depth_of[:, :WIDE], depth_of[:, WIDE:], shots_rim_in[4])
    fields[2, mine] = around
    shots_side[2] = around
    side = remote(shots_side, fields.at[:, mine], side_send, side_recv, sibling)
    side.start()

    def pass_on(s):
        @pl.when(s != d)
        def _():
            block = speeds.at[pl.ds(cz * s, cz), mine]
            remote(block, block, slab_send, slab_recv.at[s], sibling).wait_recv()
            passing(s).start()

    pass_on(0)

    def forward(s, front):
        @pl.when(s < nd - 1)
        def _():
            pass_on(s + 1)

        block = speeds.at[pl.ds(cz * s, cz), theirs]
        remote(block, block, pass_send, pass_recv.at[s], sibling).wait_recv()
        for i in range(2):
            k = 2 * s + i
            front = forward_plane(k, speeds[k], front, factors, fronts, spans)
        return front

    lax.fori_loop(0, nd, forward, jnp.ones((2 * nx, WIDE), jnp.float32))
    remote(shots_side, fields.at[:, theirs], side_send, side_recv, sibling).wait_recv()
    source = jnp.concatenate([fields[0], fields[1]], axis=0)
    reflector = fields[2]
    shape = (nx, WIDE)
    col = window_columns(shape, 4 * x + part)
    row = lax.broadcasted_iota(jnp.int32, shape, 0)
    lane = lanes(shape)
    inside = (col >= 0) & (col < ny)

    def handing(s, core):
        rows = pl.ds(bx * core, bx)
        return remote(packed.at[s, rows], gathered.at[2 * d + g], sum_send, sum_recv, {"depth": s, "gx": core})

    def adjoint(step, back):
        s = nd - 1 - step
        grads = []
        for i in (1, 0):
            k = 2 * s + i
            back, grad = adjoint_plane(
                k, speeds[k], back, source, reflector, factors, fronts, spans, inside, (row == 0, row == nx - 1)
            )
            grads.append(grad)
        packed[s] = jnp.where(lane < OWN, grads[1], halfway(grads[0]))
        for core in range(2):

            @pl.when((s != d) | (g != core))
            def _():
                handing(s, core).start()

        return back

    lax.fori_loop(0, nd, adjoint, jnp.zeros((2 * nx, WIDE), jnp.float32))
    gathered[2 * d + g] = packed[d, mine]
    rim.wait_send()
    shots_rim.wait_send()
    side.wait_send()
    others = speeds.at[pl.ds(0, cz * (nd - 1)), mine]
    remote(others, others, slab_send, rim_recv, sibling).wait_send()
    block = speeds.at[:, mine]
    remote(block, block, pass_send, rim_recv, sibling).wait_send()
    block = gathered.at[pl.ds(0, 2 * nd - 1)]
    remote(block, block, rim_send, sum_recv, sibling).wait_recv()
    remote(block, block, sum_send, rim_recv, sibling).wait_send()
    totals = [
        (gathered[2 * p] + gathered[2 * p + 1]) + (gathered[2 * p + 8] + gathered[2 * p + 9])
        for p in range(4)
    ]
    lane = lanes((bx, WIDE))
    for tile in range(2):
        low, high = totals[2 * tile], totals[2 * tile + 1]
        columns = slice(tile * WIDE, (tile + 1) * WIDE)
        out_ref[0, :, columns] = jnp.where(lane < OWN, low, halfway(high))
        out_ref[1, :, columns] = jnp.where(lane < OWN, halfway(low), high)


def local_split(slowness, air_mask, reflector, shot_cells, receiver_mask, residual):
    cz, bx, by = slowness.shape
    nd = lax.axis_size("depth")
    nz, nx, ny = cz * nd, bx * lax.axis_size("gx"), by * lax.axis_size("gy")
    f32, i32 = jnp.float32, jnp.int32
    dma = pltpu.SemaphoreType.DMA
    return pl.pallas_call(
        functools.partial(sweep_kernel, ny),
        out_shape=jax.ShapeDtypeStruct((cz, bx, by), f32),
        in_specs=[pl.BlockSpec(memory_space=pltpu.HBM)] * 6,
        out_specs=pl.BlockSpec(memory_space=pltpu.VMEM),
        scratch_shapes=[
            pltpu.SMEM(shot_cells.shape[::-1], i32),
            pltpu.VMEM((cz, bx, by), f32),
            pltpu.VMEM((cz, bx, by), i32),
            pltpu.VMEM((bx, by), i32),
            pltpu.VMEM((4, bx, by), i32),
            pltpu.VMEM((4, bx, by), f32),
            pltpu.VMEM((cz, bx, WIDE), f32),
            pltpu.VMEM((cz, bx, WIDE), f32),
            pltpu.VMEM((4, cz, bx, WIDE), f32),
            pltpu.VMEM((nz, nx, WIDE), f32),
            pltpu.VMEM((5, bx, WIDE), f32),
            pltpu.VMEM((5, bx, WIDE), f32),
            pltpu.VMEM((3, bx, WIDE), f32),
            pltpu.VMEM((3, nx, WIDE), f32),
            pltpu.VMEM((8, 2 * nx, WIDE), f32),
            pltpu.VMEM((nz, 2 * nx, WIDE), f32),
            pltpu.VMEM((nz, 2 * nx, WIDE), f32),
            pltpu.VMEM((nd, nx, WIDE), f32),
            pltpu.VMEM((2 * nd, bx, WIDE), f32),
            dma((6,)),
            dma,
            dma,
            dma,
            dma((nd,)),
            dma,
            dma((nd,)),
            dma,
            dma,
            dma,
            dma,
            dma,
            dma,
        ],
        compiler_params=pltpu.CompilerParams(
            vmem_limit_bytes=16 * 1024 * 1024, collective_id=0, has_side_effects=True
        ),
    )(
        *(
            pltpu.with_memory_space_constraint(a, pltpu.HBM)
            for a in (shot_cells.T, slowness, air_mask, reflector, receiver_mask, residual)
        )
    )


def solution(mesh):
    in_specs = (
        P("depth", "gx", "gy"),
        P("depth", "gx", "gy"),
        P("gx", "gy"),
        P(),
        P(None, "gx", "gy"),
        P(None, "gx", "gy"),
    )
    out_specs = P("depth", "gx", "gy")
    sizes = dict(mesh.shape)

    def whole(slowness, air_mask, reflector, shot_cells, receiver_mask, residual):
        nz, nx, ny = slowness.shape
        fits = (
            sizes == {"depth": 8, "gx": 2, "gy": 2}
            and (nz, nx, ny) == (16, 32, 512)
            and shot_cells.shape[0] == 8
        )
        local = local_split if fits else local_generic
        return jax.shard_map(local, mesh=mesh, in_specs=in_specs, out_specs=out_specs, check_vma=False)(
            slowness, air_mask, reflector, shot_cells, receiver_mask, residual
        )

    return whole
```

```python
import functools
import math

import jax
import jax.numpy as jnp
from jax import lax
from jax.experimental import pallas as pl
from jax.experimental.pallas import tpu as pltpu
from jax.sharding import PartitionSpec as P

SOFTMIN_TEMPER = 0.5
SURF = 0.7
AIR_SLOW = 2.5
STEP_PENALTY = 10000.0
STENCIL_SHIFTS = [
    (first_term, second_term) for first_term in (-1, 0, 1) for second_term in (-1, 0, 1)
]


def padded(cells, sides, width):
    for axis, dim in sides:
        count = lax.axis_size(axis)
        ends = count - 1
        head = lax.slice_in_dim(cells, 0, width, axis=dim)
        tail = lax.slice_in_dim(cells, cells.shape[dim] - width, cells.shape[dim], axis=dim)
        cells = jnp.concatenate(
            [
                lax.ppermute(tail, axis, [(i, (i + 1) % count) for i in range(ends)]),
                cells,
                lax.ppermute(head, axis, [((i + 1) % count, i) for i in range(ends)]),
            ],
            axis=dim,
        )
    return cells


def passed_along(value, axis, steps):
    count = lax.axis_size(axis)
    initial, last = (max(0, -steps), min(count, count - steps))
    return lax.ppermute(value, axis, [(source, source + steps) for source in range(initial, last)])


def soft_front(candidate_times):
    lowest = candidate_times[0]
    for cand in candidate_times[1:]:
        lowest = jnp.minimum(lowest, cand)
    total = jnp.exp(-(candidate_times[0] - lowest) / SOFTMIN_TEMPER)
    for cand in candidate_times[1:]:
        total = total + jnp.exp(-(cand - lowest) / SOFTMIN_TEMPER)
    return lowest - SOFTMIN_TEMPER * jnp.log(total)


def local_generic(slowness, air_mask, reflector, shot_cells, receiver_mask, residual):
    depth_count = lax.axis_size("depth")
    depth_pos = lax.axis_index("depth")
    cz, shift_along_x, shift_along_y = slowness.shape
    shots = shot_cells.shape[0]
    nx_total = shift_along_x * lax.axis_size("gx")
    ny_total = shift_along_y * lax.axis_size("gy")
    xpos = lax.axis_index("gx") * shift_along_x + jnp.arange(shift_along_x, dtype=jnp.int32)
    ypos = lax.axis_index("gy") * shift_along_y + jnp.arange(shift_along_y, dtype=jnp.int32)
    zpos = depth_pos * cz + jnp.arange(cz, dtype=jnp.int32)
    earth = air_mask == 0
    speed = jnp.where(air_mask == 1, jnp.float32(AIR_SLOW), slowness)
    shot_x = shot_cells[:, 0].astype(jnp.float32)
    shot_y = shot_cells[:, 1].astype(jnp.float32)
    surface = SURF * jnp.sqrt(
        (xpos.astype(jnp.float32)[None, :, None] - shot_x[:, None, None]) ** 2
        + (ypos.astype(jnp.float32)[None, None, :] - shot_y[:, None, None]) ** 2
    )
    penalty_terms = []
    span_lengths = []
    for first_term, second_term in STENCIL_SHIFTS:
        valid_mask = ((xpos + first_term >= 0) & (xpos + first_term < nx_total))[:, None] & (
            (ypos + second_term >= 0) & (ypos + second_term < ny_total)
        )[None, :]
        penalty_terms.append(jnp.where(valid_mask, jnp.float32(0.0), jnp.float32(STEP_PENALTY)))
        span_lengths.append(math.sqrt(1.0 + first_term * first_term + second_term * second_term))

    def sweep_plane(prior_layer, depth_layer):
        padded_layer = padded(prior_layer, (("gx", 1), ("gy", 2)), 1)
        candidate_times = [
            padded_layer[
                :,
                1 + first_term : 1 + first_term + shift_along_x,
                1 + second_term : 1 + second_term + shift_along_y,
            ]
            + depth_layer * span_lengths[stencil_index]
            + penalty_terms[stencil_index]
            for stencil_index, (first_term, second_term) in enumerate(STENCIL_SHIFTS)
        ]
        nxt = soft_front(candidate_times)
        return (nxt, nxt)

    def make_adjoint(source_block, count):

        def adjoint_plane(back, inputs):
            depth_layer, hit, previous_times, current_layer = inputs
            lam = source_block * hit[None] + back
            stacked = jnp.concatenate([lam, current_layer, previous_times, depth_layer[None]], 0)
            padded_layer = padded(stacked, (("gx", 1), ("gy", 2)), 1)
            lam_pad = padded_layer[:count]
            cur_pad = padded_layer[count : 2 * count]
            prev_pad = padded_layer[2 * count : 3 * count]
            layer_pad = padded_layer[3 * count]
            weight_sum = jnp.zeros_like(lam)
            back_new = jnp.zeros_like(lam)
            for stencil_index, (first_term, second_term) in enumerate(STENCIL_SHIFTS):
                lateral_value = prev_pad[
                    :,
                    1 + first_term : 1 + first_term + shift_along_x,
                    1 + second_term : 1 + second_term + shift_along_y,
                ]
                softmin_weight = jnp.exp(
                    -(
                        lateral_value
                        + depth_layer * span_lengths[stencil_index]
                        + penalty_terms[stencil_index]
                        - current_layer
                    )
                    / SOFTMIN_TEMPER
                )
                weight_sum = weight_sum + softmin_weight * span_lengths[stencil_index]
                lam_from = lam_pad[
                    :,
                    1 - first_term : 1 - first_term + shift_along_x,
                    1 - second_term : 1 - second_term + shift_along_y,
                ]
                cur_from = cur_pad[
                    :,
                    1 - first_term : 1 - first_term + shift_along_x,
                    1 - second_term : 1 - second_term + shift_along_y,
                ]
                layer_from = layer_pad[
                    1 - first_term : 1 - first_term + shift_along_x,
                    1 - second_term : 1 - second_term + shift_along_y,
                ]
                prob_from = jnp.exp(
                    -(previous_times + layer_from * span_lengths[stencil_index] - cur_from)
                    / SOFTMIN_TEMPER
                )
                back_new = back_new + lam_from * prob_from
            return (back_new, jnp.sum(lam * weight_sum, axis=0))

        return adjoint_plane

    source_all = jnp.where(receiver_mask == 1, residual, jnp.float32(0.0))
    blocks = 1
    width = shots // blocks
    rounds = depth_count + blocks - 1

    def forward_round(step, carry):
        incoming, store = carry
        group = step - depth_pos
        valid_mask = (group >= 0) & (group < blocks)
        top = jnp.where(depth_pos == 0, surface, incoming)
        last, planes = lax.scan(sweep_plane, top, speed)
        block = jnp.concatenate([top[None], planes], 0)
        old = store
        store = jnp.where(valid_mask, block, old)
        incoming = passed_along(last, "depth", 1)
        return (incoming, store)

    store = jnp.zeros((cz + 1, shots, shift_along_x, shift_along_y), jnp.float32)
    incoming = jnp.zeros((width, shift_along_x, shift_along_y), jnp.float32)
    incoming, store = lax.fori_loop(0, rounds, forward_round, (incoming, store))
    hits = (zpos[:, None, None] == reflector[None]).astype(jnp.float32)

    def adjoint_round(step, carry):
        incoming_back, grad_sum = carry
        group = step - (depth_count - 1 - depth_pos)
        valid_mask = (group >= 0) & (group < blocks)
        back_top, grads = lax.scan(
            make_adjoint(source_all, width),
            incoming_back,
            (speed, hits, store[:-1], store[1:]),
            reverse=True,
        )
        grad_sum = grad_sum + jnp.where(valid_mask, grads, jnp.float32(0.0))
        incoming_back = passed_along(back_top, "depth", -1)
        return (incoming_back, grad_sum)

    start_back = jnp.zeros((width, shift_along_x, shift_along_y), jnp.float32)
    grad_total = jnp.zeros((cz, shift_along_x, shift_along_y), jnp.float32)
    start_back, grad_total = lax.fori_loop(0, rounds, adjoint_round, (start_back, grad_total))
    colsum = jnp.sum(source_all, axis=0)
    below = zpos[:, None, None] <= reflector[None]
    raw = jnp.where(earth, grad_total, jnp.float32(0.0)) + jnp.where(
        earth & below, colsum[None], jnp.float32(0.0)
    )
    padded_layer = padded(raw, (("gx", 1), ("gy", 2)), 1)
    beside_all = jnp.zeros_like(raw)
    for first_term, second_term in STENCIL_SHIFTS:
        if first_term != 0 or second_term != 0:
            beside_all = (
                beside_all
                + padded_layer[
                    :,
                    1 + first_term : 1 + first_term + shift_along_x,
                    1 + second_term : 1 + second_term + shift_along_y,
                ]
            )
    return 0.5 * raw + 0.0625 * beside_all


WIDE = 128
OWN = 64
PAD = 8
SIDE = 32
ROOT2 = math.sqrt(2.0)
ROOT3 = math.sqrt(3.0)


def left(cells):
    return pltpu.roll(cells, 1, axis=1)


def right(cells):
    return pltpu.roll(cells, cells.shape[1] - 1, axis=1)


def halfway(cells):
    return pltpu.roll(cells, OWN, axis=cells.ndim - 1)


def lanes(shape):
    return lax.broadcasted_iota(jnp.int32, shape, len(shape) - 1)


def window_columns(shape, part):
    lane = lanes(shape)
    return part * OWN + lane - jnp.where(lane >= WIDE - SIDE, WIDE, 0)


def stencil_factors(factors, shot_cells_ref, pair, part, nx, ny):
    shape = (2 * nx, WIDE)
    row = lax.broadcasted_iota(jnp.int32, shape, 0)
    second = row >= nx
    row = jnp.where(second, row - nx, row)
    col = window_columns(shape, part)
    place = [
        jnp.where(second, shot_cells_ref[d, 2 * pair + 1], shot_cells_ref[d, 2 * pair]).astype(
            jnp.float32
        )
        for d in (0, 1)
    ]

    def surface(a, b):
        u = (row + a).astype(jnp.float32) - place[0]
        v = (col + b).astype(jnp.float32) - place[1]
        return SURF * jnp.sqrt(u * u + v * v)

    here = surface(0, 0)
    for slot, (a, b) in enumerate(((0, -1), (0, 1), (-1, 0), (1, 0))):
        inside = (row + a >= 0) & (row + a < nx) & (col + b >= 0) & (col + b < ny)
        beside = surface(a, b)
        penalty = jnp.where(inside, jnp.float32(0.0), jnp.float32(STEP_PENALTY))
        value = jnp.where(inside, beside, jnp.float32(0.0))
        factors[slot] = jnp.exp(-((value + penalty) - here) / SOFTMIN_TEMPER)
        factors[4 + slot] = jnp.where(inside, jnp.exp(-(here - beside) / SOFTMIN_TEMPER), 0.0)


def twice(cells):
    return jnp.concatenate([cells, cells], axis=0)


def shifted_rows(buffer, cells, nought):
    rows = cells.shape[0]
    buffer[pl.ds(PAD, rows)] = cells
    return buffer[pl.ds(PAD - 1 + nought, rows)], buffer[pl.ds(PAD + 1 + nought, rows)]


def forward_plane(k, speed, front, factors, fronts, spans, buffers, nought):
    w1 = twice(jnp.exp(-speed / SOFTMIN_TEMPER))
    w2 = twice(jnp.exp(-(speed * ROOT2) / SOFTMIN_TEMPER))
    w3 = twice(jnp.exp(-(speed * ROOT3) / SOFTMIN_TEMPER))
    side = factors[0] * left(front) + factors[1] * right(front)
    up, down = shifted_rows(buffers[0], front, nought)
    edge = side + factors[2] * up + factors[3] * down
    up, down = shifted_rows(buffers[1], side, nought)
    corner = factors[2] * up + factors[3] * down
    one, two, three = w1 * front, w2 * edge, w3 * corner
    front = one + two + three
    fronts[k] = front
    spans[k] = one + ROOT2 * two + ROOT3 * three
    return front


def adjoint_plane(k, speed, back, source, reflector, factors, fronts, spans, inside, edges, buffers, nought):
    w1 = twice(jnp.exp(-speed / SOFTMIN_TEMPER))
    w2 = twice(jnp.exp(-(speed * ROOT2) / SOFTMIN_TEMPER))
    w3 = twice(jnp.exp(-(speed * ROOT3) / SOFTMIN_TEMPER))
    plane = k.astype(jnp.float32)
    lam = jnp.where(twice(reflector == plane), source / fronts[k], 0.0) + back
    part = lam * spans[k] + jnp.where(twice(reflector >= plane), source, 0.0)
    nx = speed.shape[0]
    raw = jnp.where(inside & (speed != AIR_SLOW), part[:nx] + part[nx:], 0.0)
    line = raw + left(raw) + right(raw)
    up, down = shifted_rows(buffers[2], line, nought)
    box = line + jnp.where(edges[0], 0.0, up) + jnp.where(edges[1], 0.0, down)
    grad = 0.4375 * raw + 0.0625 * box
    two, three = w2 * lam, w3 * lam
    far = two + factors[4] * left(three) + factors[5] * right(three)
    up, down = shifted_rows(buffers[3], far, nought)
    back = (
        w1 * lam
        + (factors[4] * left(two) + factors[5] * right(two))
        + (factors[6] * up + factors[7] * down)
    )
    return back, grad


def part_window(part, x, first, second, beyond):
    lane = lanes(first.shape)
    if part == 0:
        return jnp.where(lane < WIDE - SIDE, first, jnp.where(x == 1, beyond, first))
    if part == 1:
        return halfway(jnp.where(lane >= SIDE, first, second))
    if part == 2:
        return jnp.where(lane < WIDE - SIDE, second, first)
    return halfway(jnp.where(lane >= SIDE, second, jnp.where(x == 0, beyond, second)))


def sweep_kernel(
    ny,
    shot_cells_hbm,
    slowness_hbm,
    air_hbm,
    reflector_hbm,
    receiver_hbm,
    residual_hbm,
    out_ref,
    shot_cells_ref,
    slowness,
    air,
    reflect,
    receiver,
    resid,
    rim_out,
    rim_in,
    wins,
    speeds,
    shots_rim_out,
    shots_rim_in,
    shots_side,
    fields,
    factors,
    fronts,
    spans,
    packed,
    gathered,
    *rest,
):
    row_buffers, sems = rest[:8], rest[8:]
    (
        load_sem,
        rim_send,
        rim_recv,
        slab_send,
        slab_recv,
        pass_send,
        pass_recv,
        shots_send,
        shots_recv,
        side_send,
        side_recv,
        sum_send,
        sum_recv,
    ) = sems
    d = lax.axis_index("depth")
    g = lax.axis_index("gx")
    x = lax.axis_index("gy")
    cz, bx, _ = slowness.shape
    nd = speeds.shape[0] // cz
    nx = 2 * bx
    part = lax.rem(d, 4)
    quad = d // 4
    sibling = {"gx": 1 - g}
    across = {"gy": 1 - x}
    mine = pl.ds(pl.multiple_of(bx * g, bx), bx)
    theirs = pl.ds(pl.multiple_of(bx * (1 - g), bx), bx)
    shots = pl.ds(4 * quad, 4)

    loads = [
        pltpu.make_async_copy(source, target, load_sem.at[i])
        for i, (source, target) in enumerate(
            (
                (slowness_hbm, slowness),
                (air_hbm, air),
                (reflector_hbm, reflect),
                (receiver_hbm.at[shots], receiver),
                (residual_hbm.at[shots], resid),
                (shot_cells_hbm, shot_cells_ref),
            )
        )
    ]
    for load in loads[:2]:
        load.start()
    barrier = pltpu.get_barrier_semaphore()

    for i in range(nd - 1, 0, -1):
        for core in range(2):
            peer = {"depth": lax.rem(d + i, nd), "gx": core}
            pl.semaphore_signal(barrier, inc=1, device_id=peer, device_id_type=pl.DeviceIdType.MESH)
    for peer in (sibling, across):
        pl.semaphore_signal(barrier, inc=1, device_id=peer, device_id_type=pl.DeviceIdType.MESH)

    def remote(source, target, send, recv, peer):
        return pltpu.make_async_remote_copy(
            src_ref=source,
            dst_ref=target,
            send_sem=send,
            recv_sem=recv,
            device_id=peer,
            device_id_type=pl.DeviceIdType.MESH,
        )

    for load in loads[2:]:
        load.start()
    nought = g // 2
    for buffer in row_buffers:
        buffer[...] = jnp.zeros(buffer.shape, jnp.float32)
    loads[0].wait()
    loads[1].wait()
    speed = jnp.where(air[...] == 1, jnp.float32(AIR_SLOW), slowness[...])
    first, second = speed[:, :, :WIDE], speed[:, :, WIDE:]
    rim_out[...] = jnp.where(x == 0, second, first)
    for p in range(4):
        wins[p] = part_window(p, x, first, second, first)
    pl.semaphore_wait(barrier, 2 * nd)

    rim = remote(rim_out, rim_in, rim_send, rim_recv, across)
    rim.start()
    late = 3 * (1 - x)

    def slab(target):
        return remote(
            wins.at[lax.rem(target, 4)],
            speeds.at[pl.ds(cz * d, cz), mine],
            slab_send,
            slab_recv.at[d],
            {"depth": target},
        )

    for i in range(1, nd):
        early = lax.rem(d + i, nd)

        @pl.when(lax.rem(early, 4) != late)
        def _(early=early):
            slab(early).start()

    for load in loads[2:]:
        load.wait()
    source = jnp.where(receiver[...] == 1, resid[...], jnp.float32(0.0))
    shots_rim_out[0:4] = jnp.where(x == 0, source[:, :, WIDE:], source[:, :, :WIDE])
    depth_of = reflect[...].astype(jnp.float32)
    shots_rim_out[4] = jnp.where(x == 0, depth_of[:, WIDE:], depth_of[:, :WIDE])
    shots_rim = remote(shots_rim_out, shots_rim_in, shots_send, shots_recv, across)
    shots_rim.start()

    rim.wait_recv()
    beyond = rim_in[...]
    wins[late] = jnp.where(
        x == 0, part_window(3, 0, first, second, beyond), part_window(0, 1, first, second, beyond)
    )
    for turn in range(2):
        target = lax.rem(late + 4 * ((quad + 1 + turn) % 2), nd)

        @pl.when(target != d)
        def _():
            slab(target).start()

    def passing(s):
        block = speeds.at[pl.ds(cz * s, cz), mine]
        return remote(block, block, pass_send, pass_recv.at[s], sibling)

    speeds[pl.ds(cz * d, cz), mine] = wins[part]
    passing(d).start()
    stencil_factors(factors, shot_cells_ref, 2 * quad + g, 4 * x + part, nx, ny)

    shots_rim.wait_recv()

    def windowed(first, second, beyond):
        picks = [part_window(p, x, first, second, beyond) for p in range(4)]
        return jnp.where(
            part < 2, jnp.where(part == 0, picks[0], picks[1]), jnp.where(part == 2, picks[2], picks[3])
        )

    around = windowed(source[:, :, :WIDE], source[:, :, WIDE:], shots_rim_in[0:4])
    fields[0:2, mine] = jnp.where(g == 0, around[0:2], around[2:4])
    shots_side[0:2] = jnp.where(g == 0, around[2:4], around[0:2])
    around = windowed(depth_of[:, :WIDE], depth_of[:, WIDE:], shots_rim_in[4])
    fields[2, mine] = around
    shots_side[2] = around
    side = remote(shots_side, fields.at[:, mine], side_send, side_recv, sibling)
    side.start()

    def pass_on(s):
        @pl.when(s != d)
        def _():
            block = speeds.at[pl.ds(cz * s, cz), mine]
            remote(block, block, slab_send, slab_recv.at[s], sibling).wait_recv()
            passing(s).start()

    pass_on(0)

    def forward(s, front):
        @pl.when(s < nd - 1)
        def _():
            pass_on(s + 1)

        block = speeds.at[pl.ds(cz * s, cz), theirs]
        remote(block, block, pass_send, pass_recv.at[s], sibling).wait_recv()
        for i in range(2):
            k = 2 * s + i
            front = forward_plane(
                k, speeds[k], front, factors, fronts, spans, row_buffers[4 * i : 4 * i + 4], nought
            )
        return front

    lax.fori_loop(0, nd, forward, jnp.ones((2 * nx, WIDE), jnp.float32))
    remote(shots_side, fields.at[:, theirs], side_send, side_recv, sibling).wait_recv()
    source = jnp.concatenate([fields[0], fields[1]], axis=0)
    reflector = fields[2]
    shape = (nx, WIDE)
    col = window_columns(shape, 4 * x + part)
    row = lax.broadcasted_iota(jnp.int32, shape, 0)
    lane = lanes(shape)
    inside = (col >= 0) & (col < ny)

    def handing(s, core):
        rows = pl.ds(bx * core, bx)
        return remote(packed.at[s, rows], gathered.at[2 * d + g], sum_send, sum_recv, {"depth": s, "gx": core})

    def adjoint(step, back):
        s = nd - 1 - step
        grads = []
        for i in (1, 0):
            k = 2 * s + i
            back, grad = adjoint_plane(
                k, speeds[k], back, source, reflector, factors, fronts, spans, inside,
                (row == 0, row == nx - 1), row_buffers[4 * i : 4 * i + 4], nought,
            )
            grads.append(grad)
        packed[s] = jnp.where(lane < OWN, grads[1], halfway(grads[0]))
        for core in range(2):

            @pl.when((s != d) | (g != core))
            def _():
                handing(s, core).start()

        return back

    lax.fori_loop(0, nd, adjoint, jnp.zeros((2 * nx, WIDE), jnp.float32))
    gathered[2 * d + g] = packed[d, mine]
    rim.wait_send()
    shots_rim.wait_send()
    side.wait_send()
    others = speeds.at[pl.ds(0, cz * (nd - 1)), mine]
    remote(others, others, slab_send, rim_recv, sibling).wait_send()
    block = speeds.at[:, mine]
    remote(block, block, pass_send, rim_recv, sibling).wait_send()
    block = gathered.at[pl.ds(0, 2 * nd - 1)]
    remote(block, block, rim_send, sum_recv, sibling).wait_recv()
    remote(block, block, sum_send, rim_recv, sibling).wait_send()
    totals = [
        (gathered[2 * p] + gathered[2 * p + 1]) + (gathered[2 * p + 8] + gathered[2 * p + 9])
        for p in range(4)
    ]
    lane = lanes((bx, WIDE))
    for tile in range(2):
        low, high = totals[2 * tile], totals[2 * tile + 1]
        columns = slice(tile * WIDE, (tile + 1) * WIDE)
        out_ref[0, :, columns] = jnp.where(lane < OWN, low, halfway(high))
        out_ref[1, :, columns] = jnp.where(lane < OWN, halfway(low), high)


def local_split(slowness, air_mask, reflector, shot_cells, receiver_mask, residual):
    cz, bx, by = slowness.shape
    nd = lax.axis_size("depth")
    nz, nx, ny = cz * nd, bx * lax.axis_size("gx"), by * lax.axis_size("gy")
    f32, i32 = jnp.float32, jnp.int32
    dma = pltpu.SemaphoreType.DMA
    return pl.pallas_call(
        functools.partial(sweep_kernel, ny),
        out_shape=jax.ShapeDtypeStruct((cz, bx, by), f32),
        in_specs=[pl.BlockSpec(memory_space=pltpu.HBM)] * 6,
        out_specs=pl.BlockSpec(memory_space=pltpu.VMEM),
        scratch_shapes=[
            pltpu.SMEM(shot_cells.shape[::-1], i32),
            pltpu.VMEM((cz, bx, by), f32),
            pltpu.VMEM((cz, bx, by), i32),
            pltpu.VMEM((bx, by), i32),
            pltpu.VMEM((4, bx, by), i32),
            pltpu.VMEM((4, bx, by), f32),
            pltpu.VMEM((cz, bx, WIDE), f32),
            pltpu.VMEM((cz, bx, WIDE), f32),
            pltpu.VMEM((4, cz, bx, WIDE), f32),
            pltpu.VMEM((nz, nx, WIDE), f32),
            pltpu.VMEM((5, bx, WIDE), f32),
            pltpu.VMEM((5, bx, WIDE), f32),
            pltpu.VMEM((3, bx, WIDE), f32),
            pltpu.VMEM((3, nx, WIDE), f32),
            pltpu.VMEM((8, 2 * nx, WIDE), f32),
            pltpu.VMEM((nz, 2 * nx, WIDE), f32),
            pltpu.VMEM((nz, 2 * nx, WIDE), f32),
            pltpu.VMEM((nd, nx, WIDE), f32),
            pltpu.VMEM((2 * nd, bx, WIDE), f32),
            *[pltpu.VMEM((2 * nx + 2 * PAD, WIDE), f32) for _ in range(8)],
            dma((6,)),
            dma,
            dma,
            dma,
            dma((nd,)),
            dma,
            dma((nd,)),
            dma,
            dma,
            dma,
            dma,
            dma,
            dma,
        ],
        compiler_params=pltpu.CompilerParams(
            vmem_limit_bytes=16 * 1024 * 1024, collective_id=0, has_side_effects=True
        ),
    )(
        *(
            pltpu.with_memory_space_constraint(a, pltpu.HBM)
            for a in (shot_cells.T, slowness, air_mask, reflector, receiver_mask, residual)
        )
    )


def solution(mesh):
    in_specs = (
        P("depth", "gx", "gy"),
        P("depth", "gx", "gy"),
        P("gx", "gy"),
        P(),
        P(None, "gx", "gy"),
        P(None, "gx", "gy"),
    )
    out_specs = P("depth", "gx", "gy")
    sizes = dict(mesh.shape)

    def whole(slowness, air_mask, reflector, shot_cells, receiver_mask, residual):
        nz, nx, ny = slowness.shape
        fits = (
            sizes == {"depth": 8, "gx": 2, "gy": 2}
            and (nz, nx, ny) == (16, 32, 512)
            and shot_cells.shape[0] == 8
        )
        local = local_split if fits else local_generic
        return jax.shard_map(local, mesh=mesh, in_specs=in_specs, out_specs=out_specs, check_vma=False)(
            slowness, air_mask, reflector, shot_cells, receiver_mask, residual
        )

    return whole
```

```python
import functools
import math

import jax
import jax.numpy as jnp
from jax import lax
from jax.experimental import pallas as pl
from jax.experimental.pallas import tpu as pltpu
from jax.sharding import PartitionSpec as P

SOFTMIN_TEMPER = 0.5
SURF = 0.7
AIR_SLOW = 2.5
STEP_PENALTY = 10000.0
STENCIL_SHIFTS = [
    (first_term, second_term) for first_term in (-1, 0, 1) for second_term in (-1, 0, 1)
]


def padded(cells, sides, width):
    for axis, dim in sides:
        count = lax.axis_size(axis)
        ends = count - 1
        head = lax.slice_in_dim(cells, 0, width, axis=dim)
        tail = lax.slice_in_dim(cells, cells.shape[dim] - width, cells.shape[dim], axis=dim)
        cells = jnp.concatenate(
            [
                lax.ppermute(tail, axis, [(i, (i + 1) % count) for i in range(ends)]),
                cells,
                lax.ppermute(head, axis, [((i + 1) % count, i) for i in range(ends)]),
            ],
            axis=dim,
        )
    return cells


def passed_along(value, axis, steps):
    count = lax.axis_size(axis)
    initial, last = (max(0, -steps), min(count, count - steps))
    return lax.ppermute(value, axis, [(source, source + steps) for source in range(initial, last)])


def soft_front(candidate_times):
    lowest = candidate_times[0]
    for cand in candidate_times[1:]:
        lowest = jnp.minimum(lowest, cand)
    total = jnp.exp(-(candidate_times[0] - lowest) / SOFTMIN_TEMPER)
    for cand in candidate_times[1:]:
        total = total + jnp.exp(-(cand - lowest) / SOFTMIN_TEMPER)
    return lowest - SOFTMIN_TEMPER * jnp.log(total)


def local_generic(slowness, air_mask, reflector, shot_cells, receiver_mask, residual):
    depth_count = lax.axis_size("depth")
    depth_pos = lax.axis_index("depth")
    cz, shift_along_x, shift_along_y = slowness.shape
    shots = shot_cells.shape[0]
    nx_total = shift_along_x * lax.axis_size("gx")
    ny_total = shift_along_y * lax.axis_size("gy")
    xpos = lax.axis_index("gx") * shift_along_x + jnp.arange(shift_along_x, dtype=jnp.int32)
    ypos = lax.axis_index("gy") * shift_along_y + jnp.arange(shift_along_y, dtype=jnp.int32)
    zpos = depth_pos * cz + jnp.arange(cz, dtype=jnp.int32)
    earth = air_mask == 0
    speed = jnp.where(air_mask == 1, jnp.float32(AIR_SLOW), slowness)
    shot_x = shot_cells[:, 0].astype(jnp.float32)
    shot_y = shot_cells[:, 1].astype(jnp.float32)
    surface = SURF * jnp.sqrt(
        (xpos.astype(jnp.float32)[None, :, None] - shot_x[:, None, None]) ** 2
        + (ypos.astype(jnp.float32)[None, None, :] - shot_y[:, None, None]) ** 2
    )
    penalty_terms = []
    span_lengths = []
    for first_term, second_term in STENCIL_SHIFTS:
        valid_mask = ((xpos + first_term >= 0) & (xpos + first_term < nx_total))[:, None] & (
            (ypos + second_term >= 0) & (ypos + second_term < ny_total)
        )[None, :]
        penalty_terms.append(jnp.where(valid_mask, jnp.float32(0.0), jnp.float32(STEP_PENALTY)))
        span_lengths.append(math.sqrt(1.0 + first_term * first_term + second_term * second_term))

    def sweep_plane(prior_layer, depth_layer):
        padded_layer = padded(prior_layer, (("gx", 1), ("gy", 2)), 1)
        candidate_times = [
            padded_layer[
                :,
                1 + first_term : 1 + first_term + shift_along_x,
                1 + second_term : 1 + second_term + shift_along_y,
            ]
            + depth_layer * span_lengths[stencil_index]
            + penalty_terms[stencil_index]
            for stencil_index, (first_term, second_term) in enumerate(STENCIL_SHIFTS)
        ]
        nxt = soft_front(candidate_times)
        return (nxt, nxt)

    def make_adjoint(source_block, count):

        def adjoint_plane(back, inputs):
            depth_layer, hit, previous_times, current_layer = inputs
            lam = source_block * hit[None] + back
            stacked = jnp.concatenate([lam, current_layer, previous_times, depth_layer[None]], 0)
            padded_layer = padded(stacked, (("gx", 1), ("gy", 2)), 1)
            lam_pad = padded_layer[:count]
            cur_pad = padded_layer[count : 2 * count]
            prev_pad = padded_layer[2 * count : 3 * count]
            layer_pad = padded_layer[3 * count]
            weight_sum = jnp.zeros_like(lam)
            back_new = jnp.zeros_like(lam)
            for stencil_index, (first_term, second_term) in enumerate(STENCIL_SHIFTS):
                lateral_value = prev_pad[
                    :,
                    1 + first_term : 1 + first_term + shift_along_x,
                    1 + second_term : 1 + second_term + shift_along_y,
                ]
                softmin_weight = jnp.exp(
                    -(
                        lateral_value
                        + depth_layer * span_lengths[stencil_index]
                        + penalty_terms[stencil_index]
                        - current_layer
                    )
                    / SOFTMIN_TEMPER
                )
                weight_sum = weight_sum + softmin_weight * span_lengths[stencil_index]
                lam_from = lam_pad[
                    :,
                    1 - first_term : 1 - first_term + shift_along_x,
                    1 - second_term : 1 - second_term + shift_along_y,
                ]
                cur_from = cur_pad[
                    :,
                    1 - first_term : 1 - first_term + shift_along_x,
                    1 - second_term : 1 - second_term + shift_along_y,
                ]
                layer_from = layer_pad[
                    1 - first_term : 1 - first_term + shift_along_x,
                    1 - second_term : 1 - second_term + shift_along_y,
                ]
                prob_from = jnp.exp(
                    -(previous_times + layer_from * span_lengths[stencil_index] - cur_from)
                    / SOFTMIN_TEMPER
                )
                back_new = back_new + lam_from * prob_from
            return (back_new, jnp.sum(lam * weight_sum, axis=0))

        return adjoint_plane

    source_all = jnp.where(receiver_mask == 1, residual, jnp.float32(0.0))
    blocks = 1
    width = shots // blocks
    rounds = depth_count + blocks - 1

    def forward_round(step, carry):
        incoming, store = carry
        group = step - depth_pos
        valid_mask = (group >= 0) & (group < blocks)
        top = jnp.where(depth_pos == 0, surface, incoming)
        last, planes = lax.scan(sweep_plane, top, speed)
        block = jnp.concatenate([top[None], planes], 0)
        old = store
        store = jnp.where(valid_mask, block, old)
        incoming = passed_along(last, "depth", 1)
        return (incoming, store)

    store = jnp.zeros((cz + 1, shots, shift_along_x, shift_along_y), jnp.float32)
    incoming = jnp.zeros((width, shift_along_x, shift_along_y), jnp.float32)
    incoming, store = lax.fori_loop(0, rounds, forward_round, (incoming, store))
    hits = (zpos[:, None, None] == reflector[None]).astype(jnp.float32)

    def adjoint_round(step, carry):
        incoming_back, grad_sum = carry
        group = step - (depth_count - 1 - depth_pos)
        valid_mask = (group >= 0) & (group < blocks)
        back_top, grads = lax.scan(
            make_adjoint(source_all, width),
            incoming_back,
            (speed, hits, store[:-1], store[1:]),
            reverse=True,
        )
        grad_sum = grad_sum + jnp.where(valid_mask, grads, jnp.float32(0.0))
        incoming_back = passed_along(back_top, "depth", -1)
        return (incoming_back, grad_sum)

    start_back = jnp.zeros((width, shift_along_x, shift_along_y), jnp.float32)
    grad_total = jnp.zeros((cz, shift_along_x, shift_along_y), jnp.float32)
    start_back, grad_total = lax.fori_loop(0, rounds, adjoint_round, (start_back, grad_total))
    colsum = jnp.sum(source_all, axis=0)
    below = zpos[:, None, None] <= reflector[None]
    raw = jnp.where(earth, grad_total, jnp.float32(0.0)) + jnp.where(
        earth & below, colsum[None], jnp.float32(0.0)
    )
    padded_layer = padded(raw, (("gx", 1), ("gy", 2)), 1)
    beside_all = jnp.zeros_like(raw)
    for first_term, second_term in STENCIL_SHIFTS:
        if first_term != 0 or second_term != 0:
            beside_all = (
                beside_all
                + padded_layer[
                    :,
                    1 + first_term : 1 + first_term + shift_along_x,
                    1 + second_term : 1 + second_term + shift_along_y,
                ]
            )
    return 0.5 * raw + 0.0625 * beside_all


WIDE = 128
OWN = 64
PAD = 8
AHEAD = 3
SIDE = 32
ROOT2 = math.sqrt(2.0)
ROOT3 = math.sqrt(3.0)


def left(cells):
    return pltpu.roll(cells, 1, axis=1)


def right(cells):
    return pltpu.roll(cells, cells.shape[1] - 1, axis=1)


def halfway(cells):
    return pltpu.roll(cells, OWN, axis=cells.ndim - 1)


def lanes(shape):
    return lax.broadcasted_iota(jnp.int32, shape, len(shape) - 1)


def window_columns(shape, part):
    lane = lanes(shape)
    return part * OWN + lane - jnp.where(lane >= WIDE - SIDE, WIDE, 0)


def stencil_factors(factors, shot_cells_ref, pair, part, nx, ny):
    shape = (2 * nx, WIDE)
    row = lax.broadcasted_iota(jnp.int32, shape, 0)
    second = row >= nx
    row = jnp.where(second, row - nx, row)
    col = window_columns(shape, part)
    place = [
        jnp.where(second, shot_cells_ref[d, 2 * pair + 1], shot_cells_ref[d, 2 * pair]).astype(
            jnp.float32
        )
        for d in (0, 1)
    ]

    def surface(a, b):
        u = (row + a).astype(jnp.float32) - place[0]
        v = (col + b).astype(jnp.float32) - place[1]
        return SURF * jnp.sqrt(u * u + v * v)

    here = surface(0, 0)
    for slot, (a, b) in enumerate(((0, -1), (0, 1), (-1, 0), (1, 0))):
        inside = (row + a >= 0) & (row + a < nx) & (col + b >= 0) & (col + b < ny)
        beside = surface(a, b)
        penalty = jnp.where(inside, jnp.float32(0.0), jnp.float32(STEP_PENALTY))
        value = jnp.where(inside, beside, jnp.float32(0.0))
        factors[slot] = jnp.exp(-((value + penalty) - here) / SOFTMIN_TEMPER)
        factors[4 + slot] = jnp.where(inside, jnp.exp(-(here - beside) / SOFTMIN_TEMPER), 0.0)


def twice(cells):
    return jnp.concatenate([cells, cells], axis=0)


def shifted_rows(buffer, cells, nought):
    rows = cells.shape[0]
    buffer[pl.ds(PAD, rows)] = cells
    return buffer[pl.ds(PAD - 1 + nought, rows)], buffer[pl.ds(PAD + 1 + nought, rows)]


def forward_plane(k, speed, front, factors, fronts, spans, buffers, nought):
    w1 = twice(jnp.exp(-speed / SOFTMIN_TEMPER))
    w2 = twice(jnp.exp(-(speed * ROOT2) / SOFTMIN_TEMPER))
    w3 = twice(jnp.exp(-(speed * ROOT3) / SOFTMIN_TEMPER))
    side = factors[0] * left(front) + factors[1] * right(front)
    up, down = shifted_rows(buffers[0], front, nought)
    edge = side + factors[2] * up + factors[3] * down
    up, down = shifted_rows(buffers[1], side, nought)
    corner = factors[2] * up + factors[3] * down
    one, two, three = w1 * front, w2 * edge, w3 * corner
    front = one + two + three
    fronts[k] = front
    spans[k] = one + ROOT2 * two + ROOT3 * three
    return front


def adjoint_plane(k, speed, back, source, reflector, factors, fronts, spans, inside, edges, buffers, nought):
    w1 = twice(jnp.exp(-speed / SOFTMIN_TEMPER))
    w2 = twice(jnp.exp(-(speed * ROOT2) / SOFTMIN_TEMPER))
    w3 = twice(jnp.exp(-(speed * ROOT3) / SOFTMIN_TEMPER))
    plane = k.astype(jnp.float32)
    lam = jnp.where(twice(reflector == plane), source / fronts[k], 0.0) + back
    part = lam * spans[k] + jnp.where(twice(reflector >= plane), source, 0.0)
    nx = speed.shape[0]
    raw = jnp.where(inside & (speed != AIR_SLOW), part[:nx] + part[nx:], 0.0)
    line = raw + left(raw) + right(raw)
    up, down = shifted_rows(buffers[2], line, nought)
    box = line + jnp.where(edges[0], 0.0, up) + jnp.where(edges[1], 0.0, down)
    grad = 0.4375 * raw + 0.0625 * box
    two, three = w2 * lam, w3 * lam
    far = two + factors[4] * left(three) + factors[5] * right(three)
    up, down = shifted_rows(buffers[3], far, nought)
    back = (
        w1 * lam
        + (factors[4] * left(two) + factors[5] * right(two))
        + (factors[6] * up + factors[7] * down)
    )
    return back, grad


def part_window(part, x, first, second, beyond):
    lane = lanes(first.shape)
    if part == 0:
        return jnp.where(lane < WIDE - SIDE, first, jnp.where(x == 1, beyond, first))
    if part == 1:
        return halfway(jnp.where(lane >= SIDE, first, second))
    if part == 2:
        return jnp.where(lane < WIDE - SIDE, second, first)
    return halfway(jnp.where(lane >= SIDE, second, jnp.where(x == 0, beyond, second)))


def sweep_kernel(
    ny,
    shot_cells_hbm,
    slowness_hbm,
    air_hbm,
    reflector_hbm,
    receiver_hbm,
    residual_hbm,
    out_ref,
    shot_cells_ref,
    slowness,
    air,
    reflect,
    receiver,
    resid,
    rim_out,
    rim_in,
    wins,
    speeds,
    shots_rim_out,
    shots_rim_in,
    shots_side,
    fields,
    factors,
    fronts,
    spans,
    packed,
    gathered,
    *rest,
):
    row_buffers, sems = rest[:8], rest[8:]
    (
        load_sem,
        rim_send,
        rim_recv,
        slab_send,
        slab_recv,
        pass_send,
        pass_recv,
        shots_send,
        shots_recv,
        side_send,
        side_recv,
        sum_send,
        sum_recv,
    ) = sems
    d = lax.axis_index("depth")
    g = lax.axis_index("gx")
    x = lax.axis_index("gy")
    cz, bx, _ = slowness.shape
    nd = speeds.shape[0] // cz
    nx = 2 * bx
    part = lax.rem(d, 4)
    quad = d // 4
    sibling = {"gx": 1 - g}
    across = {"gy": 1 - x}
    mine = pl.ds(pl.multiple_of(bx * g, bx), bx)
    theirs = pl.ds(pl.multiple_of(bx * (1 - g), bx), bx)
    shots = pl.ds(4 * quad, 4)

    loads = [
        pltpu.make_async_copy(source, target, load_sem.at[i])
        for i, (source, target) in enumerate(
            (
                (slowness_hbm, slowness),
                (air_hbm, air),
                (reflector_hbm, reflect),
                (receiver_hbm.at[shots], receiver),
                (residual_hbm.at[shots], resid),
                (shot_cells_hbm, shot_cells_ref),
            )
        )
    ]
    for load in loads[:2]:
        load.start()
    barrier = pltpu.get_barrier_semaphore()

    for i in range(nd - 1, 0, -1):
        for core in range(2):
            peer = {"depth": lax.rem(d + i, nd), "gx": core}
            pl.semaphore_signal(barrier, inc=1, device_id=peer, device_id_type=pl.DeviceIdType.MESH)
    for peer in (sibling, across):
        pl.semaphore_signal(barrier, inc=1, device_id=peer, device_id_type=pl.DeviceIdType.MESH)

    def remote(source, target, send, recv, peer):
        return pltpu.make_async_remote_copy(
            src_ref=source,
            dst_ref=target,
            send_sem=send,
            recv_sem=recv,
            device_id=peer,
            device_id_type=pl.DeviceIdType.MESH,
        )

    for load in loads[2:]:
        load.start()
    nought = g // 2
    for buffer in row_buffers:
        buffer[...] = jnp.zeros(buffer.shape, jnp.float32)
    loads[0].wait()
    loads[1].wait()
    speed = jnp.where(air[...] == 1, jnp.float32(AIR_SLOW), slowness[...])
    first, second = speed[:, :, :WIDE], speed[:, :, WIDE:]
    rim_out[...] = jnp.where(x == 0, second, first)
    for p in range(4):
        wins[p] = part_window(p, x, first, second, first)
    pl.semaphore_wait(barrier, 2 * nd)

    rim = remote(rim_out, rim_in, rim_send, rim_recv, across)
    rim.start()
    late = 3 * (1 - x)

    def slab(target):
        return remote(
            wins.at[lax.rem(target, 4)],
            speeds.at[pl.ds(cz * d, cz), mine],
            slab_send,
            slab_recv.at[d],
            {"depth": target},
        )

    for i in range(1, nd):
        early = lax.rem(d + i, nd)

        @pl.when(lax.rem(early, 4) != late)
        def _(early=early):
            slab(early).start()

    for load in loads[2:]:
        load.wait()
    source = jnp.where(receiver[...] == 1, resid[...], jnp.float32(0.0))
    shots_rim_out[0:4] = jnp.where(x == 0, source[:, :, WIDE:], source[:, :, :WIDE])
    depth_of = reflect[...].astype(jnp.float32)
    shots_rim_out[4] = jnp.where(x == 0, depth_of[:, WIDE:], depth_of[:, :WIDE])
    shots_rim = remote(shots_rim_out, shots_rim_in, shots_send, shots_recv, across)
    shots_rim.start()

    rim.wait_recv()
    beyond = rim_in[...]
    wins[late] = jnp.where(
        x == 0, part_window(3, 0, first, second, beyond), part_window(0, 1, first, second, beyond)
    )
    for turn in range(2):
        target = lax.rem(late + 4 * ((quad + 1 + turn) % 2), nd)

        @pl.when(target != d)
        def _():
            slab(target).start()

    def passing(s):
        block = speeds.at[pl.ds(cz * s, cz), mine]
        return remote(block, block, pass_send, pass_recv.at[s], sibling)

    speeds[pl.ds(cz * d, cz), mine] = wins[part]
    passing(d).start()
    stencil_factors(factors, shot_cells_ref, 2 * quad + g, 4 * x + part, nx, ny)

    shots_rim.wait_recv()

    def windowed(first, second, beyond):
        picks = [part_window(p, x, first, second, beyond) for p in range(4)]
        return jnp.where(
            part < 2, jnp.where(part == 0, picks[0], picks[1]), jnp.where(part == 2, picks[2], picks[3])
        )

    around = windowed(source[:, :, :WIDE], source[:, :, WIDE:], shots_rim_in[0:4])
    fields[0:2, mine] = jnp.where(g == 0, around[0:2], around[2:4])
    shots_side[0:2] = jnp.where(g == 0, around[2:4], around[0:2])
    around = windowed(depth_of[:, :WIDE], depth_of[:, WIDE:], shots_rim_in[4])
    fields[2, mine] = around
    shots_side[2] = around
    side = remote(shots_side, fields.at[:, mine], side_send, side_recv, sibling)
    side.start()

    def pass_on(s):
        @pl.when(s != d)
        def _():
            block = speeds.at[pl.ds(cz * s, cz), mine]
            remote(block, block, slab_send, slab_recv.at[s], sibling).wait_recv()
            passing(s).start()

    for s in range(AHEAD):
        pass_on(s)

    def forward(s, front):
        @pl.when(s < nd - AHEAD)
        def _():
            pass_on(s + AHEAD)

        block = speeds.at[pl.ds(cz * s, cz), theirs]
        remote(block, block, pass_send, pass_recv.at[s], sibling).wait_recv()
        for i in range(2):
            k = 2 * s + i
            front = forward_plane(
                k, speeds[k], front, factors, fronts, spans, row_buffers[4 * i : 4 * i + 4], nought
            )
        return front

    lax.fori_loop(0, nd, forward, jnp.ones((2 * nx, WIDE), jnp.float32))
    remote(shots_side, fields.at[:, theirs], side_send, side_recv, sibling).wait_recv()
    source = jnp.concatenate([fields[0], fields[1]], axis=0)
    reflector = fields[2]
    shape = (nx, WIDE)
    col = window_columns(shape, 4 * x + part)
    row = lax.broadcasted_iota(jnp.int32, shape, 0)
    lane = lanes(shape)
    inside = (col >= 0) & (col < ny)

    def handing(s, core):
        rows = pl.ds(bx * core, bx)
        return remote(packed.at[s, rows], gathered.at[2 * d + g], sum_send, sum_recv, {"depth": s, "gx": core})

    def adjoint(step, back):
        s = nd - 1 - step
        grads = []
        for i in (1, 0):
            k = 2 * s + i
            back, grad = adjoint_plane(
                k, speeds[k], back, source, reflector, factors, fronts, spans, inside,
                (row == 0, row == nx - 1), row_buffers[4 * i : 4 * i + 4], nought,
            )
            grads.append(grad)
        packed[s] = jnp.where(lane < OWN, grads[1], halfway(grads[0]))
        for core in range(2):

            @pl.when((s != d) | (g != core))
            def _():
                handing(s, core).start()

        return back

    lax.fori_loop(0, nd, adjoint, jnp.zeros((2 * nx, WIDE), jnp.float32))
    gathered[2 * d + g] = packed[d, mine]
    rim.wait_send()
    shots_rim.wait_send()
    side.wait_send()
    others = speeds.at[pl.ds(0, cz * (nd - 1)), mine]
    remote(others, others, slab_send, rim_recv, sibling).wait_send()
    block = speeds.at[:, mine]
    remote(block, block, pass_send, rim_recv, sibling).wait_send()
    block = gathered.at[pl.ds(0, 2 * nd - 1)]
    remote(block, block, rim_send, sum_recv, sibling).wait_recv()
    remote(block, block, sum_send, rim_recv, sibling).wait_send()
    totals = [
        (gathered[2 * p] + gathered[2 * p + 1]) + (gathered[2 * p + 8] + gathered[2 * p + 9])
        for p in range(4)
    ]
    lane = lanes((bx, WIDE))
    for tile in range(2):
        low, high = totals[2 * tile], totals[2 * tile + 1]
        columns = slice(tile * WIDE, (tile + 1) * WIDE)
        out_ref[0, :, columns] = jnp.where(lane < OWN, low, halfway(high))
        out_ref[1, :, columns] = jnp.where(lane < OWN, halfway(low), high)


def local_split(slowness, air_mask, reflector, shot_cells, receiver_mask, residual):
    cz, bx, by = slowness.shape
    nd = lax.axis_size("depth")
    nz, nx, ny = cz * nd, bx * lax.axis_size("gx"), by * lax.axis_size("gy")
    f32, i32 = jnp.float32, jnp.int32
    dma = pltpu.SemaphoreType.DMA
    return pl.pallas_call(
        functools.partial(sweep_kernel, ny),
        out_shape=jax.ShapeDtypeStruct((cz, bx, by), f32),
        in_specs=[pl.BlockSpec(memory_space=pltpu.HBM)] * 6,
        out_specs=pl.BlockSpec(memory_space=pltpu.VMEM),
        scratch_shapes=[
            pltpu.SMEM(shot_cells.shape[::-1], i32),
            pltpu.VMEM((cz, bx, by), f32),
            pltpu.VMEM((cz, bx, by), i32),
            pltpu.VMEM((bx, by), i32),
            pltpu.VMEM((4, bx, by), i32),
            pltpu.VMEM((4, bx, by), f32),
            pltpu.VMEM((cz, bx, WIDE), f32),
            pltpu.VMEM((cz, bx, WIDE), f32),
            pltpu.VMEM((4, cz, bx, WIDE), f32),
            pltpu.VMEM((nz, nx, WIDE), f32),
            pltpu.VMEM((5, bx, WIDE), f32),
            pltpu.VMEM((5, bx, WIDE), f32),
            pltpu.VMEM((3, bx, WIDE), f32),
            pltpu.VMEM((3, nx, WIDE), f32),
            pltpu.VMEM((8, 2 * nx, WIDE), f32),
            pltpu.VMEM((nz, 2 * nx, WIDE), f32),
            pltpu.VMEM((nz, 2 * nx, WIDE), f32),
            pltpu.VMEM((nd, nx, WIDE), f32),
            pltpu.VMEM((2 * nd, bx, WIDE), f32),
            *[pltpu.VMEM((2 * nx + 2 * PAD, WIDE), f32) for _ in range(8)],
            dma((6,)),
            dma,
            dma,
            dma,
            dma((nd,)),
            dma,
            dma((nd,)),
            dma,
            dma,
            dma,
            dma,
            dma,
            dma,
        ],
        compiler_params=pltpu.CompilerParams(
            vmem_limit_bytes=16 * 1024 * 1024, collective_id=0, has_side_effects=True
        ),
    )(
        *(
            pltpu.with_memory_space_constraint(a, pltpu.HBM)
            for a in (shot_cells.T, slowness, air_mask, reflector, receiver_mask, residual)
        )
    )


def solution(mesh):
    in_specs = (
        P("depth", "gx", "gy"),
        P("depth", "gx", "gy"),
        P("gx", "gy"),
        P(),
        P(None, "gx", "gy"),
        P(None, "gx", "gy"),
    )
    out_specs = P("depth", "gx", "gy")
    sizes = dict(mesh.shape)

    def whole(slowness, air_mask, reflector, shot_cells, receiver_mask, residual):
        nz, nx, ny = slowness.shape
        fits = (
            sizes == {"depth": 8, "gx": 2, "gy": 2}
            and (nz, nx, ny) == (16, 32, 512)
            and shot_cells.shape[0] == 8
        )
        local = local_split if fits else local_generic
        return jax.shard_map(local, mesh=mesh, in_specs=in_specs, out_specs=out_specs, check_vma=False)(
            slowness, air_mask, reflector, shot_cells, receiver_mask, residual
        )

    return whole
```

```python
import functools
import math

import jax
import jax.numpy as jnp
from jax import lax
from jax.experimental import pallas as pl
from jax.experimental.pallas import tpu as pltpu
from jax.sharding import PartitionSpec as P

SOFTMIN_TEMPER = 0.5
SURF = 0.7
AIR_SLOW = 2.5
STEP_PENALTY = 10000.0
STENCIL_SHIFTS = [
    (first_term, second_term) for first_term in (-1, 0, 1) for second_term in (-1, 0, 1)
]


def padded(cells, sides, width):
    for axis, dim in sides:
        count = lax.axis_size(axis)
        ends = count - 1
        head = lax.slice_in_dim(cells, 0, width, axis=dim)
        tail = lax.slice_in_dim(cells, cells.shape[dim] - width, cells.shape[dim], axis=dim)
        cells = jnp.concatenate(
            [
                lax.ppermute(tail, axis, [(i, (i + 1) % count) for i in range(ends)]),
                cells,
                lax.ppermute(head, axis, [((i + 1) % count, i) for i in range(ends)]),
            ],
            axis=dim,
        )
    return cells


def passed_along(value, axis, steps):
    count = lax.axis_size(axis)
    initial, last = (max(0, -steps), min(count, count - steps))
    return lax.ppermute(value, axis, [(source, source + steps) for source in range(initial, last)])


def soft_front(candidate_times):
    lowest = candidate_times[0]
    for cand in candidate_times[1:]:
        lowest = jnp.minimum(lowest, cand)
    total = jnp.exp(-(candidate_times[0] - lowest) / SOFTMIN_TEMPER)
    for cand in candidate_times[1:]:
        total = total + jnp.exp(-(cand - lowest) / SOFTMIN_TEMPER)
    return lowest - SOFTMIN_TEMPER * jnp.log(total)


def local_generic(slowness, air_mask, reflector, shot_cells, receiver_mask, residual):
    depth_count = lax.axis_size("depth")
    depth_pos = lax.axis_index("depth")
    cz, shift_along_x, shift_along_y = slowness.shape
    shots = shot_cells.shape[0]
    nx_total = shift_along_x * lax.axis_size("gx")
    ny_total = shift_along_y * lax.axis_size("gy")
    xpos = lax.axis_index("gx") * shift_along_x + jnp.arange(shift_along_x, dtype=jnp.int32)
    ypos = lax.axis_index("gy") * shift_along_y + jnp.arange(shift_along_y, dtype=jnp.int32)
    zpos = depth_pos * cz + jnp.arange(cz, dtype=jnp.int32)
    earth = air_mask == 0
    speed = jnp.where(air_mask == 1, jnp.float32(AIR_SLOW), slowness)
    shot_x = shot_cells[:, 0].astype(jnp.float32)
    shot_y = shot_cells[:, 1].astype(jnp.float32)
    surface = SURF * jnp.sqrt(
        (xpos.astype(jnp.float32)[None, :, None] - shot_x[:, None, None]) ** 2
        + (ypos.astype(jnp.float32)[None, None, :] - shot_y[:, None, None]) ** 2
    )
    penalty_terms = []
    span_lengths = []
    for first_term, second_term in STENCIL_SHIFTS:
        valid_mask = ((xpos + first_term >= 0) & (xpos + first_term < nx_total))[:, None] & (
            (ypos + second_term >= 0) & (ypos + second_term < ny_total)
        )[None, :]
        penalty_terms.append(jnp.where(valid_mask, jnp.float32(0.0), jnp.float32(STEP_PENALTY)))
        span_lengths.append(math.sqrt(1.0 + first_term * first_term + second_term * second_term))

    def sweep_plane(prior_layer, depth_layer):
        padded_layer = padded(prior_layer, (("gx", 1), ("gy", 2)), 1)
        candidate_times = [
            padded_layer[
                :,
                1 + first_term : 1 + first_term + shift_along_x,
                1 + second_term : 1 + second_term + shift_along_y,
            ]
            + depth_layer * span_lengths[stencil_index]
            + penalty_terms[stencil_index]
            for stencil_index, (first_term, second_term) in enumerate(STENCIL_SHIFTS)
        ]
        nxt = soft_front(candidate_times)
        return (nxt, nxt)

    def make_adjoint(source_block, count):

        def adjoint_plane(back, inputs):
            depth_layer, hit, previous_times, current_layer = inputs
            lam = source_block * hit[None] + back
            stacked = jnp.concatenate([lam, current_layer, previous_times, depth_layer[None]], 0)
            padded_layer = padded(stacked, (("gx", 1), ("gy", 2)), 1)
            lam_pad = padded_layer[:count]
            cur_pad = padded_layer[count : 2 * count]
            prev_pad = padded_layer[2 * count : 3 * count]
            layer_pad = padded_layer[3 * count]
            weight_sum = jnp.zeros_like(lam)
            back_new = jnp.zeros_like(lam)
            for stencil_index, (first_term, second_term) in enumerate(STENCIL_SHIFTS):
                lateral_value = prev_pad[
                    :,
                    1 + first_term : 1 + first_term + shift_along_x,
                    1 + second_term : 1 + second_term + shift_along_y,
                ]
                softmin_weight = jnp.exp(
                    -(
                        lateral_value
                        + depth_layer * span_lengths[stencil_index]
                        + penalty_terms[stencil_index]
                        - current_layer
                    )
                    / SOFTMIN_TEMPER
                )
                weight_sum = weight_sum + softmin_weight * span_lengths[stencil_index]
                lam_from = lam_pad[
                    :,
                    1 - first_term : 1 - first_term + shift_along_x,
                    1 - second_term : 1 - second_term + shift_along_y,
                ]
                cur_from = cur_pad[
                    :,
                    1 - first_term : 1 - first_term + shift_along_x,
                    1 - second_term : 1 - second_term + shift_along_y,
                ]
                layer_from = layer_pad[
                    1 - first_term : 1 - first_term + shift_along_x,
                    1 - second_term : 1 - second_term + shift_along_y,
                ]
                prob_from = jnp.exp(
                    -(previous_times + layer_from * span_lengths[stencil_index] - cur_from)
                    / SOFTMIN_TEMPER
                )
                back_new = back_new + lam_from * prob_from
            return (back_new, jnp.sum(lam * weight_sum, axis=0))

        return adjoint_plane

    source_all = jnp.where(receiver_mask == 1, residual, jnp.float32(0.0))
    blocks = 1
    width = shots // blocks
    rounds = depth_count + blocks - 1

    def forward_round(step, carry):
        incoming, store = carry
        group = step - depth_pos
        valid_mask = (group >= 0) & (group < blocks)
        top = jnp.where(depth_pos == 0, surface, incoming)
        last, planes = lax.scan(sweep_plane, top, speed)
        block = jnp.concatenate([top[None], planes], 0)
        old = store
        store = jnp.where(valid_mask, block, old)
        incoming = passed_along(last, "depth", 1)
        return (incoming, store)

    store = jnp.zeros((cz + 1, shots, shift_along_x, shift_along_y), jnp.float32)
    incoming = jnp.zeros((width, shift_along_x, shift_along_y), jnp.float32)
    incoming, store = lax.fori_loop(0, rounds, forward_round, (incoming, store))
    hits = (zpos[:, None, None] == reflector[None]).astype(jnp.float32)

    def adjoint_round(step, carry):
        incoming_back, grad_sum = carry
        group = step - (depth_count - 1 - depth_pos)
        valid_mask = (group >= 0) & (group < blocks)
        back_top, grads = lax.scan(
            make_adjoint(source_all, width),
            incoming_back,
            (speed, hits, store[:-1], store[1:]),
            reverse=True,
        )
        grad_sum = grad_sum + jnp.where(valid_mask, grads, jnp.float32(0.0))
        incoming_back = passed_along(back_top, "depth", -1)
        return (incoming_back, grad_sum)

    start_back = jnp.zeros((width, shift_along_x, shift_along_y), jnp.float32)
    grad_total = jnp.zeros((cz, shift_along_x, shift_along_y), jnp.float32)
    start_back, grad_total = lax.fori_loop(0, rounds, adjoint_round, (start_back, grad_total))
    colsum = jnp.sum(source_all, axis=0)
    below = zpos[:, None, None] <= reflector[None]
    raw = jnp.where(earth, grad_total, jnp.float32(0.0)) + jnp.where(
        earth & below, colsum[None], jnp.float32(0.0)
    )
    padded_layer = padded(raw, (("gx", 1), ("gy", 2)), 1)
    beside_all = jnp.zeros_like(raw)
    for first_term, second_term in STENCIL_SHIFTS:
        if first_term != 0 or second_term != 0:
            beside_all = (
                beside_all
                + padded_layer[
                    :,
                    1 + first_term : 1 + first_term + shift_along_x,
                    1 + second_term : 1 + second_term + shift_along_y,
                ]
            )
    return 0.5 * raw + 0.0625 * beside_all


WIDE = 128
OWN = 64
PAD = 8
AHEAD = 3
SIDE = 32
ROOT2 = math.sqrt(2.0)
ROOT3 = math.sqrt(3.0)


def left(cells):
    return pltpu.roll(cells, 1, axis=1)


def right(cells):
    return pltpu.roll(cells, cells.shape[1] - 1, axis=1)


def halfway(cells):
    return pltpu.roll(cells, OWN, axis=cells.ndim - 1)


def lanes(shape):
    return lax.broadcasted_iota(jnp.int32, shape, len(shape) - 1)


def window_columns(shape, part):
    lane = lanes(shape)
    return part * OWN + lane - jnp.where(lane >= WIDE - SIDE, WIDE, 0)


def stencil_factors(factors, shot_cells_ref, pair, part, nx, ny):
    shape = (2 * nx, WIDE)
    row = lax.broadcasted_iota(jnp.int32, shape, 0)
    second = row >= nx
    row = jnp.where(second, row - nx, row)
    col = window_columns(shape, part)
    place = [
        jnp.where(second, shot_cells_ref[d, 2 * pair + 1], shot_cells_ref[d, 2 * pair]).astype(
            jnp.float32
        )
        for d in (0, 1)
    ]

    def surface(a, b):
        u = (row + a).astype(jnp.float32) - place[0]
        v = (col + b).astype(jnp.float32) - place[1]
        return SURF * jnp.sqrt(u * u + v * v)

    here = surface(0, 0)
    for slot, (a, b) in enumerate(((0, -1), (0, 1), (-1, 0), (1, 0))):
        inside = (row + a >= 0) & (row + a < nx) & (col + b >= 0) & (col + b < ny)
        beside = surface(a, b)
        penalty = jnp.where(inside, jnp.float32(0.0), jnp.float32(STEP_PENALTY))
        value = jnp.where(inside, beside, jnp.float32(0.0))
        factors[slot] = jnp.exp(-((value + penalty) - here) / SOFTMIN_TEMPER)
        factors[4 + slot] = jnp.where(inside, jnp.exp(-(here - beside) / SOFTMIN_TEMPER), 0.0)


def twice(cells):
    return jnp.concatenate([cells, cells], axis=0)


def shifted_rows(buffer, cells, nought):
    rows = cells.shape[0]
    buffer[pl.ds(PAD, rows)] = cells
    return buffer[pl.ds(PAD - 1 + nought, rows)], buffer[pl.ds(PAD + 1 + nought, rows)]


def forward_plane(k, speed, front, factors, fronts, spans, buffers, nought):
    w1 = twice(jnp.exp(-speed / SOFTMIN_TEMPER))
    w2 = twice(jnp.exp(-(speed * ROOT2) / SOFTMIN_TEMPER))
    w3 = twice(jnp.exp(-(speed * ROOT3) / SOFTMIN_TEMPER))
    side = factors[0] * left(front) + factors[1] * right(front)
    up, down = shifted_rows(buffers[0], front, nought)
    edge = side + factors[2] * up + factors[3] * down
    up, down = shifted_rows(buffers[1], side, nought)
    corner = factors[2] * up + factors[3] * down
    one, two, three = w1 * front, w2 * edge, w3 * corner
    front = one + two + three
    fronts[k] = front
    spans[k] = one + ROOT2 * two + ROOT3 * three
    return front


def adjoint_plane(k, speed, back, source, reflector, factors, fronts, spans, inside, edges, buffers, nought):
    w1 = twice(jnp.exp(-speed / SOFTMIN_TEMPER))
    w2 = twice(jnp.exp(-(speed * ROOT2) / SOFTMIN_TEMPER))
    w3 = twice(jnp.exp(-(speed * ROOT3) / SOFTMIN_TEMPER))
    plane = k.astype(jnp.float32)
    lam = jnp.where(twice(reflector == plane), source / fronts[k], 0.0) + back
    part = lam * spans[k] + jnp.where(twice(reflector >= plane), source, 0.0)
    nx = speed.shape[0]
    raw = jnp.where(inside & (speed != AIR_SLOW), part[:nx] + part[nx:], 0.0)
    line = raw + left(raw) + right(raw)
    up, down = shifted_rows(buffers[2], line, nought)
    box = line + jnp.where(edges[0], 0.0, up) + jnp.where(edges[1], 0.0, down)
    grad = 0.4375 * raw + 0.0625 * box
    two, three = w2 * lam, w3 * lam
    far = two + factors[4] * left(three) + factors[5] * right(three)
    up, down = shifted_rows(buffers[3], far, nought)
    back = (
        w1 * lam
        + (factors[4] * left(two) + factors[5] * right(two))
        + (factors[6] * up + factors[7] * down)
    )
    return back, grad


def part_window(part, x, first, second, beyond):
    lane = lanes(first.shape)
    if part == 0:
        return jnp.where(lane < WIDE - SIDE, first, jnp.where(x == 1, beyond, first))
    if part == 1:
        return halfway(jnp.where(lane >= SIDE, first, second))
    if part == 2:
        return jnp.where(lane < WIDE - SIDE, second, first)
    return halfway(jnp.where(lane >= SIDE, second, jnp.where(x == 0, beyond, second)))


def sweep_kernel(
    ny,
    shot_cells_hbm,
    slowness_hbm,
    air_hbm,
    reflector_hbm,
    receiver_hbm,
    residual_hbm,
    out_ref,
    shot_cells_ref,
    slowness,
    air,
    reflect,
    receiver,
    resid,
    rim_out,
    rim_in,
    wins,
    speeds,
    shots_rim_out,
    shots_rim_in,
    shots_side,
    fields,
    factors,
    fronts,
    spans,
    packed,
    gathered,
    *rest,
):
    row_buffers, sems = rest[:8], rest[8:]
    (
        load_sem,
        rim_send,
        rim_recv,
        slab_send,
        slab_recv,
        pass_send,
        pass_recv,
        shots_send,
        shots_recv,
        side_send,
        side_recv,
        sum_send,
        sum_recv,
    ) = sems
    d = lax.axis_index("depth")
    g = lax.axis_index("gx")
    x = lax.axis_index("gy")
    cz, bx, _ = slowness.shape
    nd = speeds.shape[0] // cz
    nx = 2 * bx
    part = lax.rem(d, 4)
    quad = d // 4
    sibling = {"gx": 1 - g}
    across = {"gy": 1 - x}
    mine = pl.ds(pl.multiple_of(bx * g, bx), bx)
    theirs = pl.ds(pl.multiple_of(bx * (1 - g), bx), bx)
    shots = pl.ds(4 * quad, 4)

    loads = [
        pltpu.make_async_copy(source, target, load_sem.at[i])
        for i, (source, target) in enumerate(
            (
                (slowness_hbm, slowness),
                (air_hbm, air),
                (reflector_hbm, reflect),
                (receiver_hbm.at[shots], receiver),
                (residual_hbm.at[shots], resid),
                (shot_cells_hbm, shot_cells_ref),
            )
        )
    ]
    for load in loads[:2]:
        load.start()
    barrier = pltpu.get_barrier_semaphore()

    for i in range(nd - 1, 0, -1):
        for core in range(2):
            peer = {"depth": lax.rem(d + i, nd), "gx": core}
            pl.semaphore_signal(barrier, inc=1, device_id=peer, device_id_type=pl.DeviceIdType.MESH)
    for peer in (sibling, across):
        pl.semaphore_signal(barrier, inc=1, device_id=peer, device_id_type=pl.DeviceIdType.MESH)

    def remote(source, target, send, recv, peer):
        return pltpu.make_async_remote_copy(
            src_ref=source,
            dst_ref=target,
            send_sem=send,
            recv_sem=recv,
            device_id=peer,
            device_id_type=pl.DeviceIdType.MESH,
        )

    for load in loads[2:]:
        load.start()
    nought = g // 2
    for buffer in row_buffers:
        buffer[...] = jnp.zeros(buffer.shape, jnp.float32)
    loads[0].wait()
    loads[1].wait()
    speed = jnp.where(air[...] == 1, jnp.float32(AIR_SLOW), slowness[...])
    first, second = speed[:, :, :WIDE], speed[:, :, WIDE:]
    rim_out[...] = jnp.where(x == 0, second, first)
    for p in range(4):
        wins[p] = part_window(p, x, first, second, first)
    pl.semaphore_wait(barrier, 2 * nd)

    rim = remote(rim_out, rim_in, rim_send, rim_recv, across)
    rim.start()
    late = 3 * (1 - x)

    def slab(target):
        return remote(
            wins.at[lax.rem(target, 4)],
            speeds.at[pl.ds(cz * d, cz), mine],
            slab_send,
            slab_recv.at[d],
            {"depth": target},
        )

    for i in range(1, nd):
        early = lax.rem(d + i, nd)

        @pl.when(lax.rem(early, 4) != late)
        def _(early=early):
            slab(early).start()

    for load in loads[2:]:
        load.wait()
    source = jnp.where(receiver[...] == 1, resid[...], jnp.float32(0.0))
    shots_rim_out[0:4] = jnp.where(x == 0, source[:, :, WIDE:], source[:, :, :WIDE])
    depth_of = reflect[...].astype(jnp.float32)
    shots_rim_out[4] = jnp.where(x == 0, depth_of[:, WIDE:], depth_of[:, :WIDE])
    shots_rim = remote(shots_rim_out, shots_rim_in, shots_send, shots_recv, across)
    shots_rim.start()

    rim.wait_recv()
    beyond = rim_in[...]
    wins[late] = jnp.where(
        x == 0, part_window(3, 0, first, second, beyond), part_window(0, 1, first, second, beyond)
    )
    for turn in range(2):
        target = lax.rem(late + 4 * ((quad + 1 + turn) % 2), nd)

        @pl.when(target != d)
        def _():
            slab(target).start()

    def passing(s):
        block = speeds.at[pl.ds(cz * s, cz), mine]
        return remote(block, block, pass_send, pass_recv.at[s], sibling)

    speeds[pl.ds(cz * d, cz), mine] = wins[part]
    passing(d).start()
    stencil_factors(factors, shot_cells_ref, 2 * quad + g, 4 * x + part, nx, ny)

    def pass_on(s):
        @pl.when(s != d)
        def _():
            block = speeds.at[pl.ds(cz * s, cz), mine]
            remote(block, block, slab_send, slab_recv.at[s], sibling).wait_recv()
            passing(s).start()

    for s in range(AHEAD):
        pass_on(s)

    shots_rim.wait_recv()

    def windowed(first, second, beyond):
        picks = [part_window(p, x, first, second, beyond) for p in range(4)]
        return jnp.where(
            part < 2, jnp.where(part == 0, picks[0], picks[1]), jnp.where(part == 2, picks[2], picks[3])
        )

    around = windowed(source[:, :, :WIDE], source[:, :, WIDE:], shots_rim_in[0:4])
    fields[0:2, mine] = jnp.where(g == 0, around[0:2], around[2:4])
    shots_side[0:2] = jnp.where(g == 0, around[2:4], around[0:2])
    around = windowed(depth_of[:, :WIDE], depth_of[:, WIDE:], shots_rim_in[4])
    fields[2, mine] = around
    shots_side[2] = around
    side = remote(shots_side, fields.at[:, mine], side_send, side_recv, sibling)
    side.start()

    def forward(s, front):
        @pl.when(s < nd - AHEAD)
        def _():
            pass_on(s + AHEAD)

        block = speeds.at[pl.ds(cz * s, cz), theirs]
        remote(block, block, pass_send, pass_recv.at[s], sibling).wait_recv()
        for i in range(2):
            k = 2 * s + i
            front = forward_plane(
                k, speeds[k], front, factors, fronts, spans, row_buffers[4 * i : 4 * i + 4], nought
            )
        return front

    lax.fori_loop(0, nd, forward, jnp.ones((2 * nx, WIDE), jnp.float32))
    remote(shots_side, fields.at[:, theirs], side_send, side_recv, sibling).wait_recv()
    source = jnp.concatenate([fields[0], fields[1]], axis=0)
    reflector = fields[2]
    shape = (nx, WIDE)
    col = window_columns(shape, 4 * x + part)
    row = lax.broadcasted_iota(jnp.int32, shape, 0)
    lane = lanes(shape)
    inside = (col >= 0) & (col < ny)

    def handing(s, core):
        rows = pl.ds(bx * core, bx)
        return remote(packed.at[s, rows], gathered.at[2 * d + g], sum_send, sum_recv, {"depth": s, "gx": core})

    def adjoint(step, back):
        s = nd - 1 - step
        grads = []
        for i in (1, 0):
            k = 2 * s + i
            back, grad = adjoint_plane(
                k, speeds[k], back, source, reflector, factors, fronts, spans, inside,
                (row == 0, row == nx - 1), row_buffers[4 * i : 4 * i + 4], nought,
            )
            grads.append(grad)
        packed[s] = jnp.where(lane < OWN, grads[1], halfway(grads[0]))
        for core in range(2):

            @pl.when((s != d) | (g != core))
            def _():
                handing(s, core).start()

        return back

    lax.fori_loop(0, nd, adjoint, jnp.zeros((2 * nx, WIDE), jnp.float32))
    gathered[2 * d + g] = packed[d, mine]
    rim.wait_send()
    shots_rim.wait_send()
    side.wait_send()
    others = speeds.at[pl.ds(0, cz * (nd - 1)), mine]
    remote(others, others, slab_send, rim_recv, sibling).wait_send()
    block = speeds.at[:, mine]
    remote(block, block, pass_send, rim_recv, sibling).wait_send()
    block = gathered.at[pl.ds(0, 2 * nd - 1)]
    remote(block, block, rim_send, sum_recv, sibling).wait_recv()
    remote(block, block, sum_send, rim_recv, sibling).wait_send()
    totals = [
        (gathered[2 * p] + gathered[2 * p + 1]) + (gathered[2 * p + 8] + gathered[2 * p + 9])
        for p in range(4)
    ]
    lane = lanes((bx, WIDE))
    for tile in range(2):
        low, high = totals[2 * tile], totals[2 * tile + 1]
        columns = slice(tile * WIDE, (tile + 1) * WIDE)
        out_ref[0, :, columns] = jnp.where(lane < OWN, low, halfway(high))
        out_ref[1, :, columns] = jnp.where(lane < OWN, halfway(low), high)


def local_split(slowness, air_mask, reflector, shot_cells, receiver_mask, residual):
    cz, bx, by = slowness.shape
    nd = lax.axis_size("depth")
    nz, nx, ny = cz * nd, bx * lax.axis_size("gx"), by * lax.axis_size("gy")
    f32, i32 = jnp.float32, jnp.int32
    dma = pltpu.SemaphoreType.DMA
    return pl.pallas_call(
        functools.partial(sweep_kernel, ny),
        out_shape=jax.ShapeDtypeStruct((cz, bx, by), f32),
        in_specs=[pl.BlockSpec(memory_space=pltpu.HBM)] * 6,
        out_specs=pl.BlockSpec(memory_space=pltpu.VMEM),
        scratch_shapes=[
            pltpu.SMEM(shot_cells.shape[::-1], i32),
            pltpu.VMEM((cz, bx, by), f32),
            pltpu.VMEM((cz, bx, by), i32),
            pltpu.VMEM((bx, by), i32),
            pltpu.VMEM((4, bx, by), i32),
            pltpu.VMEM((4, bx, by), f32),
            pltpu.VMEM((cz, bx, WIDE), f32),
            pltpu.VMEM((cz, bx, WIDE), f32),
            pltpu.VMEM((4, cz, bx, WIDE), f32),
            pltpu.VMEM((nz, nx, WIDE), f32),
            pltpu.VMEM((5, bx, WIDE), f32),
            pltpu.VMEM((5, bx, WIDE), f32),
            pltpu.VMEM((3, bx, WIDE), f32),
            pltpu.VMEM((3, nx, WIDE), f32),
            pltpu.VMEM((8, 2 * nx, WIDE), f32),
            pltpu.VMEM((nz, 2 * nx, WIDE), f32),
            pltpu.VMEM((nz, 2 * nx, WIDE), f32),
            pltpu.VMEM((nd, nx, WIDE), f32),
            pltpu.VMEM((2 * nd, bx, WIDE), f32),
            *[pltpu.VMEM((2 * nx + 2 * PAD, WIDE), f32) for _ in range(8)],
            dma((6,)),
            dma,
            dma,
            dma,
            dma((nd,)),
            dma,
            dma((nd,)),
            dma,
            dma,
            dma,
            dma,
            dma,
            dma,
        ],
        compiler_params=pltpu.CompilerParams(
            vmem_limit_bytes=16 * 1024 * 1024, collective_id=0, has_side_effects=True
        ),
    )(
        *(
            pltpu.with_memory_space_constraint(a, pltpu.HBM)
            for a in (shot_cells.T, slowness, air_mask, reflector, receiver_mask, residual)
        )
    )


def solution(mesh):
    in_specs = (
        P("depth", "gx", "gy"),
        P("depth", "gx", "gy"),
        P("gx", "gy"),
        P(),
        P(None, "gx", "gy"),
        P(None, "gx", "gy"),
    )
    out_specs = P("depth", "gx", "gy")
    sizes = dict(mesh.shape)

    def whole(slowness, air_mask, reflector, shot_cells, receiver_mask, residual):
        nz, nx, ny = slowness.shape
        fits = (
            sizes == {"depth": 8, "gx": 2, "gy": 2}
            and (nz, nx, ny) == (16, 32, 512)
            and shot_cells.shape[0] == 8
        )
        local = local_split if fits else local_generic
        return jax.shard_map(local, mesh=mesh, in_specs=in_specs, out_specs=out_specs, check_vma=False)(
            slowness, air_mask, reflector, shot_cells, receiver_mask, residual
        )

    return whole
```

```python
import functools
import math

import jax
import jax.numpy as jnp
from jax import lax
from jax.experimental import pallas as pl
from jax.experimental.pallas import tpu as pltpu
from jax.sharding import PartitionSpec as P

SOFTMIN_TEMPER = 0.5
SURF = 0.7
AIR_SLOW = 2.5
STEP_PENALTY = 10000.0
STENCIL_SHIFTS = [
    (first_term, second_term) for first_term in (-1, 0, 1) for second_term in (-1, 0, 1)
]


def padded(cells, sides, width):
    for axis, dim in sides:
        count = lax.axis_size(axis)
        ends = count - 1
        head = lax.slice_in_dim(cells, 0, width, axis=dim)
        tail = lax.slice_in_dim(cells, cells.shape[dim] - width, cells.shape[dim], axis=dim)
        cells = jnp.concatenate(
            [
                lax.ppermute(tail, axis, [(i, (i + 1) % count) for i in range(ends)]),
                cells,
                lax.ppermute(head, axis, [((i + 1) % count, i) for i in range(ends)]),
            ],
            axis=dim,
        )
    return cells


def passed_along(value, axis, steps):
    count = lax.axis_size(axis)
    initial, last = (max(0, -steps), min(count, count - steps))
    return lax.ppermute(value, axis, [(source, source + steps) for source in range(initial, last)])


def soft_front(candidate_times):
    lowest = candidate_times[0]
    for cand in candidate_times[1:]:
        lowest = jnp.minimum(lowest, cand)
    total = jnp.exp(-(candidate_times[0] - lowest) / SOFTMIN_TEMPER)
    for cand in candidate_times[1:]:
        total = total + jnp.exp(-(cand - lowest) / SOFTMIN_TEMPER)
    return lowest - SOFTMIN_TEMPER * jnp.log(total)


def local_generic(slowness, air_mask, reflector, shot_cells, receiver_mask, residual):
    depth_count = lax.axis_size("depth")
    depth_pos = lax.axis_index("depth")
    cz, shift_along_x, shift_along_y = slowness.shape
    shots = shot_cells.shape[0]
    nx_total = shift_along_x * lax.axis_size("gx")
    ny_total = shift_along_y * lax.axis_size("gy")
    xpos = lax.axis_index("gx") * shift_along_x + jnp.arange(shift_along_x, dtype=jnp.int32)
    ypos = lax.axis_index("gy") * shift_along_y + jnp.arange(shift_along_y, dtype=jnp.int32)
    zpos = depth_pos * cz + jnp.arange(cz, dtype=jnp.int32)
    earth = air_mask == 0
    speed = jnp.where(air_mask == 1, jnp.float32(AIR_SLOW), slowness)
    shot_x = shot_cells[:, 0].astype(jnp.float32)
    shot_y = shot_cells[:, 1].astype(jnp.float32)
    surface = SURF * jnp.sqrt(
        (xpos.astype(jnp.float32)[None, :, None] - shot_x[:, None, None]) ** 2
        + (ypos.astype(jnp.float32)[None, None, :] - shot_y[:, None, None]) ** 2
    )
    penalty_terms = []
    span_lengths = []
    for first_term, second_term in STENCIL_SHIFTS:
        valid_mask = ((xpos + first_term >= 0) & (xpos + first_term < nx_total))[:, None] & (
            (ypos + second_term >= 0) & (ypos + second_term < ny_total)
        )[None, :]
        penalty_terms.append(jnp.where(valid_mask, jnp.float32(0.0), jnp.float32(STEP_PENALTY)))
        span_lengths.append(math.sqrt(1.0 + first_term * first_term + second_term * second_term))

    def sweep_plane(prior_layer, depth_layer):
        padded_layer = padded(prior_layer, (("gx", 1), ("gy", 2)), 1)
        candidate_times = [
            padded_layer[
                :,
                1 + first_term : 1 + first_term + shift_along_x,
                1 + second_term : 1 + second_term + shift_along_y,
            ]
            + depth_layer * span_lengths[stencil_index]
            + penalty_terms[stencil_index]
            for stencil_index, (first_term, second_term) in enumerate(STENCIL_SHIFTS)
        ]
        nxt = soft_front(candidate_times)
        return (nxt, nxt)

    def make_adjoint(source_block, count):

        def adjoint_plane(back, inputs):
            depth_layer, hit, previous_times, current_layer = inputs
            lam = source_block * hit[None] + back
            stacked = jnp.concatenate([lam, current_layer, previous_times, depth_layer[None]], 0)
            padded_layer = padded(stacked, (("gx", 1), ("gy", 2)), 1)
            lam_pad = padded_layer[:count]
            cur_pad = padded_layer[count : 2 * count]
            prev_pad = padded_layer[2 * count : 3 * count]
            layer_pad = padded_layer[3 * count]
            weight_sum = jnp.zeros_like(lam)
            back_new = jnp.zeros_like(lam)
            for stencil_index, (first_term, second_term) in enumerate(STENCIL_SHIFTS):
                lateral_value = prev_pad[
                    :,
                    1 + first_term : 1 + first_term + shift_along_x,
                    1 + second_term : 1 + second_term + shift_along_y,
                ]
                softmin_weight = jnp.exp(
                    -(
                        lateral_value
                        + depth_layer * span_lengths[stencil_index]
                        + penalty_terms[stencil_index]
                        - current_layer
                    )
                    / SOFTMIN_TEMPER
                )
                weight_sum = weight_sum + softmin_weight * span_lengths[stencil_index]
                lam_from = lam_pad[
                    :,
                    1 - first_term : 1 - first_term + shift_along_x,
                    1 - second_term : 1 - second_term + shift_along_y,
                ]
                cur_from = cur_pad[
                    :,
                    1 - first_term : 1 - first_term + shift_along_x,
                    1 - second_term : 1 - second_term + shift_along_y,
                ]
                layer_from = layer_pad[
                    1 - first_term : 1 - first_term + shift_along_x,
                    1 - second_term : 1 - second_term + shift_along_y,
                ]
                prob_from = jnp.exp(
                    -(previous_times + layer_from * span_lengths[stencil_index] - cur_from)
                    / SOFTMIN_TEMPER
                )
                back_new = back_new + lam_from * prob_from
            return (back_new, jnp.sum(lam * weight_sum, axis=0))

        return adjoint_plane

    source_all = jnp.where(receiver_mask == 1, residual, jnp.float32(0.0))
    blocks = 1
    width = shots // blocks
    rounds = depth_count + blocks - 1

    def forward_round(step, carry):
        incoming, store = carry
        group = step - depth_pos
        valid_mask = (group >= 0) & (group < blocks)
        top = jnp.where(depth_pos == 0, surface, incoming)
        last, planes = lax.scan(sweep_plane, top, speed)
        block = jnp.concatenate([top[None], planes], 0)
        old = store
        store = jnp.where(valid_mask, block, old)
        incoming = passed_along(last, "depth", 1)
        return (incoming, store)

    store = jnp.zeros((cz + 1, shots, shift_along_x, shift_along_y), jnp.float32)
    incoming = jnp.zeros((width, shift_along_x, shift_along_y), jnp.float32)
    incoming, store = lax.fori_loop(0, rounds, forward_round, (incoming, store))
    hits = (zpos[:, None, None] == reflector[None]).astype(jnp.float32)

    def adjoint_round(step, carry):
        incoming_back, grad_sum = carry
        group = step - (depth_count - 1 - depth_pos)
        valid_mask = (group >= 0) & (group < blocks)
        back_top, grads = lax.scan(
            make_adjoint(source_all, width),
            incoming_back,
            (speed, hits, store[:-1], store[1:]),
            reverse=True,
        )
        grad_sum = grad_sum + jnp.where(valid_mask, grads, jnp.float32(0.0))
        incoming_back = passed_along(back_top, "depth", -1)
        return (incoming_back, grad_sum)

    start_back = jnp.zeros((width, shift_along_x, shift_along_y), jnp.float32)
    grad_total = jnp.zeros((cz, shift_along_x, shift_along_y), jnp.float32)
    start_back, grad_total = lax.fori_loop(0, rounds, adjoint_round, (start_back, grad_total))
    colsum = jnp.sum(source_all, axis=0)
    below = zpos[:, None, None] <= reflector[None]
    raw = jnp.where(earth, grad_total, jnp.float32(0.0)) + jnp.where(
        earth & below, colsum[None], jnp.float32(0.0)
    )
    padded_layer = padded(raw, (("gx", 1), ("gy", 2)), 1)
    beside_all = jnp.zeros_like(raw)
    for first_term, second_term in STENCIL_SHIFTS:
        if first_term != 0 or second_term != 0:
            beside_all = (
                beside_all
                + padded_layer[
                    :,
                    1 + first_term : 1 + first_term + shift_along_x,
                    1 + second_term : 1 + second_term + shift_along_y,
                ]
            )
    return 0.5 * raw + 0.0625 * beside_all


WIDE = 128
OWN = 64
PAD = 8
AHEAD = 3
SIDE = 32
ROOT2 = math.sqrt(2.0)
ROOT3 = math.sqrt(3.0)


def left(cells):
    return pltpu.roll(cells, 1, axis=1)


def right(cells):
    return pltpu.roll(cells, cells.shape[1] - 1, axis=1)


def halfway(cells):
    return pltpu.roll(cells, OWN, axis=cells.ndim - 1)


def lanes(shape):
    return lax.broadcasted_iota(jnp.int32, shape, len(shape) - 1)


def window_columns(shape, part):
    lane = lanes(shape)
    return part * OWN + lane - jnp.where(lane >= WIDE - SIDE, WIDE, 0)


def stencil_factors(factors, shot_cells_ref, pair, part, nx, ny):
    shape = (2 * nx, WIDE)
    row = lax.broadcasted_iota(jnp.int32, shape, 0)
    second = row >= nx
    row = jnp.where(second, row - nx, row)
    col = window_columns(shape, part)
    place = [
        jnp.where(second, shot_cells_ref[d, 2 * pair + 1], shot_cells_ref[d, 2 * pair]).astype(
            jnp.float32
        )
        for d in (0, 1)
    ]

    def surface(a, b):
        u = (row + a).astype(jnp.float32) - place[0]
        v = (col + b).astype(jnp.float32) - place[1]
        return SURF * jnp.sqrt(u * u + v * v)

    here = surface(0, 0)
    for slot, (a, b) in enumerate(((0, -1), (0, 1), (-1, 0), (1, 0))):
        inside = (row + a >= 0) & (row + a < nx) & (col + b >= 0) & (col + b < ny)
        beside = surface(a, b)
        penalty = jnp.where(inside, jnp.float32(0.0), jnp.float32(STEP_PENALTY))
        value = jnp.where(inside, beside, jnp.float32(0.0))
        factors[slot] = jnp.exp(-((value + penalty) - here) / SOFTMIN_TEMPER)
        factors[4 + slot] = jnp.where(inside, jnp.exp(-(here - beside) / SOFTMIN_TEMPER), 0.0)


def twice(cells):
    return jnp.concatenate([cells, cells], axis=0)


def shifted_rows(buffer, cells, nought):
    rows = cells.shape[0]
    buffer[pl.ds(PAD, rows)] = cells
    return buffer[pl.ds(PAD - 1 + nought, rows)], buffer[pl.ds(PAD + 1 + nought, rows)]


def forward_plane(k, speed, front, factors, fronts, spans, buffers, nought):
    w1 = twice(jnp.exp(-speed / SOFTMIN_TEMPER))
    w2 = twice(jnp.exp(-(speed * ROOT2) / SOFTMIN_TEMPER))
    w3 = twice(jnp.exp(-(speed * ROOT3) / SOFTMIN_TEMPER))
    side = factors[0] * left(front) + factors[1] * right(front)
    up, down = shifted_rows(buffers[0], front, nought)
    edge = side + factors[2] * up + factors[3] * down
    up, down = shifted_rows(buffers[1], side, nought)
    corner = factors[2] * up + factors[3] * down
    one, two, three = w1 * front, w2 * edge, w3 * corner
    front = one + two + three
    fronts[k] = front
    spans[k] = one + ROOT2 * two + ROOT3 * three
    return front


def adjoint_plane(k, speed, back, source, reflector, factors, fronts, spans, inside, edges, buffers, nought):
    w1 = twice(jnp.exp(-speed / SOFTMIN_TEMPER))
    w2 = twice(jnp.exp(-(speed * ROOT2) / SOFTMIN_TEMPER))
    w3 = twice(jnp.exp(-(speed * ROOT3) / SOFTMIN_TEMPER))
    plane = k.astype(jnp.float32)
    lam = jnp.where(twice(reflector == plane), source / fronts[k], 0.0) + back
    part = lam * spans[k] + jnp.where(twice(reflector >= plane), source, 0.0)
    nx = speed.shape[0]
    raw = jnp.where(inside & (speed != AIR_SLOW), part[:nx] + part[nx:], 0.0)
    line = raw + left(raw) + right(raw)
    up, down = shifted_rows(buffers[2], line, nought)
    box = line + jnp.where(edges[0], 0.0, up) + jnp.where(edges[1], 0.0, down)
    grad = 0.4375 * raw + 0.0625 * box
    two, three = w2 * lam, w3 * lam
    far = two + factors[4] * left(three) + factors[5] * right(three)
    up, down = shifted_rows(buffers[3], far, nought)
    back = (
        w1 * lam
        + (factors[4] * left(two) + factors[5] * right(two))
        + (factors[6] * up + factors[7] * down)
    )
    return back, grad


def part_window(part, x, first, second, beyond):
    lane = lanes(first.shape)
    if part == 0:
        return jnp.where(lane < WIDE - SIDE, first, jnp.where(x == 1, beyond, first))
    if part == 1:
        return halfway(jnp.where(lane >= SIDE, first, second))
    if part == 2:
        return jnp.where(lane < WIDE - SIDE, second, first)
    return halfway(jnp.where(lane >= SIDE, second, jnp.where(x == 0, beyond, second)))


def sweep_kernel(
    ny,
    shot_cells_hbm,
    slowness_hbm,
    air_hbm,
    reflector_hbm,
    receiver_hbm,
    residual_hbm,
    out_ref,
    shot_cells_ref,
    slowness,
    air,
    reflect,
    receiver,
    resid,
    rim_out,
    rim_in,
    wins,
    speeds,
    shots_rim_out,
    shots_rim_in,
    shots_side,
    fields,
    factors,
    fronts,
    spans,
    packed,
    gathered,
    *rest,
):
    row_buffers, sems = rest[:8], rest[8:]
    (
        load_sem,
        rim_send,
        rim_recv,
        slab_send,
        slab_recv,
        pass_send,
        pass_recv,
        shots_send,
        shots_recv,
        side_send,
        side_recv,
        sum_send,
        sum_recv,
    ) = sems
    d = lax.axis_index("depth")
    g = lax.axis_index("gx")
    x = lax.axis_index("gy")
    cz, bx, _ = slowness.shape
    nd = speeds.shape[0] // cz
    nx = 2 * bx

    def part_of(depth):
        place = lax.rem(depth, 4)
        return place + (1 - x) * (3 - 2 * place)

    part = part_of(d)
    quad = d // 4
    sibling = {"gx": 1 - g}
    across = {"gy": 1 - x}
    mine = pl.ds(pl.multiple_of(bx * g, bx), bx)
    theirs = pl.ds(pl.multiple_of(bx * (1 - g), bx), bx)
    shots = pl.ds(4 * quad, 4)

    loads = [
        pltpu.make_async_copy(source, target, load_sem.at[i])
        for i, (source, target) in enumerate(
            (
                (slowness_hbm, slowness),
                (air_hbm, air),
                (reflector_hbm, reflect),
                (receiver_hbm.at[shots], receiver),
                (residual_hbm.at[shots], resid),
                (shot_cells_hbm, shot_cells_ref),
            )
        )
    ]
    for load in loads[:2]:
        load.start()
    barrier = pltpu.get_barrier_semaphore()

    for i in range(nd - 1, 0, -1):
        for core in range(2):
            peer = {"depth": lax.rem(d + i, nd), "gx": core}
            pl.semaphore_signal(barrier, inc=1, device_id=peer, device_id_type=pl.DeviceIdType.MESH)
    for peer in (sibling, across):
        pl.semaphore_signal(barrier, inc=1, device_id=peer, device_id_type=pl.DeviceIdType.MESH)

    def remote(source, target, send, recv, peer):
        return pltpu.make_async_remote_copy(
            src_ref=source,
            dst_ref=target,
            send_sem=send,
            recv_sem=recv,
            device_id=peer,
            device_id_type=pl.DeviceIdType.MESH,
        )

    for load in loads[2:]:
        load.start()
    nought = g // 2
    for buffer in row_buffers:
        buffer[...] = jnp.zeros(buffer.shape, jnp.float32)
    loads[0].wait()
    loads[1].wait()
    speed = jnp.where(air[...] == 1, jnp.float32(AIR_SLOW), slowness[...])
    first, second = speed[:, :, :WIDE], speed[:, :, WIDE:]
    rim_out[...] = jnp.where(x == 0, second, first)
    for p in range(4):
        wins[p] = part_window(p, x, first, second, first)
    pl.semaphore_wait(barrier, 2 * nd)

    rim = remote(rim_out, rim_in, rim_send, rim_recv, across)
    rim.start()
    late = 3 * (1 - x)

    def slab(target):
        return remote(
            wins.at[part_of(target)],
            speeds.at[pl.ds(cz * d, cz), mine],
            slab_send,
            slab_recv.at[d],
            {"depth": target},
        )

    for i in range(1, nd):
        early = lax.rem(d + i, nd)

        @pl.when(lax.rem(early, 4) != 0)
        def _(early=early):
            slab(early).start()

    rim.wait_recv()
    beyond = rim_in[...]
    wins[late] = jnp.where(
        x == 0, part_window(3, 0, first, second, beyond), part_window(0, 1, first, second, beyond)
    )
    for turn in range(2):
        target = 4 * ((quad + 1 + turn) % 2)

        @pl.when(target != d)
        def _():
            slab(target).start()

    for load in loads[2:]:
        load.wait()
    source = jnp.where(receiver[...] == 1, resid[...], jnp.float32(0.0))
    shots_rim_out[0:4] = jnp.where(x == 0, source[:, :, WIDE:], source[:, :, :WIDE])
    depth_of = reflect[...].astype(jnp.float32)
    shots_rim_out[4] = jnp.where(x == 0, depth_of[:, WIDE:], depth_of[:, :WIDE])
    shots_rim = remote(shots_rim_out, shots_rim_in, shots_send, shots_recv, across)
    shots_rim.start()

    def passing(s):
        block = speeds.at[pl.ds(cz * s, cz), mine]
        return remote(block, block, pass_send, pass_recv.at[s], sibling)

    speeds[pl.ds(cz * d, cz), mine] = wins[part]
    passing(d).start()
    stencil_factors(factors, shot_cells_ref, 2 * quad + g, 4 * x + part, nx, ny)

    def pass_on(s):
        @pl.when(s != d)
        def _():
            block = speeds.at[pl.ds(cz * s, cz), mine]
            remote(block, block, slab_send, slab_recv.at[s], sibling).wait_recv()
            passing(s).start()

    for s in range(AHEAD):
        pass_on(s)

    shots_rim.wait_recv()

    def windowed(first, second, beyond):
        picks = [part_window(p, x, first, second, beyond) for p in range(4)]
        return jnp.where(
            part < 2, jnp.where(part == 0, picks[0], picks[1]), jnp.where(part == 2, picks[2], picks[3])
        )

    around = windowed(source[:, :, :WIDE], source[:, :, WIDE:], shots_rim_in[0:4])
    fields[0:2, mine] = jnp.where(g == 0, around[0:2], around[2:4])
    shots_side[0:2] = jnp.where(g == 0, around[2:4], around[0:2])
    around = windowed(depth_of[:, :WIDE], depth_of[:, WIDE:], shots_rim_in[4])
    fields[2, mine] = around
    shots_side[2] = around
    side = remote(shots_side, fields.at[:, mine], side_send, side_recv, sibling)
    side.start()

    def forward(s, front):
        @pl.when(s < nd - AHEAD)
        def _():
            pass_on(s + AHEAD)

        block = speeds.at[pl.ds(cz * s, cz), theirs]
        remote(block, block, pass_send, pass_recv.at[s], sibling).wait_recv()
        for i in range(2):
            k = 2 * s + i
            front = forward_plane(
                k, speeds[k], front, factors, fronts, spans, row_buffers[4 * i : 4 * i + 4], nought
            )
        return front

    lax.fori_loop(0, nd, forward, jnp.ones((2 * nx, WIDE), jnp.float32))
    remote(shots_side, fields.at[:, theirs], side_send, side_recv, sibling).wait_recv()
    source = jnp.concatenate([fields[0], fields[1]], axis=0)
    reflector = fields[2]
    shape = (nx, WIDE)
    col = window_columns(shape, 4 * x + part)
    row = lax.broadcasted_iota(jnp.int32, shape, 0)
    lane = lanes(shape)
    inside = (col >= 0) & (col < ny)

    def handing(s, core):
        rows = pl.ds(bx * core, bx)
        return remote(packed.at[s, rows], gathered.at[2 * d + g], sum_send, sum_recv, {"depth": s, "gx": core})

    def adjoint(step, back):
        s = nd - 1 - step
        grads = []
        for i in (1, 0):
            k = 2 * s + i
            back, grad = adjoint_plane(
                k, speeds[k], back, source, reflector, factors, fronts, spans, inside,
                (row == 0, row == nx - 1), row_buffers[4 * i : 4 * i + 4], nought,
            )
            grads.append(grad)
        packed[s] = jnp.where(lane < OWN, grads[1], halfway(grads[0]))
        for core in range(2):

            @pl.when((s != d) | (g != core))
            def _():
                handing(s, core).start()

        return back

    lax.fori_loop(0, nd, adjoint, jnp.zeros((2 * nx, WIDE), jnp.float32))
    gathered[2 * d + g] = packed[d, mine]
    rim.wait_send()
    shots_rim.wait_send()
    side.wait_send()
    others = speeds.at[pl.ds(0, cz * (nd - 1)), mine]
    remote(others, others, slab_send, rim_recv, sibling).wait_send()
    block = speeds.at[:, mine]
    remote(block, block, pass_send, rim_recv, sibling).wait_send()
    block = gathered.at[pl.ds(0, 2 * nd - 1)]
    remote(block, block, rim_send, sum_recv, sibling).wait_recv()
    remote(block, block, sum_send, rim_recv, sibling).wait_send()
    totals = [
        (gathered[2 * p] + gathered[2 * p + 1]) + (gathered[2 * p + 8] + gathered[2 * p + 9])
        for p in range(4)
    ]
    totals = [jnp.where(x == 0, totals[3 - p], totals[p]) for p in range(4)]
    lane = lanes((bx, WIDE))
    for tile in range(2):
        low, high = totals[2 * tile], totals[2 * tile + 1]
        columns = slice(tile * WIDE, (tile + 1) * WIDE)
        out_ref[0, :, columns] = jnp.where(lane < OWN, low, halfway(high))
        out_ref[1, :, columns] = jnp.where(lane < OWN, halfway(low), high)


def local_split(slowness, air_mask, reflector, shot_cells, receiver_mask, residual):
    cz, bx, by = slowness.shape
    nd = lax.axis_size("depth")
    nz, nx, ny = cz * nd, bx * lax.axis_size("gx"), by * lax.axis_size("gy")
    f32, i32 = jnp.float32, jnp.int32
    dma = pltpu.SemaphoreType.DMA
    return pl.pallas_call(
        functools.partial(sweep_kernel, ny),
        out_shape=jax.ShapeDtypeStruct((cz, bx, by), f32),
        in_specs=[pl.BlockSpec(memory_space=pltpu.HBM)] * 6,
        out_specs=pl.BlockSpec(memory_space=pltpu.VMEM),
        scratch_shapes=[
            pltpu.SMEM(shot_cells.shape[::-1], i32),
            pltpu.VMEM((cz, bx, by), f32),
            pltpu.VMEM((cz, bx, by), i32),
            pltpu.VMEM((bx, by), i32),
            pltpu.VMEM((4, bx, by), i32),
            pltpu.VMEM((4, bx, by), f32),
            pltpu.VMEM((cz, bx, WIDE), f32),
            pltpu.VMEM((cz, bx, WIDE), f32),
            pltpu.VMEM((4, cz, bx, WIDE), f32),
            pltpu.VMEM((nz, nx, WIDE), f32),
            pltpu.VMEM((5, bx, WIDE), f32),
            pltpu.VMEM((5, bx, WIDE), f32),
            pltpu.VMEM((3, bx, WIDE), f32),
            pltpu.VMEM((3, nx, WIDE), f32),
            pltpu.VMEM((8, 2 * nx, WIDE), f32),
            pltpu.VMEM((nz, 2 * nx, WIDE), f32),
            pltpu.VMEM((nz, 2 * nx, WIDE), f32),
            pltpu.VMEM((nd, nx, WIDE), f32),
            pltpu.VMEM((2 * nd, bx, WIDE), f32),
            *[pltpu.VMEM((2 * nx + 2 * PAD, WIDE), f32) for _ in range(8)],
            dma((6,)),
            dma,
            dma,
            dma,
            dma((nd,)),
            dma,
            dma((nd,)),
            dma,
            dma,
            dma,
            dma,
            dma,
            dma,
        ],
        compiler_params=pltpu.CompilerParams(
            vmem_limit_bytes=16 * 1024 * 1024, collective_id=0, has_side_effects=True
        ),
    )(
        *(
            pltpu.with_memory_space_constraint(a, pltpu.HBM)
            for a in (shot_cells.T, slowness, air_mask, reflector, receiver_mask, residual)
        )
    )


def solution(mesh):
    in_specs = (
        P("depth", "gx", "gy"),
        P("depth", "gx", "gy"),
        P("gx", "gy"),
        P(),
        P(None, "gx", "gy"),
        P(None, "gx", "gy"),
    )
    out_specs = P("depth", "gx", "gy")
    sizes = dict(mesh.shape)

    def whole(slowness, air_mask, reflector, shot_cells, receiver_mask, residual):
        nz, nx, ny = slowness.shape
        fits = (
            sizes == {"depth": 8, "gx": 2, "gy": 2}
            and (nz, nx, ny) == (16, 32, 512)
            and shot_cells.shape[0] == 8
        )
        local = local_split if fits else local_generic
        return jax.shard_map(local, mesh=mesh, in_specs=in_specs, out_specs=out_specs, check_vma=False)(
            slowness, air_mask, reflector, shot_cells, receiver_mask, residual
        )

    return whole
```

```python
import functools
import math

import jax
import jax.numpy as jnp
from jax import lax
from jax.experimental import pallas as pl
from jax.experimental.pallas import tpu as pltpu
from jax.sharding import PartitionSpec as P

SOFTMIN_TEMPER = 0.5
SURF = 0.7
AIR_SLOW = 2.5
STEP_PENALTY = 10000.0
STENCIL_SHIFTS = [
    (first_term, second_term) for first_term in (-1, 0, 1) for second_term in (-1, 0, 1)
]


def padded(cells, sides, width):
    for axis, dim in sides:
        count = lax.axis_size(axis)
        ends = count - 1
        head = lax.slice_in_dim(cells, 0, width, axis=dim)
        tail = lax.slice_in_dim(cells, cells.shape[dim] - width, cells.shape[dim], axis=dim)
        cells = jnp.concatenate(
            [
                lax.ppermute(tail, axis, [(i, (i + 1) % count) for i in range(ends)]),
                cells,
                lax.ppermute(head, axis, [((i + 1) % count, i) for i in range(ends)]),
            ],
            axis=dim,
        )
    return cells


def passed_along(value, axis, steps):
    count = lax.axis_size(axis)
    initial, last = (max(0, -steps), min(count, count - steps))
    return lax.ppermute(value, axis, [(source, source + steps) for source in range(initial, last)])


def soft_front(candidate_times):
    lowest = candidate_times[0]
    for cand in candidate_times[1:]:
        lowest = jnp.minimum(lowest, cand)
    total = jnp.exp(-(candidate_times[0] - lowest) / SOFTMIN_TEMPER)
    for cand in candidate_times[1:]:
        total = total + jnp.exp(-(cand - lowest) / SOFTMIN_TEMPER)
    return lowest - SOFTMIN_TEMPER * jnp.log(total)


def local_generic(slowness, air_mask, reflector, shot_cells, receiver_mask, residual):
    depth_count = lax.axis_size("depth")
    depth_pos = lax.axis_index("depth")
    cz, shift_along_x, shift_along_y = slowness.shape
    shots = shot_cells.shape[0]
    nx_total = shift_along_x * lax.axis_size("gx")
    ny_total = shift_along_y * lax.axis_size("gy")
    xpos = lax.axis_index("gx") * shift_along_x + jnp.arange(shift_along_x, dtype=jnp.int32)
    ypos = lax.axis_index("gy") * shift_along_y + jnp.arange(shift_along_y, dtype=jnp.int32)
    zpos = depth_pos * cz + jnp.arange(cz, dtype=jnp.int32)
    earth = air_mask == 0
    speed = jnp.where(air_mask == 1, jnp.float32(AIR_SLOW), slowness)
    shot_x = shot_cells[:, 0].astype(jnp.float32)
    shot_y = shot_cells[:, 1].astype(jnp.float32)
    surface = SURF * jnp.sqrt(
        (xpos.astype(jnp.float32)[None, :, None] - shot_x[:, None, None]) ** 2
        + (ypos.astype(jnp.float32)[None, None, :] - shot_y[:, None, None]) ** 2
    )
    penalty_terms = []
    span_lengths = []
    for first_term, second_term in STENCIL_SHIFTS:
        valid_mask = ((xpos + first_term >= 0) & (xpos + first_term < nx_total))[:, None] & (
            (ypos + second_term >= 0) & (ypos + second_term < ny_total)
        )[None, :]
        penalty_terms.append(jnp.where(valid_mask, jnp.float32(0.0), jnp.float32(STEP_PENALTY)))
        span_lengths.append(math.sqrt(1.0 + first_term * first_term + second_term * second_term))

    def sweep_plane(prior_layer, depth_layer):
        padded_layer = padded(prior_layer, (("gx", 1), ("gy", 2)), 1)
        candidate_times = [
            padded_layer[
                :,
                1 + first_term : 1 + first_term + shift_along_x,
                1 + second_term : 1 + second_term + shift_along_y,
            ]
            + depth_layer * span_lengths[stencil_index]
            + penalty_terms[stencil_index]
            for stencil_index, (first_term, second_term) in enumerate(STENCIL_SHIFTS)
        ]
        nxt = soft_front(candidate_times)
        return (nxt, nxt)

    def make_adjoint(source_block, count):

        def adjoint_plane(back, inputs):
            depth_layer, hit, previous_times, current_layer = inputs
            lam = source_block * hit[None] + back
            stacked = jnp.concatenate([lam, current_layer, previous_times, depth_layer[None]], 0)
            padded_layer = padded(stacked, (("gx", 1), ("gy", 2)), 1)
            lam_pad = padded_layer[:count]
            cur_pad = padded_layer[count : 2 * count]
            prev_pad = padded_layer[2 * count : 3 * count]
            layer_pad = padded_layer[3 * count]
            weight_sum = jnp.zeros_like(lam)
            back_new = jnp.zeros_like(lam)
            for stencil_index, (first_term, second_term) in enumerate(STENCIL_SHIFTS):
                lateral_value = prev_pad[
                    :,
                    1 + first_term : 1 + first_term + shift_along_x,
                    1 + second_term : 1 + second_term + shift_along_y,
                ]
                softmin_weight = jnp.exp(
                    -(
                        lateral_value
                        + depth_layer * span_lengths[stencil_index]
                        + penalty_terms[stencil_index]
                        - current_layer
                    )
                    / SOFTMIN_TEMPER
                )
                weight_sum = weight_sum + softmin_weight * span_lengths[stencil_index]
                lam_from = lam_pad[
                    :,
                    1 - first_term : 1 - first_term + shift_along_x,
                    1 - second_term : 1 - second_term + shift_along_y,
                ]
                cur_from = cur_pad[
                    :,
                    1 - first_term : 1 - first_term + shift_along_x,
                    1 - second_term : 1 - second_term + shift_along_y,
                ]
                layer_from = layer_pad[
                    1 - first_term : 1 - first_term + shift_along_x,
                    1 - second_term : 1 - second_term + shift_along_y,
                ]
                prob_from = jnp.exp(
                    -(previous_times + layer_from * span_lengths[stencil_index] - cur_from)
                    / SOFTMIN_TEMPER
                )
                back_new = back_new + lam_from * prob_from
            return (back_new, jnp.sum(lam * weight_sum, axis=0))

        return adjoint_plane

    source_all = jnp.where(receiver_mask == 1, residual, jnp.float32(0.0))
    blocks = 1
    width = shots // blocks
    rounds = depth_count + blocks - 1

    def forward_round(step, carry):
        incoming, store = carry
        group = step - depth_pos
        valid_mask = (group >= 0) & (group < blocks)
        top = jnp.where(depth_pos == 0, surface, incoming)
        last, planes = lax.scan(sweep_plane, top, speed)
        block = jnp.concatenate([top[None], planes], 0)
        old = store
        store = jnp.where(valid_mask, block, old)
        incoming = passed_along(last, "depth", 1)
        return (incoming, store)

    store = jnp.zeros((cz + 1, shots, shift_along_x, shift_along_y), jnp.float32)
    incoming = jnp.zeros((width, shift_along_x, shift_along_y), jnp.float32)
    incoming, store = lax.fori_loop(0, rounds, forward_round, (incoming, store))
    hits = (zpos[:, None, None] == reflector[None]).astype(jnp.float32)

    def adjoint_round(step, carry):
        incoming_back, grad_sum = carry
        group = step - (depth_count - 1 - depth_pos)
        valid_mask = (group >= 0) & (group < blocks)
        back_top, grads = lax.scan(
            make_adjoint(source_all, width),
            incoming_back,
            (speed, hits, store[:-1], store[1:]),
            reverse=True,
        )
        grad_sum = grad_sum + jnp.where(valid_mask, grads, jnp.float32(0.0))
        incoming_back = passed_along(back_top, "depth", -1)
        return (incoming_back, grad_sum)

    start_back = jnp.zeros((width, shift_along_x, shift_along_y), jnp.float32)
    grad_total = jnp.zeros((cz, shift_along_x, shift_along_y), jnp.float32)
    start_back, grad_total = lax.fori_loop(0, rounds, adjoint_round, (start_back, grad_total))
    colsum = jnp.sum(source_all, axis=0)
    below = zpos[:, None, None] <= reflector[None]
    raw = jnp.where(earth, grad_total, jnp.float32(0.0)) + jnp.where(
        earth & below, colsum[None], jnp.float32(0.0)
    )
    padded_layer = padded(raw, (("gx", 1), ("gy", 2)), 1)
    beside_all = jnp.zeros_like(raw)
    for first_term, second_term in STENCIL_SHIFTS:
        if first_term != 0 or second_term != 0:
            beside_all = (
                beside_all
                + padded_layer[
                    :,
                    1 + first_term : 1 + first_term + shift_along_x,
                    1 + second_term : 1 + second_term + shift_along_y,
                ]
            )
    return 0.5 * raw + 0.0625 * beside_all


WIDE = 128
OWN = 64
PAD = 8
AHEAD = 5
SIDE = 32
ROOT2 = math.sqrt(2.0)
ROOT3 = math.sqrt(3.0)


def left(cells):
    return pltpu.roll(cells, 1, axis=1)


def right(cells):
    return pltpu.roll(cells, cells.shape[1] - 1, axis=1)


def halfway(cells):
    return pltpu.roll(cells, OWN, axis=cells.ndim - 1)


def lanes(shape):
    return lax.broadcasted_iota(jnp.int32, shape, len(shape) - 1)


def window_columns(shape, part):
    lane = lanes(shape)
    return part * OWN + lane - jnp.where(lane >= WIDE - SIDE, WIDE, 0)


def stencil_factors(factors, shot_cells_ref, pair, part, nx, ny):
    shape = (2 * nx, WIDE)
    row = lax.broadcasted_iota(jnp.int32, shape, 0)
    second = row >= nx
    row = jnp.where(second, row - nx, row)
    col = window_columns(shape, part)
    place = [
        jnp.where(second, shot_cells_ref[d, 2 * pair + 1], shot_cells_ref[d, 2 * pair]).astype(
            jnp.float32
        )
        for d in (0, 1)
    ]

    def surface(a, b):
        u = (row + a).astype(jnp.float32) - place[0]
        v = (col + b).astype(jnp.float32) - place[1]
        return SURF * jnp.sqrt(u * u + v * v)

    here = surface(0, 0)
    for slot, (a, b) in enumerate(((0, -1), (0, 1), (-1, 0), (1, 0))):
        inside = (row + a >= 0) & (row + a < nx) & (col + b >= 0) & (col + b < ny)
        beside = surface(a, b)
        penalty = jnp.where(inside, jnp.float32(0.0), jnp.float32(STEP_PENALTY))
        value = jnp.where(inside, beside, jnp.float32(0.0))
        factors[slot] = jnp.exp(-((value + penalty) - here) / SOFTMIN_TEMPER)
        factors[4 + slot] = jnp.where(inside, jnp.exp(-(here - beside) / SOFTMIN_TEMPER), 0.0)


def twice(cells):
    return jnp.concatenate([cells, cells], axis=0)


def shifted_rows(buffer, cells, nought):
    rows = cells.shape[0]
    buffer[pl.ds(PAD, rows)] = cells
    return buffer[pl.ds(PAD - 1 + nought, rows)], buffer[pl.ds(PAD + 1 + nought, rows)]


def forward_plane(k, speed, front, factors, fronts, spans, buffers, nought):
    w1 = twice(jnp.exp(-speed / SOFTMIN_TEMPER))
    w2 = twice(jnp.exp(-(speed * ROOT2) / SOFTMIN_TEMPER))
    w3 = twice(jnp.exp(-(speed * ROOT3) / SOFTMIN_TEMPER))
    side = factors[0] * left(front) + factors[1] * right(front)
    up, down = shifted_rows(buffers[0], front, nought)
    edge = side + factors[2] * up + factors[3] * down
    up, down = shifted_rows(buffers[1], side, nought)
    corner = factors[2] * up + factors[3] * down
    one, two, three = w1 * front, w2 * edge, w3 * corner
    front = one + two + three
    fronts[k] = front
    spans[k] = one + ROOT2 * two + ROOT3 * three
    return front


def adjoint_plane(k, speed, back, source, reflector, factors, fronts, spans, inside, edges, buffers, nought):
    w1 = twice(jnp.exp(-speed / SOFTMIN_TEMPER))
    w2 = twice(jnp.exp(-(speed * ROOT2) / SOFTMIN_TEMPER))
    w3 = twice(jnp.exp(-(speed * ROOT3) / SOFTMIN_TEMPER))
    plane = k.astype(jnp.float32)
    lam = jnp.where(twice(reflector == plane), source / fronts[k], 0.0) + back
    part = lam * spans[k] + jnp.where(twice(reflector >= plane), source, 0.0)
    nx = speed.shape[0]
    raw = jnp.where(inside & (speed != AIR_SLOW), part[:nx] + part[nx:], 0.0)
    line = raw + left(raw) + right(raw)
    up, down = shifted_rows(buffers[2], line, nought)
    box = line + jnp.where(edges[0], 0.0, up) + jnp.where(edges[1], 0.0, down)
    grad = 0.4375 * raw + 0.0625 * box
    two, three = w2 * lam, w3 * lam
    far = two + factors[4] * left(three) + factors[5] * right(three)
    up, down = shifted_rows(buffers[3], far, nought)
    back = (
        w1 * lam
        + (factors[4] * left(two) + factors[5] * right(two))
        + (factors[6] * up + factors[7] * down)
    )
    return back, grad


def part_window(part, x, first, second, beyond):
    lane = lanes(first.shape)
    if part == 0:
        return jnp.where(lane < WIDE - SIDE, first, jnp.where(x == 1, beyond, first))
    if part == 1:
        return halfway(jnp.where(lane >= SIDE, first, second))
    if part == 2:
        return jnp.where(lane < WIDE - SIDE, second, first)
    return halfway(jnp.where(lane >= SIDE, second, jnp.where(x == 0, beyond, second)))


def sweep_kernel(
    ny,
    shot_cells_hbm,
    slowness_hbm,
    air_hbm,
    reflector_hbm,
    receiver_hbm,
    residual_hbm,
    out_ref,
    shot_cells_ref,
    slowness,
    air,
    reflect,
    receiver,
    resid,
    rim_out,
    rim_in,
    wins,
    speeds,
    shots_rim_out,
    shots_rim_in,
    shots_side,
    fields,
    factors,
    fronts,
    spans,
    packed,
    gathered,
    *rest,
):
    row_buffers, sems = rest[:8], rest[8:]
    (
        load_sem,
        rim_send,
        rim_recv,
        slab_send,
        slab_recv,
        pass_send,
        pass_recv,
        shots_send,
        shots_recv,
        side_send,
        side_recv,
        sum_send,
        sum_recv,
    ) = sems
    d = lax.axis_index("depth")
    g = lax.axis_index("gx")
    x = lax.axis_index("gy")
    cz, bx, _ = slowness.shape
    nd = speeds.shape[0] // cz
    nx = 2 * bx

    def part_of(depth):
        place = lax.rem(depth, 4)
        return place + (1 - x) * (3 - 2 * place)

    part = part_of(d)
    quad = d // 4
    sibling = {"gx": 1 - g}
    across = {"gy": 1 - x}
    mine = pl.ds(pl.multiple_of(bx * g, bx), bx)
    theirs = pl.ds(pl.multiple_of(bx * (1 - g), bx), bx)
    shots = pl.ds(4 * quad, 4)

    loads = [
        pltpu.make_async_copy(source, target, load_sem.at[i])
        for i, (source, target) in enumerate(
            (
                (slowness_hbm, slowness),
                (air_hbm, air),
                (reflector_hbm, reflect),
                (receiver_hbm.at[shots], receiver),
                (residual_hbm.at[shots], resid),
                (shot_cells_hbm, shot_cells_ref),
            )
        )
    ]
    for load in loads[:2]:
        load.start()
    barrier = pltpu.get_barrier_semaphore()

    for i in range(nd - 1, 0, -1):
        for core in range(2):
            peer = {"depth": lax.rem(d + i, nd), "gx": core}
            pl.semaphore_signal(barrier, inc=1, device_id=peer, device_id_type=pl.DeviceIdType.MESH)
    for peer in (sibling, across):
        pl.semaphore_signal(barrier, inc=1, device_id=peer, device_id_type=pl.DeviceIdType.MESH)

    def remote(source, target, send, recv, peer):
        return pltpu.make_async_remote_copy(
            src_ref=source,
            dst_ref=target,
            send_sem=send,
            recv_sem=recv,
            device_id=peer,
            device_id_type=pl.DeviceIdType.MESH,
        )

    for load in loads[2:]:
        load.start()
    nought = g // 2
    for buffer in row_buffers:
        buffer[...] = jnp.zeros(buffer.shape, jnp.float32)
    loads[0].wait()
    loads[1].wait()
    speed = jnp.where(air[...] == 1, jnp.float32(AIR_SLOW), slowness[...])
    first, second = speed[:, :, :WIDE], speed[:, :, WIDE:]
    rim_out[...] = jnp.where(x == 0, second, first)
    for p in range(4):
        wins[p] = part_window(p, x, first, second, first)
    pl.semaphore_wait(barrier, 2 * nd)

    rim = remote(rim_out, rim_in, rim_send, rim_recv, across)
    rim.start()
    late = 3 * (1 - x)

    def slab(target):
        return remote(
            wins.at[part_of(target)],
            speeds.at[pl.ds(cz * d, cz), mine],
            slab_send,
            slab_recv.at[d],
            {"depth": target},
        )

    for i in range(1, nd):
        early = lax.rem(d + i, nd)

        @pl.when(lax.rem(early, 4) != 0)
        def _(early=early):
            slab(early).start()

    rim.wait_recv()
    beyond = rim_in[...]
    wins[late] = jnp.where(
        x == 0, part_window(3, 0, first, second, beyond), part_window(0, 1, first, second, beyond)
    )
    for turn in range(2):
        target = 4 * ((quad + 1 + turn) % 2)

        @pl.when(target != d)
        def _():
            slab(target).start()

    for load in loads[2:]:
        load.wait()
    source = jnp.where(receiver[...] == 1, resid[...], jnp.float32(0.0))
    shots_rim_out[0:4] = jnp.where(x == 0, source[:, :, WIDE:], source[:, :, :WIDE])
    depth_of = reflect[...].astype(jnp.float32)
    shots_rim_out[4] = jnp.where(x == 0, depth_of[:, WIDE:], depth_of[:, :WIDE])
    shots_rim = remote(shots_rim_out, shots_rim_in, shots_send, shots_recv, across)
    shots_rim.start()

    def passing(s):
        block = speeds.at[pl.ds(cz * s, cz), mine]
        return remote(block, block, pass_send, pass_recv.at[s], sibling)

    speeds[pl.ds(cz * d, cz), mine] = wins[part]
    passing(d).start()
    stencil_factors(factors, shot_cells_ref, 2 * quad + g, 4 * x + part, nx, ny)

    def pass_on(s):
        @pl.when(s != d)
        def _():
            block = speeds.at[pl.ds(cz * s, cz), mine]
            remote(block, block, slab_send, slab_recv.at[s], sibling).wait_recv()
            passing(s).start()

    for s in range(AHEAD):
        pass_on(s)

    shots_rim.wait_recv()

    def windowed(first, second, beyond):
        picks = [part_window(p, x, first, second, beyond) for p in range(4)]
        return jnp.where(
            part < 2, jnp.where(part == 0, picks[0], picks[1]), jnp.where(part == 2, picks[2], picks[3])
        )

    around = windowed(source[:, :, :WIDE], source[:, :, WIDE:], shots_rim_in[0:4])
    fields[0:2, mine] = jnp.where(g == 0, around[0:2], around[2:4])
    shots_side[0:2] = jnp.where(g == 0, around[2:4], around[0:2])
    around = windowed(depth_of[:, :WIDE], depth_of[:, WIDE:], shots_rim_in[4])
    fields[2, mine] = around
    shots_side[2] = around
    side = remote(shots_side, fields.at[:, mine], side_send, side_recv, sibling)
    side.start()

    def forward(s, front):
        @pl.when(s < nd - AHEAD)
        def _():
            pass_on(s + AHEAD)

        block = speeds.at[pl.ds(cz * s, cz), theirs]
        remote(block, block, pass_send, pass_recv.at[s], sibling).wait_recv()
        for i in range(2):
            k = 2 * s + i
            front = forward_plane(
                k, speeds[k], front, factors, fronts, spans, row_buffers[4 * i : 4 * i + 4], nought
            )
        return front

    lax.fori_loop(0, nd, forward, jnp.ones((2 * nx, WIDE), jnp.float32))
    remote(shots_side, fields.at[:, theirs], side_send, side_recv, sibling).wait_recv()
    source = jnp.concatenate([fields[0], fields[1]], axis=0)
    reflector = fields[2]
    shape = (nx, WIDE)
    col = window_columns(shape, 4 * x + part)
    row = lax.broadcasted_iota(jnp.int32, shape, 0)
    lane = lanes(shape)
    inside = (col >= 0) & (col < ny)

    def handing(s, core):
        rows = pl.ds(bx * core, bx)
        return remote(packed.at[s, rows], gathered.at[2 * d + g], sum_send, sum_recv, {"depth": s, "gx": core})

    def adjoint(step, back):
        s = nd - 1 - step
        grads = []
        for i in (1, 0):
            k = 2 * s + i
            back, grad = adjoint_plane(
                k, speeds[k], back, source, reflector, factors, fronts, spans, inside,
                (row == 0, row == nx - 1), row_buffers[4 * i : 4 * i + 4], nought,
            )
            grads.append(grad)
        packed[s] = jnp.where(lane < OWN, grads[1], halfway(grads[0]))
        for core in range(2):

            @pl.when((s != d) | (g != core))
            def _():
                handing(s, core).start()

        return back

    lax.fori_loop(0, nd, adjoint, jnp.zeros((2 * nx, WIDE), jnp.float32))
    gathered[2 * d + g] = packed[d, mine]
    rim.wait_send()
    shots_rim.wait_send()
    side.wait_send()
    others = speeds.at[pl.ds(0, cz * (nd - 1)), mine]
    remote(others, others, slab_send, rim_recv, sibling).wait_send()
    block = speeds.at[:, mine]
    remote(block, block, pass_send, rim_recv, sibling).wait_send()
    block = gathered.at[pl.ds(0, 2 * nd - 1)]
    remote(block, block, rim_send, sum_recv, sibling).wait_recv()
    remote(block, block, sum_send, rim_recv, sibling).wait_send()
    totals = [
        (gathered[2 * p] + gathered[2 * p + 1]) + (gathered[2 * p + 8] + gathered[2 * p + 9])
        for p in range(4)
    ]
    totals = [jnp.where(x == 0, totals[3 - p], totals[p]) for p in range(4)]
    lane = lanes((bx, WIDE))
    for tile in range(2):
        low, high = totals[2 * tile], totals[2 * tile + 1]
        columns = slice(tile * WIDE, (tile + 1) * WIDE)
        out_ref[0, :, columns] = jnp.where(lane < OWN, low, halfway(high))
        out_ref[1, :, columns] = jnp.where(lane < OWN, halfway(low), high)


def local_split(slowness, air_mask, reflector, shot_cells, receiver_mask, residual):
    cz, bx, by = slowness.shape
    nd = lax.axis_size("depth")
    nz, nx, ny = cz * nd, bx * lax.axis_size("gx"), by * lax.axis_size("gy")
    f32, i32 = jnp.float32, jnp.int32
    dma = pltpu.SemaphoreType.DMA
    return pl.pallas_call(
        functools.partial(sweep_kernel, ny),
        out_shape=jax.ShapeDtypeStruct((cz, bx, by), f32),
        in_specs=[pl.BlockSpec(memory_space=pltpu.HBM)] * 6,
        out_specs=pl.BlockSpec(memory_space=pltpu.VMEM),
        scratch_shapes=[
            pltpu.SMEM(shot_cells.shape[::-1], i32),
            pltpu.VMEM((cz, bx, by), f32),
            pltpu.VMEM((cz, bx, by), i32),
            pltpu.VMEM((bx, by), i32),
            pltpu.VMEM((4, bx, by), i32),
            pltpu.VMEM((4, bx, by), f32),
            pltpu.VMEM((cz, bx, WIDE), f32),
            pltpu.VMEM((cz, bx, WIDE), f32),
            pltpu.VMEM((4, cz, bx, WIDE), f32),
            pltpu.VMEM((nz, nx, WIDE), f32),
            pltpu.VMEM((5, bx, WIDE), f32),
            pltpu.VMEM((5, bx, WIDE), f32),
            pltpu.VMEM((3, bx, WIDE), f32),
            pltpu.VMEM((3, nx, WIDE), f32),
            pltpu.VMEM((8, 2 * nx, WIDE), f32),
            pltpu.VMEM((nz, 2 * nx, WIDE), f32),
            pltpu.VMEM((nz, 2 * nx, WIDE), f32),
            pltpu.VMEM((nd, nx, WIDE), f32),
            pltpu.VMEM((2 * nd, bx, WIDE), f32),
            *[pltpu.VMEM((2 * nx + 2 * PAD, WIDE), f32) for _ in range(8)],
            dma((6,)),
            dma,
            dma,
            dma,
            dma((nd,)),
            dma,
            dma((nd,)),
            dma,
            dma,
            dma,
            dma,
            dma,
            dma,
        ],
        compiler_params=pltpu.CompilerParams(
            vmem_limit_bytes=16 * 1024 * 1024, collective_id=0, has_side_effects=True
        ),
    )(
        *(
            pltpu.with_memory_space_constraint(a, pltpu.HBM)
            for a in (shot_cells.T, slowness, air_mask, reflector, receiver_mask, residual)
        )
    )


def solution(mesh):
    in_specs = (
        P("depth", "gx", "gy"),
        P("depth", "gx", "gy"),
        P("gx", "gy"),
        P(),
        P(None, "gx", "gy"),
        P(None, "gx", "gy"),
    )
    out_specs = P("depth", "gx", "gy")
    sizes = dict(mesh.shape)

    def whole(slowness, air_mask, reflector, shot_cells, receiver_mask, residual):
        nz, nx, ny = slowness.shape
        fits = (
            sizes == {"depth": 8, "gx": 2, "gy": 2}
            and (nz, nx, ny) == (16, 32, 512)
            and shot_cells.shape[0] == 8
        )
        local = local_split if fits else local_generic
        return jax.shard_map(local, mesh=mesh, in_specs=in_specs, out_specs=out_specs, check_vma=False)(
            slowness, air_mask, reflector, shot_cells, receiver_mask, residual
        )

    return whole
```
